32 devices in a mesh: ctx: 8 (over z, y), head: 4 (over x, core).
Axes of the slice: x: 2, y: 2, z: 4, core: 2. Of those that a mesh axis runs over, the one named last changes fastest.
Arguments:
- queries: bfloat16 [1536, 8192], P(('ctx', 'head')), may hold values from -16 to 16
- keys: bfloat16 [1536, 1024], P(('ctx', 'head')), may hold values from -16 to 16
- values: bfloat16 [1536, 1024], P(('ctx', 'head')), may hold values from -6 to 6
- segment_ids: int32 [8, 1536], P('head', 'ctx'), may hold values from 0 to 95, as said below
- grad_out: bfloat16 [1536, 8192], P(('ctx', 'head')), may hold values from -6 to 6
Outputs:
- grad_queries: bfloat16 [1536, 8192], P('ctx', 'head')
- grad_keys: bfloat16 [1536, 1024], P('ctx', 'head')
- grad_values: bfloat16 [1536, 1024], P('ctx', 'head')
The draws below stay inside these ranges and needn't reach their ends.
Inputs may be any that keep to these rules, and one draw needn't show every extreme that they name: `segment_ids`: for each KV head and each aligned block of 192 tokens the ids start at 0 at the block's first token, never fall, and rise by at most one from token to token; for each KV head some block uses every id up to 95.
All inputs are finite; a program needn't handle non-finite values.
Results may differ from the reference program's by a relative error of at most 0.015.
Values may be sent and summed in bfloat16 or wider, within the bound.
No kernel may reach another device: no remote copies, remote signals or barrier semaphores. Data moves between devices by JAX's collectives and lax.ppermute only.
A program may use at most 64 MiB of HBM per device.

```python
import jax
import jax.numpy as jnp
from jax import lax

QH = 64
KVH = 8
HD = 128
TOK_DEV = 192
SLOT_DEV = 96
TOKENS = 1536
SLOTS = 768


def draw_queries(key, part):
    shape = (TOKENS, QH * HD)
    drawn = jnp.clip(jax.random.normal(jax.random.fold_in(key, 21), shape, jnp.float32), -6.0, 6.0)
    return drawn.astype(jnp.bfloat16)


def draw_keys(key, part):
    shape = (TOKENS, KVH * HD)
    drawn = jnp.clip(jax.random.normal(jax.random.fold_in(key, 31), shape, jnp.float32), -6.0, 6.0)
    return drawn.astype(jnp.bfloat16)


def draw_segment_ids(key, part):
    blocks_count = TOKENS // TOK_DEV
    heavy = jax.random.randint(jax.random.fold_in(key, 41), (KVH, 1, 1), 0, blocks_count)
    rates = jax.random.randint(jax.random.fold_in(key, 42), (KVH, blocks_count, 1), 2, 7)
    rolls = jax.random.randint(jax.random.fold_in(key, 43), (KVH, blocks_count, TOK_DEV), 0, 420)
    place = jnp.arange(TOK_DEV, dtype=jnp.int32)[None, None, :]
    starts = rolls % rates == 0
    chosen = jnp.arange(blocks_count, dtype=jnp.int32)[None, :, None] == heavy
    starts = starts | chosen & (place % 2 == 0) | (place == 0)
    segment = jnp.minimum(jnp.cumsum(starts.astype(jnp.int32), axis=2) - 1, SLOT_DEV - 1)
    return segment.reshape(KVH, TOKENS).astype(jnp.int32)


def steps_of(key, shape, shards, low, high):
    def one(position, blocks):
        heights = jax.random.uniform(jax.random.fold_in(jax.random.fold_in(key, 6), position), (blocks,), jnp.float32, low / len(shards), high / len(shards))
        return jnp.repeat(jnp.exp(heights), shape[position] // blocks).reshape((-1,) + (1,) * (len(shape) - position - 1))

    loudness = one(*shards[0])
    for cut in shards[1:]:
        loudness = loudness * one(*cut)
    return loudness


def noise(rng, extent, spread, bound, pieces=(), kind=jnp.bfloat16):
    gain = steps_of(rng, extent, pieces, -0.22, 0.18) if pieces else 1.0
    values = jax.random.normal(rng, extent, jnp.float32) * spread * gain
    return jnp.minimum(jnp.maximum(values, -bound), bound).astype(kind)


def setup_inputs(seed: int = 0) -> dict:
    arg_keys = jax.random.split(jax.random.key(seed), 6)
    return {
        "queries": draw_queries(jax.random.fold_in(arg_keys[5], 71), 0),
        "keys": draw_keys(jax.random.fold_in(arg_keys[5], 71), 0),
        "values": noise(arg_keys[2], (TOKENS, KVH * HD), 1.0, 6.0, ((0, 32),)),
        "segment_ids": draw_segment_ids(jax.random.fold_in(arg_keys[5], 71), 0),
        "grad_out": noise(arg_keys[4], (TOKENS, QH * HD), 1.0, 6.0, ((0, 32),)),
    }


masked_score = -1e30


def head_backward(operands):
    query_head, key_head, value_head, cotangent_head, segment_head = operands
    group_size = QH // KVH
    score_scale = HD ** -0.5
    blocks_count = TOKENS // TOK_DEV
    slot_picks = segment_head.reshape(blocks_count, TOK_DEV)[:, :, None] == jnp.arange(SLOT_DEV, dtype=jnp.int32)[None, None, :]
    onehot = slot_picks.astype(jnp.float32)
    counts = jnp.sum(slot_picks.astype(jnp.int32), axis=1)
    slot_sizes = jnp.maximum(counts, 1).astype(jnp.float32)[:, :, None]
    key_sums = jnp.einsum("bts,btd->bsd", onehot, key_head.reshape(blocks_count, TOK_DEV, HD).astype(jnp.float32), precision=lax.Precision.HIGHEST)
    value_sums = jnp.einsum("bts,btd->bsd", onehot, value_head.reshape(blocks_count, TOK_DEV, HD).astype(jnp.float32), precision=lax.Precision.HIGHEST)
    slot_keys = (key_sums / slot_sizes).astype(jnp.bfloat16).reshape(SLOTS, HD)
    slot_values = (value_sums / slot_sizes).astype(jnp.bfloat16).reshape(SLOTS, HD)
    live_flags = (counts > 0).reshape(SLOTS)
    slot_index = jnp.arange(SLOTS, dtype=jnp.int32)
    slot_owner = slot_index // SLOT_DEV
    slot_place = slot_index % SLOT_DEV

    def block_step(carried, inputs):
        key_grads, value_grads = carried
        block_id, query_block, key_block, value_block, cotangent_block, segment_block = inputs
        query_rows = query_block.reshape(TOK_DEV * group_size, HD)
        cotangent_rows = cotangent_block.reshape(TOK_DEV * group_size, HD)
        earlier = slot_owner[None, :] < block_id
        same = (slot_owner[None, :] == block_id) & (slot_place[None, :] < segment_block[:, None])
        visible = live_flags[None, :] & (earlier | same)
        visible = jnp.repeat(visible, group_size, axis=0)
        scores = score_scale * jnp.dot(query_rows, slot_keys.T, preferred_element_type=jnp.float32)
        own_scores = score_scale * jnp.sum(query_block.astype(jnp.float32) * key_block.astype(jnp.float32)[:, None, :], axis=2).reshape(-1)
        maxima = jnp.maximum(jnp.max(jnp.where(visible, scores, masked_score), axis=1), own_scores)
        weights = jnp.exp(jnp.where(visible, scores - maxima[:, None], masked_score))
        own_weights = jnp.exp(own_scores - maxima)
        totals = jnp.sum(weights, axis=1) + own_weights
        probabilities = weights / totals[:, None]
        own_probs = own_weights / totals
        grad_probs = jnp.dot(cotangent_rows, slot_values.T, preferred_element_type=jnp.float32)
        own_grad_probs = jnp.sum(cotangent_block.astype(jnp.float32) * value_block.astype(jnp.float32)[:, None, :], axis=2).reshape(-1)
        deltas = jnp.sum(probabilities * grad_probs, axis=1) + own_probs * own_grad_probs
        grad_scores = probabilities * (grad_probs - deltas[:, None])
        own_grad_scores = own_probs * (own_grad_probs - deltas)
        low_grads = grad_scores.astype(jnp.bfloat16)
        low_probs = probabilities.astype(jnp.bfloat16)
        key_rows = jnp.repeat(key_block.astype(jnp.float32), group_size, axis=0)
        query_grads = score_scale * (jnp.dot(low_grads, slot_keys, preferred_element_type=jnp.float32) + own_grad_scores[:, None] * key_rows)
        key_grads = key_grads + score_scale * jnp.dot(low_grads.T, query_rows, preferred_element_type=jnp.float32)
        value_grads = value_grads + jnp.dot(low_probs.T, cotangent_rows, preferred_element_type=jnp.float32)
        own_key_grads = score_scale * jnp.sum((own_grad_scores[:, None] * query_rows.astype(jnp.float32)).reshape(TOK_DEV, group_size, HD), axis=1)
        own_value_grads = jnp.sum((own_probs[:, None] * cotangent_rows.astype(jnp.float32)).reshape(TOK_DEV, group_size, HD), axis=1)
        return (key_grads, value_grads), (query_grads.astype(jnp.bfloat16).reshape(TOK_DEV, group_size * HD), own_key_grads, own_value_grads)

    zero_grads = jnp.zeros((SLOTS, HD), jnp.float32)
    inputs = (jnp.arange(blocks_count, dtype=jnp.int32),
              query_head.reshape(blocks_count, TOK_DEV, group_size, HD),
              key_head.reshape(blocks_count, TOK_DEV, HD),
              value_head.reshape(blocks_count, TOK_DEV, HD),
              cotangent_head.reshape(blocks_count, TOK_DEV, group_size, HD),
              segment_head.reshape(blocks_count, TOK_DEV))
    (key_grads, value_grads), (query_grads, own_key_grads, own_value_grads) = lax.scan(block_step, (zero_grads, zero_grads), inputs)
    token_slots = ((jnp.arange(TOKENS, dtype=jnp.int32) // TOK_DEV) * SLOT_DEV + segment_head).astype(jnp.int32)
    token_sizes = counts.reshape(SLOTS)[token_slots].astype(jnp.float32)
    grad_keys = (key_grads[token_slots] / token_sizes[:, None] + own_key_grads.reshape(TOKENS, HD)).astype(jnp.bfloat16)
    grad_values = (value_grads[token_slots] / token_sizes[:, None] + own_value_grads.reshape(TOKENS, HD)).astype(jnp.bfloat16)
    return query_grads.reshape(TOKENS, group_size * HD), grad_keys, grad_values


def reference(queries, keys, values, segment_ids, grad_out):
    group_size = QH // KVH
    query_stack = queries.reshape(TOKENS, KVH, group_size, HD).transpose(1, 0, 2, 3)
    key_stack = keys.reshape(TOKENS, KVH, HD).transpose(1, 0, 2)
    value_stack = values.reshape(TOKENS, KVH, HD).transpose(1, 0, 2)
    cotangent_stack = grad_out.reshape(TOKENS, KVH, group_size, HD).transpose(1, 0, 2, 3)
    query_grads, grad_keys, grad_values = lax.map(head_backward, (query_stack, key_stack, value_stack, cotangent_stack, segment_ids))
    return (query_grads.transpose(1, 0, 2).reshape(TOKENS, QH * HD),
            grad_keys.transpose(1, 0, 2).reshape(TOKENS, KVH * HD),
            grad_values.transpose(1, 0, 2).reshape(TOKENS, KVH * HD))
```

```python
import functools

import jax
import jax.numpy as jnp
from jax import lax
from jax.experimental import pallas as pl
from jax.experimental.pallas import tpu as pltpu
from jax.sharding import PartitionSpec as P

QH = 64
KVH = 8
HD = 128
SLOT_DEV = 96
GROUP = QH // KVH
SCALE = HD ** (-0.5)
LOG2E = 1.4426950408889634
DEAD = 1024.0
HIDDEN = 2.0**96
PAIR = 2


def nt(a, b):
    return lax.dot_general(a, b, (((1,), (1,)), ((), ())), preferred_element_type=jnp.float32)


def nn(a, b):
    return lax.dot_general(a, b, (((1,), (0,)), ((), ())), preferred_element_type=jnp.float32)


def tn(a, b):
    return lax.dot_general(a, b, (((0,), (0,)), ((), ())), preferred_element_type=jnp.float32)


def slot_picks(seg_row, tokens):
    return lax.broadcasted_iota(jnp.int32, (SLOT_DEV, tokens), 0) == seg_row


def merge_kernel(seg_ref, kv_ref, out_ref):
    kv_heads, tokens = seg_ref.shape
    for g in range(kv_heads):
        picks = slot_picks(seg_ref[g : g + 1, :], tokens).astype(jnp.float32)
        counts = jnp.sum(picks, axis=1, keepdims=True)
        sums = nn(picks.astype(jnp.bfloat16), kv_ref[:, g * 2 * HD : (g + 1) * 2 * HD])
        rows = sums / jnp.maximum(counts, 1.0)
        is_key = lax.broadcasted_iota(jnp.int32, rows.shape, 1) < HD
        rows = jnp.where((counts == 0.0) & is_key, DEAD, rows)
        out_ref[:, g * 2 * HD : (g + 1) * 2 * HD] = rows.astype(jnp.bfloat16)


def attend_kernel(g, steps, place_ref, seg_ref, segcol_ref, kvtok_ref, qo_ref, *refs):
    blocks = refs[: 2 * steps]
    dq_ref, near_ref, far_ref, own_ref, kx, vx, kt = refs[2 * steps :]
    tokens = kvtok_ref.shape[0]
    slots = 2 * steps * SLOT_DEV
    outer = place_ref[0]
    inner = place_ref[1]
    base = g * 2 * HD
    lane = lax.broadcasted_iota(jnp.int32, (SLOT_DEV, HD), 1)
    row = lax.broadcasted_iota(jnp.int32, (SLOT_DEV, HD), 0)
    for r, block in enumerate(blocks):
        rows = pl.ds(r * SLOT_DEV, SLOT_DEV)
        key = block[:, base : base + HD].astype(jnp.float32)
        if r == 0:
            extra = jnp.where(lane == row, 1.0, 0.0)
        else:
            step = r % steps
            if step == 0:
                there = inner == 1
            else:
                there = outer >= step
            hide = (key[:, 0:1] > 100.0) | jnp.logical_not(there)
            extra = jnp.where(hide & (lane >= SLOT_DEV), -HIDDEN, 0.0)
        key = jnp.where(key > 100.0, 0.0, key)
        kx[rows, 0:HD] = key.astype(jnp.bfloat16)
        kx[rows, HD : 2 * HD] = extra.astype(jnp.bfloat16)
        vx[rows, :] = block[:, base + HD : base + 2 * HD]
    kx[slots : slots + tokens, 0:HD] = kvtok_ref[:, base : base + HD]
    kx[slots : slots + tokens, HD : 2 * HD] = jnp.zeros((tokens, HD), jnp.bfloat16)
    vx[slots : slots + tokens, :] = kvtok_ref[:, base + HD : base + 2 * HD]
    kt[...] = kx[:, 0:HD].astype(jnp.float32).T.astype(jnp.bfloat16)

    qlane = lax.broadcasted_iota(jnp.int32, (tokens, HD), 1)
    late = (qlane >= segcol_ref[:, g : g + 1]) & (qlane < SLOT_DEV)
    qe = jnp.where(late, -HIDDEN, jnp.where(qlane == SLOT_DEV, 1.0, 0.0)).astype(jnp.bfloat16)
    qe = jnp.concatenate([qe] * PAIR, axis=0)
    width = PAIR * tokens
    eye_row = lax.broadcasted_iota(jnp.int32, (tokens, width), 0)
    eye_lane = lax.broadcasted_iota(jnp.int32, (tokens, width), 1)
    eye = eye_row == lax.rem(eye_lane, tokens)
    factor = SCALE * LOG2E

    dk = None
    dv = None
    for first in range(0, GROUP, PAIR):
        q2 = jnp.concatenate(
            [qo_ref[:, (first + i) * HD : (first + i + 1) * HD] for i in range(PAIR)], axis=0
        )
        o2 = jnp.concatenate(
            [
                qo_ref[:, (GROUP + first + i) * HD : (GROUP + first + i + 1) * HD]
                for i in range(PAIR)
            ],
            axis=0,
        )
        scores = nt(kx[...], jnp.concatenate([q2, qe], axis=1))
        own_score = jnp.sum(jnp.where(eye, scores[slots:], 0.0), axis=0, keepdims=True)
        scores = scores[:slots]
        top = jnp.maximum(jnp.max(scores, axis=0, keepdims=True), own_score)
        weights = jnp.exp2((scores - top) * factor)
        own_weight = jnp.exp2((own_score - top) * factor)
        inverse = 1.0 / (jnp.sum(weights, axis=0, keepdims=True) + own_weight)
        probs = weights * inverse
        own_prob = own_weight * inverse
        grad_probs = nt(vx[...], o2)
        own_grad_prob = jnp.sum(jnp.where(eye, grad_probs[slots:], 0.0), axis=0, keepdims=True)
        grad_probs = grad_probs[:slots]
        delta = jnp.sum(probs * grad_probs, axis=0, keepdims=True) + own_prob * own_grad_prob
        grad_scores = probs * (grad_probs - delta)
        own_grad_score = own_prob * (own_grad_prob - delta)
        low_probs = jnp.concatenate(
            [probs.astype(jnp.bfloat16), jnp.where(eye, own_prob, 0.0).astype(jnp.bfloat16)], axis=0
        )
        low_grads = jnp.concatenate(
            [
                grad_scores.astype(jnp.bfloat16),
                jnp.where(eye, own_grad_score, 0.0).astype(jnp.bfloat16),
            ],
            axis=0,
        )
        dv_part = nn(low_probs, o2)
        dk_part = nn(low_grads, q2)
        dv = dv_part if dv is None else dv + dv_part
        dk = dk_part if dk is None else dk + dk_part
        dq = (SCALE * nn(kt[...], low_grads)).T.astype(jnp.bfloat16)
        for i in range(PAIR):
            dq_ref[:, (first + i) * HD : (first + i + 1) * HD] = dq[i * tokens : (i + 1) * tokens]
    dk = dk * SCALE
    half = steps * SLOT_DEV
    near_ref[:, 0:HD] = dk[:half].astype(near_ref.dtype)
    near_ref[:, HD : 2 * HD] = dv[:half].astype(near_ref.dtype)
    far_ref[:, 0:HD] = dk[half:slots].astype(far_ref.dtype)
    far_ref[:, HD : 2 * HD] = dv[half:slots].astype(far_ref.dtype)
    own_ref[:, 0:HD] = dk[slots:]
    own_ref[:, HD : 2 * HD] = dv[slots:]


def spread_kernel(steps, seg_ref, *refs):
    kv_heads, tokens = seg_ref.shape
    gk_ref, gv_ref = refs[-2:]
    per_head = steps + 1
    for g in range(kv_heads):
        parts = refs[g * per_head : (g + 1) * per_head]
        total = parts[0][...].astype(jnp.float32)
        for part in parts[1:steps]:
            total = total + part[...].astype(jnp.float32)
        picks = slot_picks(seg_ref[g : g + 1, :], tokens).astype(jnp.float32)
        counts = jnp.sum(picks, axis=1, keepdims=True)
        total = total / jnp.maximum(counts, 1.0)
        high = total.astype(jnp.bfloat16)
        low = (total - high.astype(jnp.float32)).astype(jnp.bfloat16)
        picks = picks.astype(jnp.bfloat16)
        spread = tn(picks, high) + tn(picks, low) + parts[steps][...]
        gk_ref[:, g * HD : (g + 1) * HD] = spread[:, 0:HD].astype(jnp.bfloat16)
        gv_ref[:, g * HD : (g + 1) * HD] = spread[:, HD : 2 * HD].astype(jnp.bfloat16)


def vmem_spec():
    return pl.BlockSpec(memory_space=pltpu.VMEM)


def smem_spec():
    return pl.BlockSpec(memory_space=pltpu.SMEM)


def params():
    return pltpu.CompilerParams(vmem_limit_bytes=28 * 2**20)


def local(queries, keys, values, segment_ids, grad_out):
    rows = queries.shape[0]
    heads = lax.axis_size("head")
    tokens = rows * heads
    kv_heads = KVH // heads
    shards = lax.axis_size("ctx")
    steps = shards // 2
    me = lax.axis_index("ctx")
    place = jnp.stack([me // 2, me % 2]).astype(jnp.int32)
    swap = [(c, c ^ 1) for c in range(shards)]

    kv = jnp.stack(
        [keys.reshape(rows, heads, kv_heads, HD), values.reshape(rows, heads, kv_heads, HD)], axis=3
    )
    kv = lax.all_to_all(
        kv.reshape(rows, heads * kv_heads * 2 * HD), "head", split_axis=1, concat_axis=0, tiled=True
    )
    q_parts = queries.reshape(rows, heads, kv_heads, GROUP * HD)
    o_parts = grad_out.reshape(rows, heads, kv_heads, GROUP * HD)
    qo = []
    for g in range(kv_heads):
        both = jnp.concatenate([q_parts[:, :, g], o_parts[:, :, g]], axis=2)
        qo.append(
            lax.all_to_all(
                both.reshape(rows, heads * 2 * GROUP * HD),
                "head",
                split_axis=1,
                concat_axis=0,
                tiled=True,
            )
        )

    merged = pl.pallas_call(
        merge_kernel,
        out_shape=jax.ShapeDtypeStruct((SLOT_DEV, kv_heads * 2 * HD), jnp.bfloat16),
        in_specs=[vmem_spec(), vmem_spec()],
        out_specs=vmem_spec(),
        compiler_params=params(),
        name="merge",
    )(segment_ids, kv)

    near = [merged]
    for k in range(1, steps):
        near.append(lax.ppermute(merged, "ctx", [(c, c + 2 * k) for c in range(shards - 2 * k)]))
    far = [lax.ppermute(block, "ctx", swap) for block in near]
    blocks = near + far

    seg_col = segment_ids.T
    slots = shards * SLOT_DEV
    half = steps * SLOT_DEV
    dq = []
    spread_args = []
    for g in range(kv_heads):
        dq_g, near_g, far_g, own_g = pl.pallas_call(
            functools.partial(attend_kernel, g, steps),
            out_shape=(
                jax.ShapeDtypeStruct((tokens, GROUP * HD), jnp.bfloat16),
                jax.ShapeDtypeStruct((half, 2 * HD), jnp.float32),
                jax.ShapeDtypeStruct((half, 2 * HD), jnp.bfloat16),
                jax.ShapeDtypeStruct((tokens, 2 * HD), jnp.float32),
            ),
            in_specs=[smem_spec()] + [vmem_spec()] * (4 + shards),
            out_specs=[vmem_spec()] * 4,
            scratch_shapes=[
                pltpu.VMEM((slots + tokens, 2 * HD), jnp.bfloat16),
                pltpu.VMEM((slots + tokens, HD), jnp.bfloat16),
                pltpu.VMEM((HD, slots + tokens), jnp.bfloat16),
            ],
            compiler_params=params(),
            cost_estimate=pl.CostEstimate(
                flops=10 * tokens * GROUP * (slots + tokens) * HD,
                bytes_accessed=4 * 2**20,
                transcendentals=tokens * GROUP * slots,
            ),
            name="attend",
        )(place, segment_ids, seg_col, kv, qo[g], *blocks)
        dq.append(dq_g)
        sums = near_g + lax.ppermute(far_g, "ctx", swap).astype(jnp.float32)
        low_sums = sums.astype(jnp.bfloat16)
        spread_args.append(sums[:SLOT_DEV])
        for k in range(1, steps):
            part = low_sums[k * SLOT_DEV : (k + 1) * SLOT_DEV]
            spread_args.append(
                lax.ppermute(part, "ctx", [(c, c - 2 * k) for c in range(2 * k, shards)])
            )
        spread_args.append(own_g)

    grad_keys, grad_values = pl.pallas_call(
        functools.partial(spread_kernel, steps),
        out_shape=(jax.ShapeDtypeStruct((tokens, kv_heads * HD), jnp.bfloat16),) * 2,
        in_specs=[vmem_spec()] * (1 + len(spread_args)),
        out_specs=[vmem_spec()] * 2,
        compiler_params=params(),
        name="spread",
    )(segment_ids, *spread_args)
    return jnp.concatenate(dq, axis=1), grad_keys, grad_values


def solution(mesh):
    return jax.shard_map(
        local,
        mesh=mesh,
        in_specs=(
            P(("ctx", "head"), None),
            P(("ctx", "head"), None),
            P(("ctx", "head"), None),
            P("head", "ctx"),
            P(("ctx", "head"), None),
        ),
        out_specs=(P("ctx", "head"), P("ctx", "head"), P("ctx", "head")),
        check_vma=False,
    )
```

```python
import functools

import jax
import jax.numpy as jnp
from jax import lax
from jax.experimental import pallas as pl
from jax.experimental.pallas import tpu as pltpu
from jax.sharding import PartitionSpec as P

QH = 64
KVH = 8
HD = 128
SLOT_DEV = 96
GROUP = QH // KVH
GW = GROUP * HD
SCALE = HD ** (-0.5)
LOG2E = 1.4426950408889634
DEAD = 1024.0
HIDDEN = 2.0**96
NEAR = 4


def nt(a, b):
    return lax.dot_general(a, b, (((1,), (1,)), ((), ())), preferred_element_type=jnp.float32)


def nn(a, b):
    return lax.dot_general(a, b, (((1,), (0,)), ((), ())), preferred_element_type=jnp.float32)


def tn(a, b):
    return lax.dot_general(a, b, (((0,), (0,)), ((), ())), preferred_element_type=jnp.float32)


def slot_picks(seg_row, tokens):
    return lax.broadcasted_iota(jnp.int32, (SLOT_DEV, tokens), 0) == seg_row


def lanes(start, size):
    return pl.ds(pl.multiple_of(start, HD), size)


def pack_kv_kernel(kv_heads, place_ref, key_ref, value_ref, *out_refs):
    me = place_ref[1]
    for m, out in enumerate(out_refs):
        other = lax.bitwise_xor(me, m)
        for g in range(kv_heads):
            start = (other * kv_heads + g) * HD
            out[:, 2 * g * HD : (2 * g + 1) * HD] = key_ref[:, lanes(start, HD)]
            out[:, (2 * g + 1) * HD : (2 * g + 2) * HD] = value_ref[:, lanes(start, HD)]


def pack_qo_kernel(kv_heads, heads, place_ref, q_ref, o_ref, *refs):
    outs, sems = refs[:-1], refs[-1]
    me = place_ref[1]
    copies = []
    for g in range(kv_heads):
        for m in range(1, heads):
            start = (lax.bitwise_xor(me, m) * kv_heads + g) * GW
            out = outs[g * (heads - 1) + m - 1]
            for part, source in enumerate((q_ref, o_ref)):
                copies.append(
                    pltpu.make_async_copy(
                        source.at[:, lanes(start, GW)],
                        out.at[:, part * GW : (part + 1) * GW],
                        sems.at[len(copies)],
                    )
                )
    for copy in copies:
        copy.start()
    for copy in copies:
        copy.wait()


def merge_kernel(heads, place_ref, seg_ref, *refs):
    pieces, outs, whole = refs[:heads], refs[heads:-1], refs[-1]
    tokens = seg_ref.shape[1]
    rows = tokens // heads
    me = place_ref[1]
    for m, piece in enumerate(pieces):
        start = pl.multiple_of(lax.bitwise_xor(me, m) * rows, 16)
        whole[pl.ds(start, rows), :] = piece[...]
    for g, out in enumerate(outs):
        picks = slot_picks(seg_ref[g : g + 1, :], tokens).astype(jnp.float32)
        counts = jnp.sum(picks, axis=1, keepdims=True)
        sums = nn(picks.astype(jnp.bfloat16), whole[:, g * 2 * HD : (g + 1) * 2 * HD])
        merged = sums / jnp.maximum(counts, 1.0)
        is_key = lax.broadcasted_iota(jnp.int32, merged.shape, 1) < HD
        out[...] = jnp.where((counts == 0.0) & is_key, DEAD, merged).astype(jnp.bfloat16)


def attend_kernel(g, order, heads, place_ref, segcol_ref, q_ref, o_ref, *refs):
    shards = len(order)
    kv_pieces, refs = refs[:heads], refs[heads:]
    qo_pieces, refs = refs[: heads - 1], refs[heads - 1 :]
    blocks, refs = refs[:shards], refs[shards:]
    dq_ref, own_ref, refs = refs[0], refs[1], refs[2:]
    term_refs, (kx, vx, kt, mine, sems) = refs[:-5], refs[-5:]
    rows = kv_pieces[0].shape[0]
    slots = shards * SLOT_DEV
    shard = place_ref[0]
    me = place_ref[1]
    start = (me * kv_pieces[0].shape[1] // (2 * HD) + g) * GW
    copies = [
        pltpu.make_async_copy(
            source.at[:, lanes(start, GW)], mine.at[:, part * GW : (part + 1) * GW], sems.at[part]
        )
        for part, source in enumerate((q_ref, o_ref))
    ]
    for copy in copies:
        copy.start()

    lane = lax.broadcasted_iota(jnp.int32, (SLOT_DEV, HD), 1)
    row = lax.broadcasted_iota(jnp.int32, (SLOT_DEV, HD), 0)
    for r, (m, block) in enumerate(zip(order, blocks)):
        at = pl.ds(r * SLOT_DEV, SLOT_DEV)
        key = block[:, 0:HD].astype(jnp.float32)
        if m == 0:
            extra = jnp.where(lane == row, 1.0, 0.0)
        else:
            hide = (key[:, 0:1] > 100.0) | (lax.bitwise_xor(shard, m) > shard)
            extra = jnp.where(hide & (lane >= SLOT_DEV), -HIDDEN, 0.0)
        kx[at, 0:HD] = jnp.where(key > 100.0, 0.0, key).astype(jnp.bfloat16)
        kx[at, HD : 2 * HD] = extra.astype(jnp.bfloat16)
        vx[at, :] = block[:, HD : 2 * HD]
    kx[slots : slots + rows, HD : 2 * HD] = jnp.zeros((rows, HD), jnp.bfloat16)
    kt[...] = kx[0:slots, 0:HD].astype(jnp.float32).T.astype(jnp.bfloat16)

    width = GROUP * rows
    qlane = lax.broadcasted_iota(jnp.int32, (rows, HD), 1)
    eye_row = lax.broadcasted_iota(jnp.int32, (rows, width), 0)
    eye_lane = lax.broadcasted_iota(jnp.int32, (rows, width), 1)
    eye = eye_row == lax.rem(eye_lane, rows)
    factor = SCALE * LOG2E
    for copy in copies:
        copy.wait()

    dk = None
    dv = None
    for m in range(heads):
        qo = mine if m == 0 else qo_pieces[m - 1]
        at = pl.ds(pl.multiple_of(lax.bitwise_xor(me, m) * rows, 16), rows)
        own_key = kv_pieces[m][:, 2 * g * HD : (2 * g + 1) * HD]
        kx[slots : slots + rows, 0:HD] = own_key
        vx[slots : slots + rows, :] = kv_pieces[m][:, (2 * g + 1) * HD : (2 * g + 2) * HD]
        late = (qlane >= segcol_ref[at, g : g + 1]) & (qlane < SLOT_DEV)
        qe = jnp.where(late, -HIDDEN, jnp.where(qlane == SLOT_DEV, 1.0, 0.0)).astype(jnp.bfloat16)
        q2 = jnp.concatenate([qo[:, h * HD : (h + 1) * HD] for h in range(GROUP)], axis=0)
        o2 = jnp.concatenate([qo[:, GW + h * HD : GW + (h + 1) * HD] for h in range(GROUP)], axis=0)
        qx = jnp.concatenate([q2, jnp.concatenate([qe] * GROUP, axis=0)], axis=1)
        scores = nt(kx[...], qx)
        own_score = jnp.sum(jnp.where(eye, scores[slots:], 0.0), axis=0, keepdims=True)
        scores = scores[:slots]
        top = jnp.maximum(jnp.max(scores, axis=0, keepdims=True), own_score)
        weights = jnp.exp2((scores - top) * factor)
        own_weight = jnp.exp2((own_score - top) * factor)
        inverse = 1.0 / (jnp.sum(weights, axis=0, keepdims=True) + own_weight)
        probs = weights * inverse
        own_prob = own_weight * inverse
        grad_probs = nt(vx[...], o2)
        own_grad_prob = jnp.sum(jnp.where(eye, grad_probs[slots:], 0.0), axis=0, keepdims=True)
        grad_probs = grad_probs[:slots]
        delta = jnp.sum(probs * grad_probs, axis=0, keepdims=True) + own_prob * own_grad_prob
        low_grads = (probs * (grad_probs - delta)).astype(jnp.bfloat16)
        low_probs = probs.astype(jnp.bfloat16)
        own_grad_score = own_prob * (own_grad_prob - delta)
        own_low_probs = jnp.where(eye, own_prob, 0.0).astype(jnp.bfloat16)
        own_low_grads = jnp.where(eye, own_grad_score, 0.0).astype(jnp.bfloat16)
        dv_part = nn(low_probs, o2)
        dk_part = nn(low_grads, q2)
        dv = dv_part if dv is None else dv + dv_part
        dk = dk_part if dk is None else dk + dk_part
        own_ref[at, 0:HD] = SCALE * nn(own_low_grads, q2)
        own_ref[at, HD : 2 * HD] = nn(own_low_probs, o2)
        dq = nn(kt[...], low_grads) + tn(own_key, own_low_grads)
        dq = (SCALE * dq).T.astype(jnp.bfloat16)
        for h in range(GROUP):
            dq_ref[at, h * HD : (h + 1) * HD] = dq[h * rows : (h + 1) * rows]
    dk = dk * SCALE
    span = slots // len(term_refs)
    for m, term in enumerate(term_refs):
        part = slice(m * span, (m + 1) * span)
        term[:, 0:HD] = dk[part].astype(term.dtype)
        term[:, HD : 2 * HD] = dv[part].astype(term.dtype)


def spread_kernel(parts_per_head, seg_ref, *refs):
    kv_heads, tokens = seg_ref.shape
    gk_ref, gv_ref = refs[-2:]
    for g in range(kv_heads):
        parts = refs[g * parts_per_head : (g + 1) * parts_per_head]
        total = parts[0][...].astype(jnp.float32)
        for part in parts[1:-1]:
            total = total + part[...].astype(jnp.float32)
        picks = slot_picks(seg_ref[g : g + 1, :], tokens).astype(jnp.float32)
        counts = jnp.sum(picks, axis=1, keepdims=True)
        total = total / jnp.maximum(counts, 1.0)
        high = total.astype(jnp.bfloat16)
        low = (total - high.astype(jnp.float32)).astype(jnp.bfloat16)
        picks = picks.astype(jnp.bfloat16)
        spread = tn(picks, high) + tn(picks, low) + parts[-1][...]
        gk_ref[:, g * HD : (g + 1) * HD] = spread[:, 0:HD].astype(jnp.bfloat16)
        gv_ref[:, g * HD : (g + 1) * HD] = spread[:, HD : 2 * HD].astype(jnp.bfloat16)


def in_vmem(count):
    return [pl.BlockSpec(memory_space=pltpu.VMEM)] * count


def in_smem():
    return [pl.BlockSpec(memory_space=pltpu.SMEM)]


def anywhere(count):
    return [pl.BlockSpec(memory_space=pl.ANY)] * count


def params():
    return pltpu.CompilerParams(vmem_limit_bytes=28 * 2**20)


def shape(*dims, dtype=jnp.bfloat16):
    return jax.ShapeDtypeStruct(dims, dtype)


def swap(x, axis, size, m):
    return lax.ppermute(x, axis, [(i, i ^ m) for i in range(size)])


def local(queries, keys, values, segment_ids, grad_out):
    rows = queries.shape[0]
    heads = lax.axis_size("head")
    tokens = rows * heads
    kv_heads = KVH // heads
    shards = lax.axis_size("ctx")
    place = jnp.stack([lax.axis_index("ctx"), lax.axis_index("head")]).astype(jnp.int32)
    near = min(NEAR, shards)
    far = shards // near
    order = [m + near * h for m in range(near) for h in range(far)]

    kv_out = pl.pallas_call(
        functools.partial(pack_kv_kernel, kv_heads),
        out_shape=[shape(rows, kv_heads * 2 * HD)] * heads,
        in_specs=in_smem() + in_vmem(2),
        out_specs=in_vmem(heads),
        compiler_params=params(),
        name="pack_kv",
    )(place, keys, values)
    kv = [kv_out[0]] + [swap(kv_out[m], "head", heads, m) for m in range(1, heads)]

    qo_out = pl.pallas_call(
        functools.partial(pack_qo_kernel, kv_heads, heads),
        out_shape=[shape(rows, 2 * GW)] * (kv_heads * (heads - 1)),
        in_specs=in_smem() + anywhere(2),
        out_specs=in_vmem(kv_heads * (heads - 1)),
        scratch_shapes=[pltpu.SemaphoreType.DMA((2 * kv_heads * (heads - 1),))],
        compiler_params=params(),
        name="pack_qo",
    )(place, queries, grad_out)
    qo = [
        [swap(qo_out[g * (heads - 1) + m - 1], "head", heads, m) for m in range(1, heads)]
        for g in range(kv_heads)
    ]

    merged = pl.pallas_call(
        functools.partial(merge_kernel, heads),
        out_shape=[shape(SLOT_DEV, 2 * HD)] * kv_heads,
        in_specs=in_smem() + in_vmem(1 + heads),
        out_specs=in_vmem(kv_heads),
        scratch_shapes=[pltpu.VMEM((tokens, kv_heads * 2 * HD), jnp.bfloat16)],
        compiler_params=params(),
        name="merge",
    )(place, segment_ids, *kv)

    seg_col = segment_ids.T
    slots = shards * SLOT_DEV
    span = far * SLOT_DEV
    dq = []
    spread_args = []
    for g in range(kv_heads):
        held = {0: merged[g]}
        for h in range(1, far):
            held[near * h] = swap(merged[g], "ctx", shards, near * h)
        for h in range(far):
            for m in range(1, near):
                held[near * h + m] = swap(held[near * h], "ctx", shards, m)
        outs = pl.pallas_call(
            functools.partial(attend_kernel, g, order, heads),
            out_shape=[shape(tokens, GW), shape(tokens, 2 * HD, dtype=jnp.float32)]
            + [shape(span, 2 * HD, dtype=jnp.float32)]
            + [shape(span, 2 * HD)] * (near - 1),
            in_specs=in_smem()
            + in_vmem(1)
            + anywhere(2)
            + in_vmem(heads + heads - 1 + shards),
            out_specs=in_vmem(2 + near),
            scratch_shapes=[
                pltpu.VMEM((slots + rows, 2 * HD), jnp.bfloat16),
                pltpu.VMEM((slots + rows, HD), jnp.bfloat16),
                pltpu.VMEM((HD, slots), jnp.bfloat16),
                pltpu.VMEM((rows, 2 * GW), jnp.bfloat16),
                pltpu.SemaphoreType.DMA((2,)),
            ],
            compiler_params=params(),
            cost_estimate=pl.CostEstimate(
                flops=10 * tokens * GROUP * (slots + rows) * HD,
                bytes_accessed=4 * 2**20,
                transcendentals=tokens * GROUP * slots,
            ),
            name="attend",
        )(place, seg_col, queries, grad_out, *kv, *qo[g], *[held[m] for m in order])
        dq.append(outs[0])
        sums = outs[2]
        for m in range(1, near):
            sums = sums + swap(outs[2 + m], "ctx", shards, m).astype(jnp.float32)
        spread_args.append(sums[:SLOT_DEV])
        for h in range(1, far):
            part = sums[h * SLOT_DEV : (h + 1) * SLOT_DEV].astype(jnp.bfloat16)
            spread_args.append(swap(part, "ctx", shards, near * h))
        spread_args.append(outs[1])

    grad_keys, grad_values = pl.pallas_call(
        functools.partial(spread_kernel, far + 1),
        out_shape=[shape(tokens, kv_heads * HD)] * 2,
        in_specs=in_vmem(1 + len(spread_args)),
        out_specs=in_vmem(2),
        compiler_params=params(),
        name="spread",
    )(segment_ids, *spread_args)
    return jnp.concatenate(dq, axis=1), grad_keys, grad_values


def solution(mesh):
    return jax.shard_map(
        local,
        mesh=mesh,
        in_specs=(
            P(("ctx", "head"), None),
            P(("ctx", "head"), None),
            P(("ctx", "head"), None),
            P("head", "ctx"),
            P(("ctx", "head"), None),
        ),
        out_specs=(P("ctx", "head"), P("ctx", "head"), P("ctx", "head")),
        check_vma=False,
    )
```

```python
import functools

import jax
import jax.numpy as jnp
from jax import lax
from jax.experimental import pallas as pl
from jax.experimental.pallas import tpu as pltpu
from jax.sharding import PartitionSpec as P

QH = 64
KVH = 8
HD = 128
SLOT_DEV = 96
GROUP = QH // KVH
GW = GROUP * HD
SCALE = HD ** (-0.5)
LOG2E = 1.4426950408889634
DEAD = 1024.0
HIDDEN = 2.0**96


def nt(a, b):
    return lax.dot_general(a, b, (((1,), (1,)), ((), ())), preferred_element_type=jnp.float32)


def nn(a, b):
    return lax.dot_general(a, b, (((1,), (0,)), ((), ())), preferred_element_type=jnp.float32)


def tn(a, b):
    return lax.dot_general(a, b, (((0,), (0,)), ((), ())), preferred_element_type=jnp.float32)


def slot_picks(seg_row, tokens):
    return lax.broadcasted_iota(jnp.int32, (SLOT_DEV, tokens), 0) == seg_row


def lanes(start, size):
    return pl.ds(pl.multiple_of(start, HD), size)


def run_copies(copies):
    for copy in copies:
        copy.start()
    return copies


def wait_copies(copies):
    for copy in copies:
        copy.wait()


def pack_kernel(jobs, place_ref, *refs):
    outs = [out for _, dests in jobs for out in dests]
    sources, out_refs, sems = refs[:2], refs[-len(outs) - 1 : -1], refs[-1]
    me = place_ref[1]
    copies = []
    done = 0
    for width, dests in jobs:
        for out, pieces in zip(out_refs[done:], dests):
            for at, (m, scale, offset) in enumerate(pieces):
                start = lax.bitwise_xor(me, m) * scale + offset
                for part, source in enumerate(sources):
                    rows = source.shape[0]
                    copies.append(
                        pltpu.make_async_copy(
                            source.at[:, lanes(start, width)],
                            out.at[at * rows : (at + 1) * rows, part * width : (part + 1) * width],
                            sems.at[len(copies)],
                        )
                    )
        done += len(dests)
    wait_copies(run_copies(copies))


def gate_kernel(*refs):
    pass


def join_kernel(core_ref, across_ref, *refs):
    out, sems = refs[-2:]
    rows = core_ref.shape[0]
    wait_copies(
        run_copies(
            [
                pltpu.make_async_copy(core_ref, out.at[0:rows, :], sems.at[0]),
                pltpu.make_async_copy(
                    across_ref.at[rows : 2 * rows, :], out.at[rows : 2 * rows, :], sems.at[1]
                ),
            ]
        )
    )


def merge_kernel(place_ref, seg_ref, own_ref, across_ref, core_ref, out, whole):
    kv_heads, tokens = seg_ref.shape
    rows = own_ref.shape[0]
    me = place_ref[1]
    for m, (piece, half) in enumerate(((own_ref, 0), (core_ref, 0), (across_ref, 0), (core_ref, 1))):
        start = pl.multiple_of(lax.bitwise_xor(me, m) * rows, 16)
        whole[pl.ds(start, rows), :] = piece[half * rows : (half + 1) * rows, :]
    for g in range(kv_heads):
        picks = slot_picks(seg_ref[g : g + 1, :], tokens).astype(jnp.float32)
        counts = jnp.sum(picks, axis=1, keepdims=True)
        low_picks = picks.astype(jnp.bfloat16)
        sizes = jnp.maximum(counts, 1.0)
        for part in range(2):
            at = slice((part * kv_heads + g) * HD, (part * kv_heads + g + 1) * HD)
            rows_out = nn(low_picks, whole[:, at]) / sizes
            if part == 0:
                rows_out = jnp.where(counts == 0.0, DEAD, rows_out)
            out[:, at] = rows_out.astype(jnp.bfloat16)


def attend_kernel(
    g, order, qo_at, place_ref, segcol_ref, q_ref, o_ref, kvo_ref, kva_ref, kvc_ref, *refs
):
    shards = len(order)
    heads = 4
    kv_pieces = ((kvo_ref, 0), (kvc_ref, 0), (kva_ref, 0), (kvc_ref, 1))
    qo_pieces = [(refs[shards + i], half) for i, half in qo_at]
    blocks, refs = refs[:shards], refs[-12:]
    dq_ref, own_ref, near_ref, far_ref = refs[:4]
    kx, vx, kt, qo_all, kv_own, qo_sems, kv_sems, block_sems = refs[4:]
    rows = q_ref.shape[0]
    kv_heads = kvo_ref.shape[1] // (2 * HD)
    slots = shards * SLOT_DEV
    shard = place_ref[0]
    me = place_ref[1]
    key_at = slice(g * HD, (g + 1) * HD)
    value_at = slice((kv_heads + g) * HD, (kv_heads + g + 1) * HD)

    block_copies = []
    for r, block in enumerate(blocks):
        at = pl.ds(r * SLOT_DEV, SLOT_DEV)
        block_copies.append(
            pltpu.make_async_copy(block.at[:, key_at], kx.at[at, 0:HD], block_sems.at[2 * r])
        )
        block_copies.append(
            pltpu.make_async_copy(block.at[:, value_at], vx.at[at, :], block_sems.at[2 * r + 1])
        )
    kv_copies = []
    for m, (piece, half) in enumerate(kv_pieces):
        for part, at in enumerate((key_at, value_at)):
            kv_copies.append(
                pltpu.make_async_copy(
                    piece.at[half * rows : (half + 1) * rows, at],
                    kv_own.at[m, part],
                    kv_sems.at[2 * m + part],
                )
            )
    start = (me * kv_heads + g) * GW
    qo_copies = [
        pltpu.make_async_copy(
            source.at[:, lanes(start, GW)],
            qo_all.at[0, :, part * GW : (part + 1) * GW],
            qo_sems.at[part],
        )
        for part, source in enumerate((q_ref, o_ref))
    ]
    for m, (piece, half) in enumerate(qo_pieces):
        qo_copies.append(
            pltpu.make_async_copy(
                piece.at[half * rows : (half + 1) * rows, :], qo_all.at[m + 1], qo_sems.at[m + 2]
            )
        )
    run_copies(block_copies)
    run_copies(kv_copies)
    run_copies(qo_copies)
    wait_copies(block_copies)

    lane = lax.broadcasted_iota(jnp.int32, (SLOT_DEV, HD), 1)
    row = lax.broadcasted_iota(jnp.int32, (SLOT_DEV, HD), 0)
    for r, m in enumerate(order):
        at = pl.ds(r * SLOT_DEV, SLOT_DEV)
        key = kx[at, 0:HD].astype(jnp.float32)
        if m == 0:
            extra = jnp.where(lane == row, 1.0, 0.0)
        else:
            hide = (key[:, 0:1] > 100.0) | (lax.bitwise_xor(shard, m) > shard)
            extra = jnp.where(hide & (lane >= SLOT_DEV), -HIDDEN, 0.0)
        kx[at, 0:HD] = jnp.where(key > 100.0, 0.0, key).astype(jnp.bfloat16)
        kx[at, HD : 2 * HD] = extra.astype(jnp.bfloat16)
    kx[slots : slots + rows, HD : 2 * HD] = jnp.zeros((rows, HD), jnp.bfloat16)
    kt[...] = kx[0:slots, 0:HD].astype(jnp.float32).T.astype(jnp.bfloat16)

    width = GROUP * rows
    qlane = lax.broadcasted_iota(jnp.int32, (rows, HD), 1)
    eye_row = lax.broadcasted_iota(jnp.int32, (rows, width), 0)
    eye_lane = lax.broadcasted_iota(jnp.int32, (rows, width), 1)
    eye = eye_row == lax.rem(eye_lane, rows)
    factor = SCALE * LOG2E
    wait_copies(kv_copies)
    wait_copies(qo_copies)

    dk = None
    dv = None
    for m in range(heads):
        at = pl.ds(pl.multiple_of(lax.bitwise_xor(me, m) * rows, 16), rows)
        own_key = kv_own[m, 0]
        kx[slots : slots + rows, 0:HD] = own_key
        vx[slots : slots + rows, :] = kv_own[m, 1]
        late = (qlane >= segcol_ref[at, g : g + 1]) & (qlane < SLOT_DEV)
        qe = jnp.where(late, -HIDDEN, jnp.where(qlane == SLOT_DEV, 1.0, 0.0)).astype(jnp.bfloat16)
        q2 = jnp.concatenate([qo_all[m, :, h * HD : (h + 1) * HD] for h in range(GROUP)], axis=0)
        o2 = jnp.concatenate(
            [qo_all[m, :, GW + h * HD : GW + (h + 1) * HD] for h in range(GROUP)], axis=0
        )
        qx = jnp.concatenate([q2, jnp.concatenate([qe] * GROUP, axis=0)], axis=1)
        scores = nt(kx[...], qx)
        own_score = jnp.sum(jnp.where(eye, scores[slots:], 0.0), axis=0, keepdims=True)
        scores = scores[:slots]
        top = jnp.maximum(jnp.max(scores, axis=0, keepdims=True), own_score)
        weights = jnp.exp2((scores - top) * factor)
        own_weight = jnp.exp2((own_score - top) * factor)
        inverse = 1.0 / (jnp.sum(weights, axis=0, keepdims=True) + own_weight)
        probs = weights * inverse
        own_prob = own_weight * inverse
        grad_probs = nt(vx[...], o2)
        own_grad_prob = jnp.sum(jnp.where(eye, grad_probs[slots:], 0.0), axis=0, keepdims=True)
        grad_probs = grad_probs[:slots]
        delta = jnp.sum(probs * grad_probs, axis=0, keepdims=True) + own_prob * own_grad_prob
        low_grads = (probs * (grad_probs - delta)).astype(jnp.bfloat16)
        low_probs = probs.astype(jnp.bfloat16)
        own_grad_score = own_prob * (own_grad_prob - delta)
        own_low_probs = jnp.where(eye, own_prob, 0.0).astype(jnp.bfloat16)
        own_low_grads = jnp.where(eye, own_grad_score, 0.0).astype(jnp.bfloat16)
        dv_part = nn(low_probs, o2)
        dk_part = nn(low_grads, q2)
        dv = dv_part if dv is None else dv + dv_part
        dk = dk_part if dk is None else dk + dk_part
        own_ref[at, 0:HD] = SCALE * nn(own_low_grads, q2)
        own_ref[at, HD : 2 * HD] = nn(own_low_probs, o2)
        dq = nn(kt[...], low_grads) + tn(own_key, own_low_grads)
        dq = (SCALE * dq).T.astype(jnp.bfloat16)
        for h in range(GROUP):
            dq_ref[at, h * HD : (h + 1) * HD] = dq[h * rows : (h + 1) * rows]
    dk = dk * SCALE
    half = slots // 2
    for term, part in ((near_ref, slice(0, half)), (far_ref, slice(half, slots))):
        term[:, 0:HD] = dk[part].astype(term.dtype)
        term[:, HD : 2 * HD] = dv[part].astype(term.dtype)


def add_kernel(near_ref, far_ref, after_ref, own_ref, *part_refs):
    total = near_ref[...] + far_ref[...].astype(jnp.float32)
    own_ref[...] = total[:SLOT_DEV]
    for k, part in enumerate(part_refs):
        part[...] = total[(k + 1) * SLOT_DEV : (k + 2) * SLOT_DEV].astype(part.dtype)


def spread_kernel(parts_per_head, seg_ref, *refs):
    kv_heads, tokens = seg_ref.shape
    gk_ref, gv_ref = refs[-2:]
    for g in range(kv_heads):
        parts = refs[g * parts_per_head : (g + 1) * parts_per_head]
        total = parts[0][...].astype(jnp.float32)
        for part in parts[1:-1]:
            total = total + part[...].astype(jnp.float32)
        picks = slot_picks(seg_ref[g : g + 1, :], tokens).astype(jnp.float32)
        counts = jnp.sum(picks, axis=1, keepdims=True)
        total = total / jnp.maximum(counts, 1.0)
        high = total.astype(jnp.bfloat16)
        low = (total - high.astype(jnp.float32)).astype(jnp.bfloat16)
        picks = picks.astype(jnp.bfloat16)
        spread = tn(picks, high) + tn(picks, low) + parts[-1][...]
        gk_ref[:, g * HD : (g + 1) * HD] = spread[:, 0:HD].astype(jnp.bfloat16)
        gv_ref[:, g * HD : (g + 1) * HD] = spread[:, HD : 2 * HD].astype(jnp.bfloat16)


def in_vmem(count):
    return [pl.BlockSpec(memory_space=pltpu.VMEM)] * count


def in_smem():
    return [pl.BlockSpec(memory_space=pltpu.SMEM)]


def anywhere(count):
    return [pl.BlockSpec(memory_space=pl.ANY)] * count


def in_hbm(count):
    return [pl.BlockSpec(memory_space=pltpu.HBM)] * count


def params(mib):
    return pltpu.CompilerParams(vmem_limit_bytes=mib * 2**20)


def shape(*dims, dtype=jnp.bfloat16):
    return jax.ShapeDtypeStruct(dims, dtype)


def swap(x, axis, size, m):
    return lax.ppermute(x, axis, [(i, i ^ m) for i in range(size)])


def gate(values, after):
    return pl.pallas_call(
        gate_kernel,
        out_shape=[shape(*v.shape, dtype=v.dtype) for v in values],
        in_specs=anywhere(len(values) + len(after)),
        out_specs=anywhere(len(values)),
        input_output_aliases={i: i for i in range(len(values))},
        compiler_params=params(1),
        name="gate",
    )(*values, *after)


def exchange(across, core, heads, after=lambda: ()):
    from_across = swap(across, "head", heads, 2)
    after = after()
    both = pl.pallas_call(
        join_kernel,
        out_shape=shape(*across.shape),
        in_specs=anywhere(2 + len(after)),
        out_specs=in_vmem(1)[0],
        scratch_shapes=[pltpu.SemaphoreType.DMA((2,))],
        compiler_params=params(2),
        name="join",
    )(core, from_across, *after)
    return from_across, swap(both, "head", heads, 1), both


def local(queries, keys, values, segment_ids, grad_out):
    rows = queries.shape[0]
    heads = lax.axis_size("head")
    tokens = rows * heads
    kv_heads = KVH // heads
    shards = lax.axis_size("ctx")
    place = jnp.stack([lax.axis_index("ctx"), lax.axis_index("head")]).astype(jnp.int32)
    order = list(range(0, shards, 2)) + list(range(1, shards, 2))
    half = SLOT_DEV * shards // 2
    slots = SLOT_DEV * shards
    kv_width = kv_heads * HD

    def kv_at(m):
        return (m, kv_width, 0)

    def qo_at(m, g):
        return (m, kv_heads * GW, g * GW)

    def pack(jobs, sources, after, mib, name):
        outs = [pieces for _, dests in jobs for pieces in dests]
        return pl.pallas_call(
            functools.partial(pack_kernel, jobs),
            out_shape=[
                shape(len(pieces) * rows, 2 * width) for width, dests in jobs for pieces in dests
            ],
            in_specs=in_smem() + anywhere(2 + len(after)),
            out_specs=anywhere(len(outs)),
            scratch_shapes=[
                pltpu.SemaphoreType.DMA((2 * sum(len(p) for _, dests in jobs for p in dests),))
            ],
            compiler_params=params(mib),
            name=name,
        )(place, *sources, *after)

    kv_across, kv_core, kv_own = pack(
        [(kv_width, [[kv_at(2), kv_at(3)], [kv_at(1)], [kv_at(0)]])], (keys, values), (), 56, "pack_kv"
    )
    from_across, from_core, both = exchange(kv_across, kv_core, heads)
    kv = (kv_own, from_across, from_core)

    jobs = [(GW, [[qo_at(2, 0), qo_at(3, 0)], [qo_at(1, 0)]])]
    for g in range(1, kv_heads):
        jobs.append((GW, [[qo_at(m, g)] for m in range(1, heads)]))
    packed = pack(jobs, (queries, grad_out), (both,), 4, "pack_qo")

    merged = pl.pallas_call(
        merge_kernel,
        out_shape=shape(SLOT_DEV, 2 * kv_width),
        in_specs=in_smem() + in_vmem(4),
        out_specs=in_vmem(1)[0],
        scratch_shapes=[pltpu.VMEM((tokens, 2 * kv_width), jnp.bfloat16)],
        compiler_params=params(4),
        name="merge",
    )(place, segment_ids, *kv)

    held = {0: merged}
    for m in range(2, shards, 2):
        held[m] = swap(merged, "ctx", shards, m)
    for m in range(0, shards, 2):
        held[m + 1] = swap(held[m], "ctx", shards, 1)

    late = [held[m] for m in range(1, shards - 1)]
    qo = [exchange(*packed[:2], heads, lambda: late)[:2]]
    qo_places = [((1, 0), (0, 0), (1, 1))]
    for g in range(1, kv_heads):
        pieces = packed[2 + (g - 1) * (heads - 1) : 2 + g * (heads - 1)]
        pieces = gate(pieces, late)
        qo.append([swap(piece, "head", heads, m + 1) for m, piece in enumerate(pieces)])
        qo_places.append(((0, 0), (1, 0), (2, 0)))

    seg_col = segment_ids.T
    dq = []
    own = []
    near = []
    far = []
    for g in range(kv_heads):
        outs = pl.pallas_call(
            functools.partial(attend_kernel, g, order, qo_places[g]),
            out_shape=[
                shape(tokens, GW),
                shape(tokens, 2 * HD, dtype=jnp.float32),
                shape(half, 2 * HD, dtype=jnp.float32),
                shape(half, 2 * HD),
            ],
            in_specs=in_smem() + in_vmem(1) + in_hbm(2) + anywhere(3 + shards + len(qo[g]) + (g > 0)),
            out_specs=in_vmem(4),
            scratch_shapes=[
                pltpu.VMEM((slots + rows, 2 * HD), jnp.bfloat16),
                pltpu.VMEM((slots + rows, HD), jnp.bfloat16),
                pltpu.VMEM((HD, slots), jnp.bfloat16),
                pltpu.VMEM((heads, rows, 2 * GW), jnp.bfloat16),
                pltpu.VMEM((heads, 2, rows, HD), jnp.bfloat16),
                pltpu.SemaphoreType.DMA((heads + 1,)),
                pltpu.SemaphoreType.DMA((2 * heads,)),
                pltpu.SemaphoreType.DMA((2 * shards,)),
            ],
            compiler_params=params(24),
            cost_estimate=pl.CostEstimate(
                flops=10 * tokens * GROUP * (slots + rows) * HD,
                bytes_accessed=4 * 2**20,
                transcendentals=tokens * GROUP * slots,
            ),
            name="attend",
        )(place, seg_col, queries, grad_out, *kv, *[held[m] for m in order], *qo[g], *own[-1:])
        dq.append(outs[0])
        own.append(outs[1])
        near.append(outs[2])
        far.append(swap(outs[3], "ctx", shards, 1))

    spread_args = []
    for g in range(kv_heads):
        parts = pl.pallas_call(
            add_kernel,
            out_shape=[shape(SLOT_DEV, 2 * HD, dtype=jnp.float32)]
            + [shape(SLOT_DEV, 2 * HD)] * (shards // 2 - 1),
            in_specs=in_vmem(2) + anywhere(1),
            out_specs=in_vmem(shards // 2),
            compiler_params=params(8),
            name="add",
        )(near[g], far[g], own[-1])
        spread_args.append(parts[0])
        for k in range(1, shards // 2):
            spread_args.append(swap(parts[k], "ctx", shards, 2 * k))
        spread_args.append(own[g])

    grad_keys, grad_values = pl.pallas_call(
        functools.partial(spread_kernel, shards // 2 + 1),
        out_shape=[shape(tokens, kv_width)] * 2,
        in_specs=in_vmem(1 + len(spread_args)),
        out_specs=in_vmem(2),
        compiler_params=params(12),
        name="spread",
    )(segment_ids, *spread_args)
    return jnp.concatenate(dq, axis=1), grad_keys, grad_values


def solution(mesh):
    return jax.shard_map(
        local,
        mesh=mesh,
        in_specs=(
            P(("ctx", "head"), None),
            P(("ctx", "head"), None),
            P(("ctx", "head"), None),
            P("head", "ctx"),
            P(("ctx", "head"), None),
        ),
        out_specs=(P("ctx", "head"), P("ctx", "head"), P("ctx", "head")),
        check_vma=False,
    )
```

```python
import functools

import jax
import jax.numpy as jnp
from jax import lax
from jax.experimental import pallas as pl
from jax.experimental.pallas import tpu as pltpu
from jax.sharding import PartitionSpec as P

QH = 64
KVH = 8
HD = 128
SLOT_DEV = 96
GROUP = QH // KVH
GW = GROUP * HD
SCALE = HD ** (-0.5)
LOG2E = 1.4426950408889634
DEAD = 1024.0
HIDDEN = 2.0**96


def nt(a, b):
    return lax.dot_general(a, b, (((1,), (1,)), ((), ())), preferred_element_type=jnp.float32)


def nn(a, b):
    return lax.dot_general(a, b, (((1,), (0,)), ((), ())), preferred_element_type=jnp.float32)


def tn(a, b):
    return lax.dot_general(a, b, (((0,), (0,)), ((), ())), preferred_element_type=jnp.float32)


def slot_picks(seg_row, tokens):
    return lax.broadcasted_iota(jnp.int32, (SLOT_DEV, tokens), 0) == seg_row


def place():
    return lax.axis_index("ctx"), lax.axis_index("head")


def lanes(start, size):
    return pl.ds(pl.multiple_of(start, HD), size)


def run_copies(copies):
    for copy in copies:
        copy.start()
    return copies


def wait_copies(copies):
    for copy in copies:
        copy.wait()


def pack_kernel(jobs, *refs):
    outs = [out for _, dests in jobs for out in dests]
    sources, out_refs, sems = refs[:2], refs[-len(outs) - 1 : -1], refs[-1]
    me = place()[1]
    copies = []
    done = 0
    for width, dests in jobs:
        for out, pieces in zip(out_refs[done:], dests):
            for at, (m, scale, offset) in enumerate(pieces):
                start = lax.bitwise_xor(me, m) * scale + offset
                for part, source in enumerate(sources):
                    rows = source.shape[0]
                    copies.append(
                        pltpu.make_async_copy(
                            source.at[:, lanes(start, width)],
                            out.at[at * rows : (at + 1) * rows, part * width : (part + 1) * width],
                            sems.at[len(copies)],
                        )
                    )
        done += len(dests)
    wait_copies(run_copies(copies))


def gate_kernel(*refs):
    pass


def join_kernel(core_ref, across_ref, *refs):
    out, sems = refs[-2:]
    rows = core_ref.shape[0]
    wait_copies(
        run_copies(
            [
                pltpu.make_async_copy(core_ref, out.at[0:rows, :], sems.at[0]),
                pltpu.make_async_copy(
                    across_ref.at[rows : 2 * rows, :], out.at[rows : 2 * rows, :], sems.at[1]
                ),
            ]
        )
    )


def pack_kv_kernel(kv_heads, key_ref, value_ref, *outs):
    me = place()[1]
    width = kv_heads * HD
    for m, out in enumerate(outs):
        start = lax.bitwise_xor(me, m) * width
        out[:, 0:width] = key_ref[:, lanes(start, width)]
        out[:, width : 2 * width] = value_ref[:, lanes(start, width)]


def merge_kernel(heads, seg_ref, *refs):
    pieces, (out, hide_ref, whole) = refs[:heads], refs[-3:]
    kv_heads, tokens = seg_ref.shape
    rows = tokens // heads
    me = place()[1]
    for m, piece in enumerate(pieces):
        start = pl.multiple_of(lax.bitwise_xor(me, m) * rows, 16)
        whole[pl.ds(start, rows), :] = piece[...]
    for g in range(kv_heads):
        picks = slot_picks(seg_ref[g : g + 1, :], tokens).astype(jnp.float32)
        counts = jnp.sum(picks, axis=1, keepdims=True)
        low_picks = picks.astype(jnp.bfloat16)
        sizes = jnp.maximum(counts, 1.0)
        for part in range(2):
            at = slice((part * kv_heads + g) * HD, (part * kv_heads + g + 1) * HD)
            rows_out = nn(low_picks, whole[:, at]) / sizes
            if part == 0:
                rows_out = jnp.where(counts == 0.0, DEAD, rows_out)
            out[:, at] = rows_out.astype(jnp.bfloat16)
        padded = -(-tokens // HD) * HD
        place_in = lax.broadcasted_iota(jnp.int32, (HD, padded), 0)
        seg = jnp.concatenate([seg_ref[g : g + 1, :]] * 2, axis=1)[:, :padded]
        late = (place_in >= seg) & (place_in < SLOT_DEV)
        hide = jnp.where(late, -HIDDEN, jnp.where(place_in == SLOT_DEV, 1.0, 0.0))
        hide_ref[g] = hide.T[:tokens].astype(jnp.bfloat16)


def attend_kernel(g, order, qo_at, q_ref, o_ref, hide_ref, *refs):
    shards = len(order)
    heads = 4
    kv_pieces, blocks, refs = refs[:heads], refs[heads : heads + shards], refs[heads + shards :]
    qo_pieces = [(refs[i], half) for i, half in qo_at]
    dq_ref, own_ref, near_ref, far_ref, kx, vx, kt, mine, sems = refs[-9:]
    rows = q_ref.shape[0]
    kv_heads = hide_ref.shape[0]
    slots = shards * SLOT_DEV
    shard, me = place()
    key_at = slice(g * HD, (g + 1) * HD)
    value_at = slice((kv_heads + g) * HD, (kv_heads + g + 1) * HD)
    start = (me * kv_heads + g) * GW
    copies = run_copies(
        [
            pltpu.make_async_copy(
                source.at[:, lanes(start, GW)], mine.at[:, part * GW : (part + 1) * GW], sems.at[part]
            )
            for part, source in enumerate((q_ref, o_ref))
        ]
    )

    lane = lax.broadcasted_iota(jnp.int32, (SLOT_DEV, HD), 1)
    row = lax.broadcasted_iota(jnp.int32, (SLOT_DEV, HD), 0)
    for r, (m, block) in enumerate(zip(order, blocks)):
        at = pl.ds(r * SLOT_DEV, SLOT_DEV)
        key = block[:, key_at].astype(jnp.float32)
        vx[at, :] = block[:, value_at]
        if m == 0:
            extra = jnp.where(lane == row, 1.0, 0.0)
        else:
            hide = (key[:, 0:1] > 100.0) | (lax.bitwise_xor(shard, m) > shard)
            extra = jnp.where(hide & (lane >= SLOT_DEV), -HIDDEN, 0.0)
        kx[at, 0:HD] = jnp.where(key > 100.0, 0.0, key).astype(jnp.bfloat16)
        kx[at, HD : 2 * HD] = extra.astype(jnp.bfloat16)
    kx[slots : slots + rows, HD : 2 * HD] = jnp.zeros((rows, HD), jnp.bfloat16)
    kt[...] = kx[0:slots, 0:HD].astype(jnp.float32).T.astype(jnp.bfloat16)

    width = GROUP * rows
    eye_row = lax.broadcasted_iota(jnp.int32, (rows, width), 0)
    eye_lane = lax.broadcasted_iota(jnp.int32, (rows, width), 1)
    eye = eye_row == lax.rem(eye_lane, rows)
    factor = SCALE * LOG2E
    wait_copies(copies)

    dk = None
    dv = None
    for m, (qo, half) in enumerate([(mine, 0)] + qo_pieces):
        span = slice(half * rows, (half + 1) * rows)
        at = pl.ds(pl.multiple_of(lax.bitwise_xor(me, m) * rows, 16), rows)
        own_key = kv_pieces[m][:, key_at]
        kx[slots : slots + rows, 0:HD] = own_key
        vx[slots : slots + rows, :] = kv_pieces[m][:, value_at]
        q2 = jnp.concatenate([qo[span, h * HD : (h + 1) * HD] for h in range(GROUP)], axis=0)
        o2 = jnp.concatenate(
            [qo[span, GW + h * HD : GW + (h + 1) * HD] for h in range(GROUP)], axis=0
        )
        qx = jnp.concatenate([q2, jnp.concatenate([hide_ref[g, at, :]] * GROUP, axis=0)], axis=1)
        scores = nt(kx[...], qx)
        own_score = jnp.sum(jnp.where(eye, scores[slots:], 0.0), axis=0, keepdims=True)
        scores = scores[:slots]
        top = jnp.maximum(jnp.max(scores, axis=0, keepdims=True), own_score)
        weights = jnp.exp2((scores - top) * factor)
        own_weight = jnp.exp2((own_score - top) * factor)
        inverse = 1.0 / (jnp.sum(weights, axis=0, keepdims=True) + own_weight)
        probs = weights * inverse
        own_prob = own_weight * inverse
        grad_probs = nt(vx[...], o2)
        own_grad_prob = jnp.sum(jnp.where(eye, grad_probs[slots:], 0.0), axis=0, keepdims=True)
        grad_probs = grad_probs[:slots]
        delta = jnp.sum(probs * grad_probs, axis=0, keepdims=True) + own_prob * own_grad_prob
        low_grads = (probs * (grad_probs - delta)).astype(jnp.bfloat16)
        low_probs = probs.astype(jnp.bfloat16)
        own_grad_score = own_prob * (own_grad_prob - delta)
        own_low_probs = jnp.where(eye, own_prob, 0.0).astype(jnp.bfloat16)
        own_low_grads = jnp.where(eye, own_grad_score, 0.0).astype(jnp.bfloat16)
        dv_part = nn(low_probs, o2)
        dk_part = nn(low_grads, q2)
        dv = dv_part if dv is None else dv + dv_part
        dk = dk_part if dk is None else dk + dk_part
        own_ref[at, 0:HD] = SCALE * nn(own_low_grads, q2)
        own_ref[at, HD : 2 * HD] = nn(own_low_probs, o2)
        dq = nn(kt[...], low_grads) + tn(own_key, own_low_grads)
        dq = (SCALE * dq).T.astype(jnp.bfloat16)
        for h in range(GROUP):
            dq_ref[at, h * HD : (h + 1) * HD] = dq[h * rows : (h + 1) * rows]
    dk = dk * SCALE
    half = slots // 2
    for term, part in ((near_ref, slice(0, half)), (far_ref, slice(half, slots))):
        term[:, 0:HD] = dk[part].astype(term.dtype)
        term[:, HD : 2 * HD] = dv[part].astype(term.dtype)


def add_kernel(near_ref, far_ref, after_ref, own_ref, *part_refs):
    total = near_ref[...] + far_ref[...].astype(jnp.float32)
    own_ref[...] = total[:SLOT_DEV]
    for k, part in enumerate(part_refs):
        part[...] = total[(k + 1) * SLOT_DEV : (k + 2) * SLOT_DEV].astype(part.dtype)


def spread_kernel(parts_per_head, seg_ref, *refs):
    kv_heads, tokens = seg_ref.shape
    gk_ref, gv_ref = refs[-2:]
    for g in range(kv_heads):
        parts = refs[g * parts_per_head : (g + 1) * parts_per_head]
        total = parts[0][...].astype(jnp.float32)
        for part in parts[1:-1]:
            total = total + part[...].astype(jnp.float32)
        picks = slot_picks(seg_ref[g : g + 1, :], tokens).astype(jnp.float32)
        counts = jnp.sum(picks, axis=1, keepdims=True)
        total = total / jnp.maximum(counts, 1.0)
        high = total.astype(jnp.bfloat16)
        low = (total - high.astype(jnp.float32)).astype(jnp.bfloat16)
        picks = picks.astype(jnp.bfloat16)
        spread = tn(picks, high) + tn(picks, low) + parts[-1][...]
        gk_ref[:, g * HD : (g + 1) * HD] = spread[:, 0:HD].astype(jnp.bfloat16)
        gv_ref[:, g * HD : (g + 1) * HD] = spread[:, HD : 2 * HD].astype(jnp.bfloat16)


def in_vmem(count):
    return [pl.BlockSpec(memory_space=pltpu.VMEM)] * count


def anywhere(count):
    return [pl.BlockSpec(memory_space=pl.ANY)] * count


def params(mib):
    return pltpu.CompilerParams(vmem_limit_bytes=mib * 2**20)


def shape(*dims, dtype=jnp.bfloat16):
    return jax.ShapeDtypeStruct(dims, dtype)


def swap(x, axis, size, m):
    return lax.ppermute(x, axis, [(i, i ^ m) for i in range(size)])


def gate(values, after):
    return pl.pallas_call(
        gate_kernel,
        out_shape=[shape(*v.shape, dtype=v.dtype) for v in values],
        in_specs=anywhere(len(values) + len(after)),
        out_specs=anywhere(len(values)),
        input_output_aliases={i: i for i in range(len(values))},
        compiler_params=params(1),
        name="gate",
    )(*values, *after)


def exchange(across, core, heads, after=lambda: ()):
    from_across = swap(across, "head", heads, 2)
    after = after()
    both = pl.pallas_call(
        join_kernel,
        out_shape=shape(*across.shape),
        in_specs=anywhere(2 + len(after)),
        out_specs=in_vmem(1)[0],
        scratch_shapes=[pltpu.SemaphoreType.DMA((2,))],
        compiler_params=params(2),
        name="join",
    )(core, from_across, *after)
    return from_across, swap(both, "head", heads, 1)


def local(queries, keys, values, segment_ids, grad_out):
    rows = queries.shape[0]
    heads = lax.axis_size("head")
    tokens = rows * heads
    kv_heads = KVH // heads
    shards = lax.axis_size("ctx")
    order = list(range(0, shards, 2)) + list(range(1, shards, 2))
    half = SLOT_DEV * shards // 2
    slots = SLOT_DEV * shards
    kv_width = kv_heads * HD

    def kv_at(m):
        return (m, kv_width, 0)

    def qo_at(m, g):
        return (m, kv_heads * GW, g * GW)

    def pack(jobs, sources, after, mib, name):
        outs = [pieces for _, dests in jobs for pieces in dests]
        return pl.pallas_call(
            functools.partial(pack_kernel, jobs),
            out_shape=[
                shape(len(pieces) * rows, 2 * width) for width, dests in jobs for pieces in dests
            ],
            in_specs=anywhere(2 + len(after)),
            out_specs=anywhere(len(outs)),
            scratch_shapes=[
                pltpu.SemaphoreType.DMA((2 * sum(len(p) for _, dests in jobs for p in dests),))
            ],
            compiler_params=params(mib),
            name=name,
        )(*sources, *after)

    kv_out = pl.pallas_call(
        functools.partial(pack_kv_kernel, kv_heads),
        out_shape=[shape(rows, 2 * kv_width)] * heads,
        in_specs=in_vmem(2),
        out_specs=in_vmem(heads),
        compiler_params=params(2),
        name="pack_kv",
    )(keys, values)
    kv = [kv_out[0]] + [swap(kv_out[m], "head", heads, m) for m in range(1, heads)]

    jobs = [(GW, [[qo_at(2, 0), qo_at(3, 0)], [qo_at(1, 0)]])]
    for g in range(1, kv_heads):
        jobs.append((GW, [[qo_at(m, g)] for m in range(1, heads)]))
    packed = pack(jobs, (queries, grad_out), kv_out[:1], 4, "pack_qo")

    merged, hide = pl.pallas_call(
        functools.partial(merge_kernel, heads),
        out_shape=[shape(SLOT_DEV, 2 * kv_width), shape(kv_heads, tokens, HD)],
        in_specs=in_vmem(1 + heads) + anywhere(1),
        out_specs=in_vmem(2),
        scratch_shapes=[pltpu.VMEM((tokens, 2 * kv_width), jnp.bfloat16)],
        compiler_params=params(4),
        name="merge",
    )(segment_ids, *kv, packed[1])

    held = {0: merged}
    for m in range(2, shards, 2):
        held[m] = swap(merged, "ctx", shards, m)
    for m in range(0, shards, 2):
        held[m + 1] = swap(held[m], "ctx", shards, 1)

    late = [held[m] for m in range(1, shards - 1)]
    soon = [held[m] for m in range(1, shards) if m % 2 == 0 or m in (1, shards // 2 + 1)]
    qo_across = gate(packed[:1], kv[1:])[0]
    qo = [exchange(qo_across, packed[1], heads, lambda: soon)]
    qo_places = [((1, 0), (0, 0), (1, 1))]
    for g in range(1, kv_heads):
        pieces = packed[2 + (g - 1) * (heads - 1) : 2 + g * (heads - 1)]
        pieces = gate(pieces, late)
        qo.append([swap(piece, "head", heads, m + 1) for m, piece in enumerate(pieces)])
        qo_places.append(((0, 0), (1, 0), (2, 0)))

    dq = []
    own = []
    near = []
    far = []
    for g in range(kv_heads):
        outs = pl.pallas_call(
            functools.partial(attend_kernel, g, order, qo_places[g]),
            out_shape=[
                shape(tokens, GW),
                shape(tokens, 2 * HD, dtype=jnp.float32),
                shape(half, 2 * HD, dtype=jnp.float32),
                shape(half, 2 * HD),
            ],
            in_specs=anywhere(2) + in_vmem(1 + heads + shards + len(qo[g])) + anywhere(g > 0),
            out_specs=in_vmem(4),
            scratch_shapes=[
                pltpu.VMEM((slots + rows, 2 * HD), jnp.bfloat16),
                pltpu.VMEM((slots + rows, HD), jnp.bfloat16),
                pltpu.VMEM((HD, slots), jnp.bfloat16),
                pltpu.VMEM((rows, 2 * GW), jnp.bfloat16),
                pltpu.SemaphoreType.DMA((2,)),
            ],
            compiler_params=params(24),
            cost_estimate=pl.CostEstimate(
                flops=10 * tokens * GROUP * (slots + rows) * HD,
                bytes_accessed=4 * 2**20,
                transcendentals=tokens * GROUP * slots,
            ),
            name="attend",
        )(queries, grad_out, hide, *kv, *[held[m] for m in order], *qo[g], *own[-1:])
        dq.append(outs[0])
        own.append(outs[1])
        near.append(outs[2])
        far.append(swap(outs[3], "ctx", shards, 1))

    spread_args = []
    for g in range(kv_heads):
        parts = pl.pallas_call(
            add_kernel,
            out_shape=[shape(SLOT_DEV, 2 * HD, dtype=jnp.float32)]
            + [shape(SLOT_DEV, 2 * HD)] * (shards // 2 - 1),
            in_specs=in_vmem(2) + anywhere(1),
            out_specs=in_vmem(shards // 2),
            compiler_params=params(8),
            name="add",
        )(near[g], far[g], own[-1])
        spread_args.append(parts[0])
        for k in range(1, shards // 2):
            spread_args.append(swap(parts[k], "ctx", shards, 2 * k))
        spread_args.append(own[g])

    grad_keys, grad_values = pl.pallas_call(
        functools.partial(spread_kernel, shards // 2 + 1),
        out_shape=[shape(tokens, kv_width)] * 2,
        in_specs=in_vmem(1 + len(spread_args)),
        out_specs=in_vmem(2),
        compiler_params=params(12),
        name="spread",
    )(segment_ids, *spread_args)
    return jnp.concatenate(dq, axis=1), grad_keys, grad_values


def solution(mesh):
    return jax.shard_map(
        local,
        mesh=mesh,
        in_specs=(
            P(("ctx", "head"), None),
            P(("ctx", "head"), None),
            P(("ctx", "head"), None),
            P("head", "ctx"),
            P(("ctx", "head"), None),
        ),
        out_specs=(P("ctx", "head"), P("ctx", "head"), P("ctx", "head")),
        check_vma=False,
    )
```

```python
import functools

import jax
import jax.numpy as jnp
from jax import lax
from jax.experimental import pallas as pl
from jax.experimental.pallas import tpu as pltpu
from jax.sharding import PartitionSpec as P

QH = 64
KVH = 8
HD = 128
SLOT_DEV = 96
GROUP = QH // KVH
GW = GROUP * HD
SCALE = HD ** (-0.5)
LOG2E = 1.4426950408889634
DEAD = 1024.0
HIDDEN = 2.0**96


def nt(a, b):
    return lax.dot_general(a, b, (((1,), (1,)), ((), ())), preferred_element_type=jnp.float32)


def nn(a, b):
    return lax.dot_general(a, b, (((1,), (0,)), ((), ())), preferred_element_type=jnp.float32)


def tn(a, b):
    return lax.dot_general(a, b, (((0,), (0,)), ((), ())), preferred_element_type=jnp.float32)


def slot_picks(seg_row, tokens):
    return lax.broadcasted_iota(jnp.int32, (SLOT_DEV, tokens), 0) == seg_row


def place():
    return lax.axis_index("ctx"), lax.axis_index("head")


def lanes(start, size):
    return pl.ds(pl.multiple_of(start, HD), size)


def run_copies(copies):
    for copy in copies:
        copy.start()
    return copies


def wait_copies(copies):
    for copy in copies:
        copy.wait()


def pack_kernel(jobs, *refs):
    outs = [out for _, dests in jobs for out in dests]
    sources, out_refs, sems = refs[:2], refs[-len(outs) - 1 : -1], refs[-1]
    me = place()[1]
    copies = []
    done = 0
    for width, dests in jobs:
        for out, pieces in zip(out_refs[done:], dests):
            for at, (m, scale, offset) in enumerate(pieces):
                start = lax.bitwise_xor(me, m) * scale + offset
                for part, source in enumerate(sources):
                    rows = source.shape[0]
                    copies.append(
                        pltpu.make_async_copy(
                            source.at[:, lanes(start, width)],
                            out.at[at * rows : (at + 1) * rows, part * width : (part + 1) * width],
                            sems.at[len(copies)],
                        )
                    )
        done += len(dests)
    wait_copies(run_copies(copies))


def gate_kernel(*refs):
    pass


def join_kernel(own_ref, core_ref, *refs):
    out, sems = refs[-2:]
    rows = own_ref.shape[0]
    wait_copies(
        run_copies(
            [
                pltpu.make_async_copy(own_ref, out.at[0:rows, :], sems.at[0]),
                pltpu.make_async_copy(
                    core_ref.at[rows : 2 * rows, :], out.at[rows : 2 * rows, :], sems.at[1]
                ),
            ]
        )
    )


def pack_kv_kernel(kv_heads, key_ref, value_ref, *outs):
    me = place()[1]
    width = kv_heads * HD
    for m, out in enumerate(outs):
        start = lax.bitwise_xor(me, m) * width
        out[:, 0:width] = key_ref[:, lanes(start, width)]
        out[:, width : 2 * width] = value_ref[:, lanes(start, width)]


def merge_kernel(heads, seg_ref, *refs):
    pieces, (out, hide_ref, whole) = refs[:heads], refs[-3:]
    kv_heads, tokens = seg_ref.shape
    rows = tokens // heads
    me = place()[1]
    for m, piece in enumerate(pieces):
        start = pl.multiple_of(lax.bitwise_xor(me, m) * rows, 16)
        whole[pl.ds(start, rows), :] = piece[...]
    for g in range(kv_heads):
        picks = slot_picks(seg_ref[g : g + 1, :], tokens).astype(jnp.float32)
        counts = jnp.sum(picks, axis=1, keepdims=True)
        low_picks = picks.astype(jnp.bfloat16)
        sizes = jnp.maximum(counts, 1.0)
        for part in range(2):
            at = slice((part * kv_heads + g) * HD, (part * kv_heads + g + 1) * HD)
            rows_out = nn(low_picks, whole[:, at]) / sizes
            if part == 0:
                rows_out = jnp.where(counts == 0.0, DEAD, rows_out)
            out[:, at] = rows_out.astype(jnp.bfloat16)
        padded = -(-tokens // HD) * HD
        place_in = lax.broadcasted_iota(jnp.int32, (HD, padded), 0)
        seg = jnp.concatenate([seg_ref[g : g + 1, :]] * 2, axis=1)[:, :padded]
        late = (place_in >= seg) & (place_in < SLOT_DEV)
        hide = jnp.where(late, -HIDDEN, jnp.where(place_in == SLOT_DEV, 1.0, 0.0))
        hide_ref[g] = hide.T[:tokens].astype(jnp.bfloat16)


def attend_kernel(g, order, q_ref, o_ref, hide_ref, *refs):
    shards = len(order)
    heads = 4
    kv_pieces, blocks, refs = refs[:heads], refs[heads : heads + shards], refs[heads + shards :]
    qo_pieces = [(refs[0], 0), (refs[1], 0), (refs[1], 1)]
    dq_ref, own_ref, near_ref, far_ref, kx, vx, kt, mine, sems = refs[-9:]
    rows = q_ref.shape[0]
    kv_heads = hide_ref.shape[0]
    slots = shards * SLOT_DEV
    shard, me = place()
    key_at = slice(g * HD, (g + 1) * HD)
    value_at = slice((kv_heads + g) * HD, (kv_heads + g + 1) * HD)
    start = (me * kv_heads + g) * GW
    copies = run_copies(
        [
            pltpu.make_async_copy(
                source.at[:, lanes(start, GW)], mine.at[:, part * GW : (part + 1) * GW], sems.at[part]
            )
            for part, source in enumerate((q_ref, o_ref))
        ]
    )

    lane = lax.broadcasted_iota(jnp.int32, (SLOT_DEV, HD), 1)
    row = lax.broadcasted_iota(jnp.int32, (SLOT_DEV, HD), 0)
    for r, (m, block) in enumerate(zip(order, blocks)):
        at = pl.ds(r * SLOT_DEV, SLOT_DEV)
        key = block[:, key_at].astype(jnp.float32)
        vx[at, :] = block[:, value_at]
        if m == 0:
            extra = jnp.where(lane == row, 1.0, 0.0)
        else:
            hide = (key[:, 0:1] > 100.0) | (lax.bitwise_xor(shard, m) > shard)
            extra = jnp.where(hide & (lane >= SLOT_DEV), -HIDDEN, 0.0)
        kx[at, 0:HD] = jnp.where(key > 100.0, 0.0, key).astype(jnp.bfloat16)
        kx[at, HD : 2 * HD] = extra.astype(jnp.bfloat16)
    kx[slots : slots + rows, HD : 2 * HD] = jnp.zeros((rows, HD), jnp.bfloat16)
    kt[...] = kx[0:slots, 0:HD].astype(jnp.float32).T.astype(jnp.bfloat16)

    width = GROUP * rows
    eye_row = lax.broadcasted_iota(jnp.int32, (rows, width), 0)
    eye_lane = lax.broadcasted_iota(jnp.int32, (rows, width), 1)
    eye = eye_row == lax.rem(eye_lane, rows)
    factor = SCALE * LOG2E
    wait_copies(copies)

    dk = None
    dv = None
    for m, (qo, half) in enumerate([(mine, 0)] + qo_pieces):
        span = slice(half * rows, (half + 1) * rows)
        at = pl.ds(pl.multiple_of(lax.bitwise_xor(me, m) * rows, 16), rows)
        own_key = kv_pieces[m][:, key_at]
        kx[slots : slots + rows, 0:HD] = own_key
        vx[slots : slots + rows, :] = kv_pieces[m][:, value_at]
        q2 = jnp.concatenate([qo[span, h * HD : (h + 1) * HD] for h in range(GROUP)], axis=0)
        o2 = jnp.concatenate(
            [qo[span, GW + h * HD : GW + (h + 1) * HD] for h in range(GROUP)], axis=0
        )
        qx = jnp.concatenate([q2, jnp.concatenate([hide_ref[g, at, :]] * GROUP, axis=0)], axis=1)
        scores = nt(kx[...], qx)
        own_score = jnp.sum(jnp.where(eye, scores[slots:], 0.0), axis=0, keepdims=True)
        scores = scores[:slots]
        top = jnp.maximum(jnp.max(scores, axis=0, keepdims=True), own_score)
        weights = jnp.exp2((scores - top) * factor)
        own_weight = jnp.exp2((own_score - top) * factor)
        inverse = 1.0 / (jnp.sum(weights, axis=0, keepdims=True) + own_weight)
        probs = weights * inverse
        own_prob = own_weight * inverse
        grad_probs = nt(vx[...], o2)
        own_grad_prob = jnp.sum(jnp.where(eye, grad_probs[slots:], 0.0), axis=0, keepdims=True)
        grad_probs = grad_probs[:slots]
        delta = jnp.sum(probs * grad_probs, axis=0, keepdims=True) + own_prob * own_grad_prob
        low_grads = (probs * (grad_probs - delta)).astype(jnp.bfloat16)
        low_probs = probs.astype(jnp.bfloat16)
        own_grad_score = own_prob * (own_grad_prob - delta)
        own_low_probs = jnp.where(eye, own_prob, 0.0).astype(jnp.bfloat16)
        own_low_grads = jnp.where(eye, own_grad_score, 0.0).astype(jnp.bfloat16)
        dv_part = nn(low_probs, o2)
        dk_part = nn(low_grads, q2)
        dv = dv_part if dv is None else dv + dv_part
        dk = dk_part if dk is None else dk + dk_part
        own_ref[at, 0:HD] = SCALE * nn(own_low_grads, q2)
        own_ref[at, HD : 2 * HD] = nn(own_low_probs, o2)
        dq = nn(kt[...], low_grads) + tn(own_key, own_low_grads)
        dq = (SCALE * dq).T.astype(jnp.bfloat16)
        for h in range(GROUP):
            dq_ref[at, h * HD : (h + 1) * HD] = dq[h * rows : (h + 1) * rows]
    dk = dk * SCALE
    half = slots // 2
    for term, part in ((near_ref, slice(0, half)), (far_ref, slice(half, slots))):
        term[:, 0:HD] = dk[part].astype(term.dtype)
        term[:, HD : 2 * HD] = dv[part].astype(term.dtype)


def add_kernel(near_ref, far_ref, after_ref, keep_ref, send_ref):
    total = near_ref[...] + far_ref[...].astype(jnp.float32)
    half = keep_ref.shape[0]
    keep_ref[...] = total[:half]
    send_ref[...] = total[half:].astype(send_ref.dtype)


def spread_kernel(parts_per_head, seg_ref, *refs):
    kv_heads, tokens = seg_ref.shape
    gk_ref, gv_ref = refs[-2:]
    for g in range(kv_heads):
        parts = refs[g * parts_per_head : (g + 1) * parts_per_head]
        total = parts[0][...].astype(jnp.float32)
        for part in parts[1:-1]:
            total = total + part[...].astype(jnp.float32)
        picks = slot_picks(seg_ref[g : g + 1, :], tokens).astype(jnp.float32)
        counts = jnp.sum(picks, axis=1, keepdims=True)
        total = total / jnp.maximum(counts, 1.0)
        high = total.astype(jnp.bfloat16)
        low = (total - high.astype(jnp.float32)).astype(jnp.bfloat16)
        picks = picks.astype(jnp.bfloat16)
        spread = tn(picks, high) + tn(picks, low) + parts[-1][...]
        gk_ref[:, g * HD : (g + 1) * HD] = spread[:, 0:HD].astype(jnp.bfloat16)
        gv_ref[:, g * HD : (g + 1) * HD] = spread[:, HD : 2 * HD].astype(jnp.bfloat16)


def in_vmem(count):
    return [pl.BlockSpec(memory_space=pltpu.VMEM)] * count


def anywhere(count):
    return [pl.BlockSpec(memory_space=pl.ANY)] * count


def params(mib):
    return pltpu.CompilerParams(vmem_limit_bytes=mib * 2**20)


def shape(*dims, dtype=jnp.bfloat16):
    return jax.ShapeDtypeStruct(dims, dtype)


def swap(x, axis, size, m):
    return lax.ppermute(x, axis, [(i, i ^ m) for i in range(size)])


def gate(value, after):
    return pl.pallas_call(
        gate_kernel,
        out_shape=shape(*value.shape, dtype=value.dtype),
        in_specs=anywhere(1 + len(after)),
        out_specs=anywhere(1)[0],
        input_output_aliases={0: 0},
        compiler_params=params(1),
        name="gate",
    )(value, *after)


def across(own, from_core, heads, after):
    both = pl.pallas_call(
        join_kernel,
        out_shape=shape(*from_core.shape),
        in_specs=anywhere(2 + len(after)),
        out_specs=in_vmem(1)[0],
        scratch_shapes=[pltpu.SemaphoreType.DMA((2,))],
        compiler_params=params(2),
        name="join",
    )(own, from_core, *after)
    return swap(both, "head", heads, 2)


def bit_reversed(count):
    if count == 1:
        return [0]
    half = [2 * i for i in bit_reversed(count // 2)]
    return half + [i + 1 for i in half]


def local(queries, keys, values, segment_ids, grad_out):
    rows = queries.shape[0]
    heads = lax.axis_size("head")
    tokens = rows * heads
    kv_heads = KVH // heads
    shards = lax.axis_size("ctx")
    order = bit_reversed(shards)
    half = SLOT_DEV * shards // 2
    slots = SLOT_DEV * shards
    kv_width = kv_heads * HD

    def kv_at(m):
        return (m, kv_width, 0)

    def qo_at(m, g):
        return (m, kv_heads * GW, g * GW)

    def pack(jobs, sources, after, mib, name):
        outs = [pieces for _, dests in jobs for pieces in dests]
        return pl.pallas_call(
            functools.partial(pack_kernel, jobs),
            out_shape=[
                shape(len(pieces) * rows, 2 * width) for width, dests in jobs for pieces in dests
            ],
            in_specs=anywhere(2 + len(after)),
            out_specs=anywhere(len(outs)),
            scratch_shapes=[
                pltpu.SemaphoreType.DMA((2 * sum(len(p) for _, dests in jobs for p in dests),))
            ],
            compiler_params=params(mib),
            name=name,
        )(*sources, *after)

    kv_out = pl.pallas_call(
        functools.partial(pack_kv_kernel, kv_heads),
        out_shape=[shape(rows, 2 * kv_width)] * heads,
        in_specs=in_vmem(2),
        out_specs=in_vmem(heads),
        compiler_params=params(2),
        name="pack_kv",
    )(keys, values)
    kv = [kv_out[0]] + [swap(kv_out[m], "head", heads, m) for m in range(1, heads)]

    jobs = [(GW, [[qo_at(1, g), qo_at(3, g)], [qo_at(2, g)]]) for g in range(kv_heads)]
    packed = pack(jobs, (queries, grad_out), kv_out[:1], 4, "pack_qo")
    from_core = [swap(gate(packed[2 * g], kv[1:]), "head", heads, 1) for g in range(kv_heads)]

    merged, hide = pl.pallas_call(
        functools.partial(merge_kernel, heads),
        out_shape=[shape(SLOT_DEV, 2 * kv_width), shape(kv_heads, tokens, HD)],
        in_specs=in_vmem(1 + heads) + anywhere(1),
        out_specs=in_vmem(2),
        scratch_shapes=[pltpu.VMEM((tokens, 2 * kv_width), jnp.bfloat16)],
        compiler_params=params(4),
        name="merge",
    )(segment_ids, *kv, packed[1])

    held = {0: merged}
    for m in range(1, shards):
        low = m & -m
        held[m] = swap(held[m - low], "ctx", shards, low)

    qo = [(from_core[0], across(packed[1], from_core[0], heads, [merged] + from_core[1:]))]
    late = [held[m] for m in range(1, shards - 1)] + [qo[0][1]]
    for g in range(1, kv_heads):
        qo.append((from_core[g], across(packed[2 * g + 1], from_core[g], heads, late)))

    dq = []
    own = []
    near = []
    far = []
    for g in range(kv_heads):
        outs = pl.pallas_call(
            functools.partial(attend_kernel, g, order),
            out_shape=[
                shape(tokens, GW),
                shape(tokens, 2 * HD, dtype=jnp.float32),
                shape(half, 2 * HD, dtype=jnp.float32),
                shape(half, 2 * HD),
            ],
            in_specs=anywhere(2) + in_vmem(1 + heads + shards + len(qo[g])) + anywhere(g > 0),
            out_specs=in_vmem(4),
            scratch_shapes=[
                pltpu.VMEM((slots + rows, 2 * HD), jnp.bfloat16),
                pltpu.VMEM((slots + rows, HD), jnp.bfloat16),
                pltpu.VMEM((HD, slots), jnp.bfloat16),
                pltpu.VMEM((rows, 2 * GW), jnp.bfloat16),
                pltpu.SemaphoreType.DMA((2,)),
            ],
            compiler_params=params(24),
            cost_estimate=pl.CostEstimate(
                flops=10 * tokens * GROUP * (slots + rows) * HD,
                bytes_accessed=4 * 2**20,
                transcendentals=tokens * GROUP * slots,
            ),
            name="attend",
        )(queries, grad_out, hide, *kv, *[held[m] for m in order], *qo[g], *own[-1:])
        dq.append(outs[0])
        own.append(outs[1])
        near.append(outs[2])
        far.append(swap(outs[3], "ctx", shards, 1))

    spread_args = []
    for g in range(kv_heads):
        keep, received, step = near[g], far[g], 2
        while step < shards:
            count = keep.shape[0] // 2
            keep, send = pl.pallas_call(
                add_kernel,
                out_shape=[shape(count, 2 * HD, dtype=jnp.float32), shape(count, 2 * HD)],
                in_specs=in_vmem(2) + anywhere(1),
                out_specs=in_vmem(2),
                compiler_params=params(8),
                name="add",
            )(keep, received, own[-1])
            received = swap(send, "ctx", shards, step)
            step *= 2
        spread_args += [keep, received, own[g]]

    grad_keys, grad_values = pl.pallas_call(
        functools.partial(spread_kernel, 3),
        out_shape=[shape(tokens, kv_width)] * 2,
        in_specs=in_vmem(1 + len(spread_args)),
        out_specs=in_vmem(2),
        compiler_params=params(12),
        name="spread",
    )(segment_ids, *spread_args)
    return jnp.concatenate(dq, axis=1), grad_keys, grad_values


def solution(mesh):
    return jax.shard_map(
        local,
        mesh=mesh,
        in_specs=(
            P(("ctx", "head"), None),
            P(("ctx", "head"), None),
            P(("ctx", "head"), None),
            P("head", "ctx"),
            P(("ctx", "head"), None),
        ),
        out_specs=(P("ctx", "head"), P("ctx", "head"), P("ctx", "head")),
        check_vma=False,
    )
```

```python
import functools

import jax
import jax.numpy as jnp
from jax import lax
from jax.experimental import pallas as pl
from jax.experimental.pallas import tpu as pltpu
from jax.sharding import PartitionSpec as P

QH = 64
KVH = 8
HD = 128
SLOT_DEV = 96
GROUP = QH // KVH
GW = GROUP * HD
SCALE = HD ** (-0.5)
LOG2E = 1.4426950408889634
DEAD = 1024.0
HIDDEN = 2.0**96


def nt(a, b):
    return lax.dot_general(a, b, (((1,), (1,)), ((), ())), preferred_element_type=jnp.float32)


def nn(a, b):
    return lax.dot_general(a, b, (((1,), (0,)), ((), ())), preferred_element_type=jnp.float32)


def tn(a, b):
    return lax.dot_general(a, b, (((0,), (0,)), ((), ())), preferred_element_type=jnp.float32)


def slot_picks(seg_row, tokens):
    return lax.broadcasted_iota(jnp.int32, (SLOT_DEV, tokens), 0) == seg_row


def place():
    return lax.axis_index("ctx"), lax.axis_index("head")


def lanes(start, size):
    return pl.ds(pl.multiple_of(start, HD), size)


def run_copies(copies):
    for copy in copies:
        copy.start()
    return copies


def wait_copies(copies):
    for copy in copies:
        copy.wait()


def pack_kernel(jobs, *refs):
    outs = [out for _, dests in jobs for out in dests]
    sources, out_refs, sems = refs[:2], refs[-len(outs) - 1 : -1], refs[-1]
    me = place()[1]
    copies = []
    done = 0
    for width, dests in jobs:
        for out, pieces in zip(out_refs[done:], dests):
            for at, (m, scale, offset) in enumerate(pieces):
                start = lax.bitwise_xor(me, m) * scale + offset
                for part, source in enumerate(sources):
                    rows = source.shape[0]
                    copies.append(
                        pltpu.make_async_copy(
                            source.at[:, lanes(start, width)],
                            out.at[at * rows : (at + 1) * rows, part * width : (part + 1) * width],
                            sems.at[len(copies)],
                        )
                    )
        done += len(dests)
    wait_copies(run_copies(copies))


def gate_kernel(*refs):
    pass


def join_kernel(own_ref, core_ref, *refs):
    out, sems = refs[-2:]
    rows = own_ref.shape[0]
    wait_copies(
        run_copies(
            [
                pltpu.make_async_copy(own_ref, out.at[0:rows, :], sems.at[0]),
                pltpu.make_async_copy(
                    core_ref.at[rows : 2 * rows, :], out.at[rows : 2 * rows, :], sems.at[1]
                ),
            ]
        )
    )


def pack_kv_kernel(kv_heads, key_ref, value_ref, *outs):
    me = place()[1]
    width = kv_heads * HD
    for m, out in enumerate(outs):
        start = lax.bitwise_xor(me, m) * width
        out[:, 0:width] = key_ref[:, lanes(start, width)]
        out[:, width : 2 * width] = value_ref[:, lanes(start, width)]


def merge_kernel(heads, seg_ref, *refs):
    pieces, (out, hide_ref, whole) = refs[:heads], refs[-3:]
    kv_heads, tokens = seg_ref.shape
    rows = tokens // heads
    me = place()[1]
    for m, piece in enumerate(pieces):
        start = pl.multiple_of(lax.bitwise_xor(me, m) * rows, 16)
        whole[pl.ds(start, rows), :] = piece[...]
    for g in range(kv_heads):
        picks = slot_picks(seg_ref[g : g + 1, :], tokens).astype(jnp.float32)
        counts = jnp.sum(picks, axis=1, keepdims=True)
        low_picks = picks.astype(jnp.bfloat16)
        sizes = jnp.maximum(counts, 1.0)
        for part in range(2):
            at = slice((part * kv_heads + g) * HD, (part * kv_heads + g + 1) * HD)
            rows_out = nn(low_picks, whole[:, at]) / sizes
            if part == 0:
                rows_out = jnp.where(counts == 0.0, DEAD, rows_out)
            out[:, at] = rows_out.astype(jnp.bfloat16)
        padded = -(-tokens // HD) * HD
        place_in = lax.broadcasted_iota(jnp.int32, (HD, padded), 0)
        seg = jnp.concatenate([seg_ref[g : g + 1, :]] * 2, axis=1)[:, :padded]
        late = (place_in >= seg) & (place_in < SLOT_DEV)
        hide = jnp.where(late, -HIDDEN, jnp.where(place_in == SLOT_DEV, 1.0, 0.0))
        hide_ref[g] = hide.T[:tokens].astype(jnp.bfloat16)


def attend_kernel(g, order, q_ref, o_ref, hide_ref, *refs):
    shards = len(order)
    heads = 4
    kv_pieces, blocks, refs = refs[:heads], refs[heads : heads + shards], refs[heads + shards :]
    qo_pieces = [(refs[0], 0), (refs[1], 0), (refs[1], 1)]
    (
        p_ref, ds_ref, own_p_ref, own_ds_ref, qs_ref, os_ref, kt_ref, far_ref,
        kx, vx, mine, sems,
    ) = refs[-12:]
    rows = q_ref.shape[0]
    kv_heads = hide_ref.shape[0]
    slots = shards * SLOT_DEV
    shard, me = place()
    key_at = slice(g * HD, (g + 1) * HD)
    value_at = slice((kv_heads + g) * HD, (kv_heads + g + 1) * HD)
    start = (me * kv_heads + g) * GW
    copies = run_copies(
        [
            pltpu.make_async_copy(
                source.at[:, lanes(start, GW)], mine.at[:, part * GW : (part + 1) * GW], sems.at[part]
            )
            for part, source in enumerate((q_ref, o_ref))
        ]
    )

    lane = lax.broadcasted_iota(jnp.int32, (SLOT_DEV, HD), 1)
    row = lax.broadcasted_iota(jnp.int32, (SLOT_DEV, HD), 0)
    for r, (m, block) in enumerate(zip(order, blocks)):
        at = pl.ds(r * SLOT_DEV, SLOT_DEV)
        key = block[:, key_at].astype(jnp.float32)
        vx[at, :] = block[:, value_at]
        if m == 0:
            extra = jnp.where(lane == row, 1.0, 0.0)
        else:
            hide = (key[:, 0:1] > 100.0) | (lax.bitwise_xor(shard, m) > shard)
            extra = jnp.where(hide & (lane >= SLOT_DEV), -HIDDEN, 0.0)
        kx[at, 0:HD] = jnp.where(key > 100.0, 0.0, key).astype(jnp.bfloat16)
        kx[at, HD : 2 * HD] = extra.astype(jnp.bfloat16)
    kx[slots : slots + rows, HD : 2 * HD] = jnp.zeros((rows, HD), jnp.bfloat16)

    width = GROUP * rows
    eye_row = lax.broadcasted_iota(jnp.int32, (rows, width), 0)
    eye_lane = lax.broadcasted_iota(jnp.int32, (rows, width), 1)
    eye = eye_row == lax.rem(eye_lane, rows)
    factor = SCALE * LOG2E

    for m in list(range(1, heads)) + [0]:
        if m == 0:
            wait_copies(copies)
        qo, half = qo_pieces[m - 1] if m else (mine, 0)
        span = slice(half * rows, (half + 1) * rows)
        at = pl.ds(pl.multiple_of(lax.bitwise_xor(me, m) * rows, 16), rows)
        chunk = slice(m * width, (m + 1) * width)
        kx[slots : slots + rows, 0:HD] = kv_pieces[m][:, key_at]
        vx[slots : slots + rows, :] = kv_pieces[m][:, value_at]
        q2 = jnp.concatenate([qo[span, h * HD : (h + 1) * HD] for h in range(GROUP)], axis=0)
        o2 = jnp.concatenate(
            [qo[span, GW + h * HD : GW + (h + 1) * HD] for h in range(GROUP)], axis=0
        )
        qs_ref[chunk, :] = q2
        os_ref[chunk, :] = o2
        qx = jnp.concatenate([q2, jnp.concatenate([hide_ref[g, at, :]] * GROUP, axis=0)], axis=1)
        scores = nt(kx[...], qx)
        own_score = jnp.sum(jnp.where(eye, scores[slots:], 0.0), axis=0, keepdims=True)
        scores = scores[:slots]
        top = jnp.maximum(jnp.max(scores, axis=0, keepdims=True), own_score)
        weights = jnp.exp2((scores - top) * factor)
        own_weight = jnp.exp2((own_score - top) * factor)
        inverse = 1.0 / (jnp.sum(weights, axis=0, keepdims=True) + own_weight)
        probs = weights * inverse
        own_prob = own_weight * inverse
        grad_probs = nt(vx[...], o2)
        own_grad_prob = jnp.sum(jnp.where(eye, grad_probs[slots:], 0.0), axis=0, keepdims=True)
        grad_probs = grad_probs[:slots]
        delta = jnp.sum(probs * grad_probs, axis=0, keepdims=True) + own_prob * own_grad_prob
        ds_ref[:, chunk] = (probs * (grad_probs - delta)).astype(jnp.bfloat16)
        p_ref[:, chunk] = probs.astype(jnp.bfloat16)
        own_grad_score = own_prob * (own_grad_prob - delta)
        own_p_ref[:, chunk] = jnp.where(eye, own_prob, 0.0).astype(jnp.bfloat16)
        own_ds_ref[:, chunk] = jnp.where(eye, own_grad_score, 0.0).astype(jnp.bfloat16)
    far = slice(slots // 2, slots)
    far_ref[:, 0:HD] = (SCALE * nn(ds_ref[far, :], qs_ref[...])).astype(far_ref.dtype)
    far_ref[:, HD : 2 * HD] = nn(p_ref[far, :], os_ref[...]).astype(far_ref.dtype)
    kt_ref[...] = kx[0:slots, 0:HD].astype(jnp.float32).T.astype(jnp.bfloat16)


def finish_kernel(
    g, heads, p_ref, ds_ref, own_p_ref, own_ds_ref, qs_ref, os_ref, kt_ref, after_ref, *refs
):
    kv_pieces, (near_ref, own_ref, dq_ref) = refs[:heads], refs[heads:]
    rows = own_p_ref.shape[0]
    near = slice(0, near_ref.shape[0])
    near_ref[:, 0:HD] = SCALE * nn(ds_ref[near, :], qs_ref[...])
    near_ref[:, HD : 2 * HD] = nn(p_ref[near, :], os_ref[...])
    me = place()[1]
    width = GROUP * rows
    for m in range(heads):
        at = pl.ds(pl.multiple_of(lax.bitwise_xor(me, m) * rows, 16), rows)
        chunk = slice(m * width, (m + 1) * width)
        own_ref[at, 0:HD] = SCALE * nn(own_ds_ref[:, chunk], qs_ref[chunk, :])
        own_ref[at, HD : 2 * HD] = nn(own_p_ref[:, chunk], os_ref[chunk, :])
        own_key = kv_pieces[m][:, g * HD : (g + 1) * HD]
        dq = nn(kt_ref[...], ds_ref[:, chunk]) + tn(own_key, own_ds_ref[:, chunk])
        dq = (SCALE * dq).T.astype(jnp.bfloat16)
        for h in range(GROUP):
            dq_ref[at, h * HD : (h + 1) * HD] = dq[h * rows : (h + 1) * rows]


def add_kernel(near_ref, far_ref, keep_ref, send_ref):
    total = near_ref[...] + far_ref[...].astype(jnp.float32)
    half = keep_ref.shape[0]
    keep_ref[...] = total[:half]
    send_ref[...] = total[half:].astype(send_ref.dtype)


def spread_kernel(parts_per_head, seg_ref, *refs):
    kv_heads, tokens = seg_ref.shape
    gk_ref, gv_ref = refs[-2:]
    for g in range(kv_heads):
        parts = refs[g * parts_per_head : (g + 1) * parts_per_head]
        total = parts[0][...].astype(jnp.float32)
        for part in parts[1:-1]:
            total = total + part[...].astype(jnp.float32)
        picks = slot_picks(seg_ref[g : g + 1, :], tokens).astype(jnp.float32)
        counts = jnp.sum(picks, axis=1, keepdims=True)
        total = total / jnp.maximum(counts, 1.0)
        high = total.astype(jnp.bfloat16)
        low = (total - high.astype(jnp.float32)).astype(jnp.bfloat16)
        picks = picks.astype(jnp.bfloat16)
        spread = tn(picks, high) + tn(picks, low) + parts[-1][...]
        gk_ref[:, g * HD : (g + 1) * HD] = spread[:, 0:HD].astype(jnp.bfloat16)
        gv_ref[:, g * HD : (g + 1) * HD] = spread[:, HD : 2 * HD].astype(jnp.bfloat16)


def in_vmem(count):
    return [pl.BlockSpec(memory_space=pltpu.VMEM)] * count


def anywhere(count):
    return [pl.BlockSpec(memory_space=pl.ANY)] * count


def params(mib):
    return pltpu.CompilerParams(vmem_limit_bytes=mib * 2**20)


def shape(*dims, dtype=jnp.bfloat16):
    return jax.ShapeDtypeStruct(dims, dtype)


def swap(x, axis, size, m):
    return lax.ppermute(x, axis, [(i, i ^ m) for i in range(size)])


def gate(value, after):
    return pl.pallas_call(
        gate_kernel,
        out_shape=shape(*value.shape, dtype=value.dtype),
        in_specs=anywhere(1 + len(after)),
        out_specs=anywhere(1)[0],
        input_output_aliases={0: 0},
        compiler_params=params(1),
        name="gate",
    )(value, *after)


def across(own, from_core, heads, after, late=()):
    both = pl.pallas_call(
        join_kernel,
        out_shape=shape(*from_core.shape),
        in_specs=anywhere(2 + len(after)),
        out_specs=in_vmem(1)[0],
        scratch_shapes=[pltpu.SemaphoreType.DMA((2,))],
        compiler_params=params(2),
        name="join",
    )(own, from_core, *after)
    return swap(gate(both, late) if late else both, "head", heads, 2)


def bit_reversed(count):
    if count == 1:
        return [0]
    half = [2 * i for i in bit_reversed(count // 2)]
    return half + [i + 1 for i in half]


def local(queries, keys, values, segment_ids, grad_out):
    rows = queries.shape[0]
    heads = lax.axis_size("head")
    tokens = rows * heads
    kv_heads = KVH // heads
    shards = lax.axis_size("ctx")
    order = bit_reversed(shards)
    half = SLOT_DEV * shards // 2
    slots = SLOT_DEV * shards
    kv_width = kv_heads * HD

    def kv_at(m):
        return (m, kv_width, 0)

    def qo_at(m, g):
        return (m, kv_heads * GW, g * GW)

    def pack(jobs, sources, after, mib, name):
        outs = [pieces for _, dests in jobs for pieces in dests]
        return pl.pallas_call(
            functools.partial(pack_kernel, jobs),
            out_shape=[
                shape(len(pieces) * rows, 2 * width) for width, dests in jobs for pieces in dests
            ],
            in_specs=anywhere(2 + len(after)),
            out_specs=anywhere(len(outs)),
            scratch_shapes=[
                pltpu.SemaphoreType.DMA((2 * sum(len(p) for _, dests in jobs for p in dests),))
            ],
            compiler_params=params(mib),
            name=name,
        )(*sources, *after)

    kv_out = pl.pallas_call(
        functools.partial(pack_kv_kernel, kv_heads),
        out_shape=[shape(rows, 2 * kv_width)] * heads,
        in_specs=in_vmem(2),
        out_specs=in_vmem(heads),
        compiler_params=params(2),
        name="pack_kv",
    )(keys, values)
    kv = [kv_out[0]] + [swap(kv_out[m], "head", heads, m) for m in range(1, heads)]

    jobs = [(GW, [[qo_at(1, g), qo_at(3, g)], [qo_at(2, g)]]) for g in range(kv_heads)]
    packed = pack(jobs, (queries, grad_out), kv_out[:1], 4, "pack_qo")
    from_core = [swap(gate(packed[2 * g], kv[1:]), "head", heads, 1) for g in range(kv_heads)]

    merged, hide = pl.pallas_call(
        functools.partial(merge_kernel, heads),
        out_shape=[shape(SLOT_DEV, 2 * kv_width), shape(kv_heads, tokens, HD)],
        in_specs=in_vmem(1 + heads) + anywhere(1),
        out_specs=in_vmem(2),
        scratch_shapes=[pltpu.VMEM((tokens, 2 * kv_width), jnp.bfloat16)],
        compiler_params=params(4),
        name="merge",
    )(segment_ids, *kv, packed[1])

    held = {0: merged}
    for m in range(1, shards):
        low = m & -m
        held[m] = swap(held[m - low], "ctx", shards, low)

    early = [merged] + from_core
    qo = [(from_core[0], across(packed[1], from_core[0], heads, early))]
    late = [held[m] for m in range(1, shards - 1)] + [qo[0][1]]
    for g in range(1, kv_heads):
        qo.append((from_core[g], across(packed[2 * g + 1], from_core[g], heads, early, late)))

    all_rows = tokens * GROUP
    saved = []
    for g in range(kv_heads):
        outs = pl.pallas_call(
            functools.partial(attend_kernel, g, order),
            out_shape=[
                shape(slots, all_rows),
                shape(slots, all_rows),
                shape(rows, all_rows),
                shape(rows, all_rows),
                shape(all_rows, HD),
                shape(all_rows, HD),
                shape(HD, slots),
                shape(half, 2 * HD),
            ],
            in_specs=anywhere(2) + in_vmem(1 + heads + shards + len(qo[g])) + anywhere(g > 0),
            out_specs=in_vmem(8),
            scratch_shapes=[
                pltpu.VMEM((slots + rows, 2 * HD), jnp.bfloat16),
                pltpu.VMEM((slots + rows, HD), jnp.bfloat16),
                pltpu.VMEM((rows, 2 * GW), jnp.bfloat16),
                pltpu.SemaphoreType.DMA((2,)),
            ],
            compiler_params=params(24),
            cost_estimate=pl.CostEstimate(
                flops=6 * all_rows * (slots + rows) * HD,
                bytes_accessed=8 * 2**20,
                transcendentals=all_rows * slots,
            ),
            name="attend",
        )(
            queries,
            grad_out,
            hide,
            *kv,
            *[held[m] for m in order],
            *qo[g],
            *([saved[-1][2]] if g else []),
        )
        saved.append(outs)
    far = [swap(outs[7], "ctx", shards, 1) for outs in saved]
    near = []
    own = []
    dq = []
    for g in range(kv_heads):
        outs = pl.pallas_call(
            functools.partial(finish_kernel, g, heads),
            out_shape=[
                shape(half, 2 * HD, dtype=jnp.float32),
                shape(tokens, 2 * HD, dtype=jnp.float32),
                shape(tokens, GW),
            ],
            in_specs=in_vmem(7) + anywhere(1) + in_vmem(heads),
            out_specs=in_vmem(3),
            compiler_params=params(16),
            cost_estimate=pl.CostEstimate(
                flops=4 * all_rows * (slots + rows) * HD,
                bytes_accessed=8 * 2**20,
                transcendentals=0,
            ),
            name="finish",
        )(*saved[g][:7], saved[-1][2], *kv)
        near.append(outs[0])
        own.append(outs[1])
        dq.append(outs[2])

    spread_args = []
    for g in range(kv_heads):
        keep, received, step = near[g], far[g], 2
        while step < shards:
            count = keep.shape[0] // 2
            keep, send = pl.pallas_call(
                add_kernel,
                out_shape=[shape(count, 2 * HD, dtype=jnp.float32), shape(count, 2 * HD)],
                in_specs=in_vmem(2),
                out_specs=in_vmem(2),
                compiler_params=params(8),
                name="add",
            )(keep, received)
            received = swap(send, "ctx", shards, step)
            step *= 2
        spread_args += [keep, received, own[g]]

    grad_keys, grad_values = pl.pallas_call(
        functools.partial(spread_kernel, 3),
        out_shape=[shape(tokens, kv_width)] * 2,
        in_specs=in_vmem(1 + len(spread_args)),
        out_specs=in_vmem(2),
        compiler_params=params(12),
        name="spread",
    )(segment_ids, *spread_args)
    return jnp.concatenate(dq, axis=1), grad_keys, grad_values


def solution(mesh):
    return jax.shard_map(
        local,
        mesh=mesh,
        in_specs=(
            P(("ctx", "head"), None),
            P(("ctx", "head"), None),
            P(("ctx", "head"), None),
            P("head", "ctx"),
            P(("ctx", "head"), None),
        ),
        out_specs=(P("ctx", "head"), P("ctx", "head"), P("ctx", "head")),
        check_vma=False,
    )
```

```python
import functools

import jax
import jax.numpy as jnp
from jax import lax
from jax.experimental import pallas as pl
from jax.experimental.pallas import tpu as pltpu
from jax.sharding import PartitionSpec as P

QH = 64
KVH = 8
HD = 128
SLOT_DEV = 96
GROUP = QH // KVH
GW = GROUP * HD
SCALE = HD ** (-0.5)
LOG2E = 1.4426950408889634
DEAD = 1024.0
HIDDEN = 2.0**96


def nt(a, b):
    return lax.dot_general(a, b, (((1,), (1,)), ((), ())), preferred_element_type=jnp.float32)


def nn(a, b):
    return lax.dot_general(a, b, (((1,), (0,)), ((), ())), preferred_element_type=jnp.float32)


def tn(a, b):
    return lax.dot_general(a, b, (((0,), (0,)), ((), ())), preferred_element_type=jnp.float32)


def slot_picks(seg_row, tokens):
    return lax.broadcasted_iota(jnp.int32, (SLOT_DEV, tokens), 0) == seg_row


def place():
    return lax.axis_index("ctx"), lax.axis_index("head")


def lanes(start, size):
    return pl.ds(pl.multiple_of(start, HD), size)


def run_copies(copies):
    for copy in copies:
        copy.start()
    return copies


def wait_copies(copies):
    for copy in copies:
        copy.wait()


def pack_kernel(jobs, *refs):
    outs = [out for _, dests in jobs for out in dests]
    sources, out_refs, sems = refs[:2], refs[-len(outs) - 1 : -1], refs[-1]
    me = place()[1]
    copies = []
    done = 0
    for width, dests in jobs:
        for out, pieces in zip(out_refs[done:], dests):
            for at, (m, scale, offset) in enumerate(pieces):
                start = lax.bitwise_xor(me, m) * scale + offset
                for part, source in enumerate(sources):
                    rows = source.shape[0]
                    copies.append(
                        pltpu.make_async_copy(
                            source.at[:, lanes(start, width)],
                            out.at[at * rows : (at + 1) * rows, part * width : (part + 1) * width],
                            sems.at[len(copies)],
                        )
                    )
        done += len(dests)
    wait_copies(run_copies(copies))


def gate_kernel(*refs):
    pass


def join_kernel(first_ref, second_ref, *refs):
    out, sems = refs[-2:]
    rows = first_ref.shape[0]
    wait_copies(
        run_copies(
            [
                pltpu.make_async_copy(first_ref, out.at[0:rows, :], sems.at[0]),
                pltpu.make_async_copy(second_ref, out.at[rows : 2 * rows, :], sems.at[1]),
            ]
        )
    )


def pack_kv_kernel(kv_heads, key_ref, value_ref, *outs):
    me = place()[1]
    width = kv_heads * HD
    for m, out in enumerate(outs):
        start = lax.bitwise_xor(me, m) * width
        out[:, 0:width] = key_ref[:, lanes(start, width)]
        out[:, width : 2 * width] = value_ref[:, lanes(start, width)]


def merge_kernel(heads, seg_ref, *refs):
    pieces, (out, hide_ref, whole) = refs[:heads], refs[-3:]
    kv_heads, tokens = seg_ref.shape
    rows = tokens // heads
    me = place()[1]
    for m, piece in enumerate(pieces):
        start = pl.multiple_of(lax.bitwise_xor(me, m) * rows, 16)
        whole[pl.ds(start, rows), :] = piece[...]
    for g in range(kv_heads):
        picks = slot_picks(seg_ref[g : g + 1, :], tokens).astype(jnp.float32)
        counts = jnp.sum(picks, axis=1, keepdims=True)
        low_picks = picks.astype(jnp.bfloat16)
        sizes = jnp.maximum(counts, 1.0)
        for part in range(2):
            at = slice((part * kv_heads + g) * HD, (part * kv_heads + g + 1) * HD)
            rows_out = nn(low_picks, whole[:, at]) / sizes
            if part == 0:
                rows_out = jnp.where(counts == 0.0, DEAD, rows_out)
            out[:, at] = rows_out.astype(jnp.bfloat16)
        padded = -(-tokens // HD) * HD
        place_in = lax.broadcasted_iota(jnp.int32, (HD, padded), 0)
        seg = jnp.concatenate([seg_ref[g : g + 1, :]] * 2, axis=1)[:, :padded]
        late = (place_in >= seg) & (place_in < SLOT_DEV)
        hide = jnp.where(late, -HIDDEN, jnp.where(place_in == SLOT_DEV, 1.0, 0.0))
        hide_ref[g] = hide.T[:tokens].astype(jnp.bfloat16)


def attend_kernel(g, order, q_ref, o_ref, hide_ref, *refs):
    shards = len(order)
    heads = 4
    kv_pieces, blocks, refs = refs[:heads], refs[heads : heads + shards], refs[heads + shards :]
    qo_pieces = ((refs[0], g), (refs[1], 0), (refs[1], 1))
    (
        p_ref, ds_ref, own_p_ref, own_ds_ref, qs_ref, os_ref, kt_ref, far_ref,
        kx, vx, mine, sems,
    ) = refs[-12:]
    rows = q_ref.shape[0]
    kv_heads = hide_ref.shape[0]
    slots = shards * SLOT_DEV
    shard, me = place()
    key_at = slice(g * HD, (g + 1) * HD)
    value_at = slice((kv_heads + g) * HD, (kv_heads + g + 1) * HD)
    start = (me * kv_heads + g) * GW
    copies = run_copies(
        [
            pltpu.make_async_copy(
                source.at[:, lanes(start, GW)], mine.at[:, part * GW : (part + 1) * GW], sems.at[part]
            )
            for part, source in enumerate((q_ref, o_ref))
        ]
    )

    lane = lax.broadcasted_iota(jnp.int32, (SLOT_DEV, HD), 1)
    row = lax.broadcasted_iota(jnp.int32, (SLOT_DEV, HD), 0)
    for r, (m, block) in enumerate(zip(order, blocks)):
        at = pl.ds(r * SLOT_DEV, SLOT_DEV)
        key = block[:, key_at].astype(jnp.float32)
        vx[at, :] = block[:, value_at]
        if m == 0:
            extra = jnp.where(lane == row, 1.0, 0.0)
        else:
            hide = (key[:, 0:1] > 100.0) | (lax.bitwise_xor(shard, m) > shard)
            extra = jnp.where(hide & (lane >= SLOT_DEV), -HIDDEN, 0.0)
        kx[at, 0:HD] = jnp.where(key > 100.0, 0.0, key).astype(jnp.bfloat16)
        kx[at, HD : 2 * HD] = extra.astype(jnp.bfloat16)
    kx[slots : slots + rows, HD : 2 * HD] = jnp.zeros((rows, HD), jnp.bfloat16)

    width = GROUP * rows
    eye_row = lax.broadcasted_iota(jnp.int32, (rows, width), 0)
    eye_lane = lax.broadcasted_iota(jnp.int32, (rows, width), 1)
    eye = eye_row == lax.rem(eye_lane, rows)
    factor = SCALE * LOG2E

    for m in list(range(1, heads)) + [0]:
        if m == 0:
            wait_copies(copies)
        qo, part = qo_pieces[m - 1] if m else (mine, 0)
        span = slice(part * rows, (part + 1) * rows)
        at = pl.ds(pl.multiple_of(lax.bitwise_xor(me, m) * rows, 16), rows)
        chunk = slice(m * width, (m + 1) * width)
        kx[slots : slots + rows, 0:HD] = kv_pieces[m][:, key_at]
        vx[slots : slots + rows, :] = kv_pieces[m][:, value_at]
        q2 = jnp.concatenate([qo[span, h * HD : (h + 1) * HD] for h in range(GROUP)], axis=0)
        o2 = jnp.concatenate(
            [qo[span, GW + h * HD : GW + (h + 1) * HD] for h in range(GROUP)], axis=0
        )
        qs_ref[chunk, :] = q2
        os_ref[chunk, :] = o2
        qx = jnp.concatenate([q2, jnp.concatenate([hide_ref[g, at, :]] * GROUP, axis=0)], axis=1)
        scores = nt(kx[...], qx)
        own_score = jnp.sum(jnp.where(eye, scores[slots:], 0.0), axis=0, keepdims=True)
        scores = scores[:slots]
        top = jnp.maximum(jnp.max(scores, axis=0, keepdims=True), own_score)
        weights = jnp.exp2((scores - top) * factor)
        own_weight = jnp.exp2((own_score - top) * factor)
        inverse = 1.0 / (jnp.sum(weights, axis=0, keepdims=True) + own_weight)
        probs = weights * inverse
        own_prob = own_weight * inverse
        grad_probs = nt(vx[...], o2)
        own_grad_prob = jnp.sum(jnp.where(eye, grad_probs[slots:], 0.0), axis=0, keepdims=True)
        grad_probs = grad_probs[:slots]
        delta = jnp.sum(probs * grad_probs, axis=0, keepdims=True) + own_prob * own_grad_prob
        ds_ref[:, chunk] = (probs * (grad_probs - delta)).astype(jnp.bfloat16)
        p_ref[:, chunk] = probs.astype(jnp.bfloat16)
        own_grad_score = own_prob * (own_grad_prob - delta)
        own_p_ref[:, chunk] = jnp.where(eye, own_prob, 0.0).astype(jnp.bfloat16)
        own_ds_ref[:, chunk] = jnp.where(eye, own_grad_score, 0.0).astype(jnp.bfloat16)
    far = slice(slots // 2, slots)
    far_ref[:, 0:HD] = (SCALE * nn(ds_ref[far, :], qs_ref[...])).astype(far_ref.dtype)
    far_ref[:, HD : 2 * HD] = nn(p_ref[far, :], os_ref[...]).astype(far_ref.dtype)
    kt_ref[...] = kx[0:slots, 0:HD].astype(jnp.float32).T.astype(jnp.bfloat16)


def terms_kernel(heads, p_ref, ds_ref, own_p_ref, own_ds_ref, qs_ref, os_ref, after_ref, near_ref, own_ref):
    rows = own_p_ref.shape[0]
    near = slice(0, near_ref.shape[0])
    near_ref[:, 0:HD] = SCALE * nn(ds_ref[near, :], qs_ref[...])
    near_ref[:, HD : 2 * HD] = nn(p_ref[near, :], os_ref[...])
    me = place()[1]
    width = GROUP * rows
    for m in range(heads):
        at = pl.ds(pl.multiple_of(lax.bitwise_xor(me, m) * rows, 16), rows)
        chunk = slice(m * width, (m + 1) * width)
        own_ref[at, 0:HD] = SCALE * nn(own_ds_ref[:, chunk], qs_ref[chunk, :])
        own_ref[at, HD : 2 * HD] = nn(own_p_ref[:, chunk], os_ref[chunk, :])


def queries_kernel(heads, *refs):
    kv_pieces, refs, dq_ref = refs[:heads], refs[heads:-1], refs[-1]
    me = place()[1]
    for g in range(len(refs) // 3):
        ds_ref, own_ds_ref, kt_ref = refs[3 * g : 3 * g + 3]
        rows = own_ds_ref.shape[0]
        width = GROUP * rows
        for m in range(heads):
            at = pl.ds(pl.multiple_of(lax.bitwise_xor(me, m) * rows, 16), rows)
            chunk = slice(m * width, (m + 1) * width)
            own_key = kv_pieces[m][:, g * HD : (g + 1) * HD]
            dq = nn(kt_ref[...], ds_ref[:, chunk]) + tn(own_key, own_ds_ref[:, chunk])
            dq = (SCALE * dq).T.astype(jnp.bfloat16)
            for h in range(GROUP):
                column = (g * GROUP + h) * HD
                dq_ref[at, column : column + HD] = dq[h * rows : (h + 1) * rows]


def add_kernel(near_ref, far_ref, keep_ref, send_ref):
    total = near_ref[...] + far_ref[...].astype(jnp.float32)
    half = keep_ref.shape[0]
    keep_ref[...] = total[:half]
    send_ref[...] = total[half:].astype(send_ref.dtype)


def spread_kernel(parts_per_head, seg_ref, *refs):
    kv_heads, tokens = seg_ref.shape
    gk_ref, gv_ref = refs[-2:]
    for g in range(kv_heads):
        parts = refs[g * parts_per_head : (g + 1) * parts_per_head]
        total = parts[0][...].astype(jnp.float32)
        for part in parts[1:-1]:
            total = total + part[...].astype(jnp.float32)
        picks = slot_picks(seg_ref[g : g + 1, :], tokens).astype(jnp.float32)
        counts = jnp.sum(picks, axis=1, keepdims=True)
        total = total / jnp.maximum(counts, 1.0)
        high = total.astype(jnp.bfloat16)
        low = (total - high.astype(jnp.float32)).astype(jnp.bfloat16)
        picks = picks.astype(jnp.bfloat16)
        spread = tn(picks, high) + tn(picks, low) + parts[-1][...]
        gk_ref[:, g * HD : (g + 1) * HD] = spread[:, 0:HD].astype(jnp.bfloat16)
        gv_ref[:, g * HD : (g + 1) * HD] = spread[:, HD : 2 * HD].astype(jnp.bfloat16)


def in_vmem(count):
    return [pl.BlockSpec(memory_space=pltpu.VMEM)] * count


def anywhere(count):
    return [pl.BlockSpec(memory_space=pl.ANY)] * count


def params(mib):
    return pltpu.CompilerParams(vmem_limit_bytes=mib * 2**20)


def shape(*dims, dtype=jnp.bfloat16):
    return jax.ShapeDtypeStruct(dims, dtype)


def swap(x, axis, size, m):
    return lax.ppermute(x, axis, [(i, i ^ m) for i in range(size)])


def gate(value, after):
    return pl.pallas_call(
        gate_kernel,
        out_shape=shape(*value.shape, dtype=value.dtype),
        in_specs=anywhere(1 + len(after)),
        out_specs=anywhere(1)[0],
        input_output_aliases={0: 0},
        compiler_params=params(1),
        name="gate",
    )(value, *after)


def join(first, second, after):
    rows, columns = first.shape
    return pl.pallas_call(
        join_kernel,
        out_shape=shape(2 * rows, columns),
        in_specs=anywhere(2 + len(after)),
        out_specs=in_vmem(1)[0],
        scratch_shapes=[pltpu.SemaphoreType.DMA((2,))],
        compiler_params=params(2),
        name="join",
    )(first, second, *after)


def bit_reversed(count):
    if count == 1:
        return [0]
    half = [2 * i for i in bit_reversed(count // 2)]
    return half + [i + 1 for i in half]


def local(queries, keys, values, segment_ids, grad_out):
    rows = queries.shape[0]
    heads = lax.axis_size("head")
    tokens = rows * heads
    kv_heads = KVH // heads
    shards = lax.axis_size("ctx")
    order = bit_reversed(shards)
    half = SLOT_DEV * shards // 2
    slots = SLOT_DEV * shards
    kv_width = kv_heads * HD

    def kv_at(m):
        return (m, kv_width, 0)

    def qo_at(m, g):
        return (m, kv_heads * GW, g * GW)

    def pack(jobs, sources, after, mib, name):
        outs = [pieces for _, dests in jobs for pieces in dests]
        return pl.pallas_call(
            functools.partial(pack_kernel, jobs),
            out_shape=[
                shape(len(pieces) * rows, 2 * width) for width, dests in jobs for pieces in dests
            ],
            in_specs=anywhere(2 + len(after)),
            out_specs=anywhere(len(outs)),
            scratch_shapes=[
                pltpu.SemaphoreType.DMA((2 * sum(len(p) for _, dests in jobs for p in dests),))
            ],
            compiler_params=params(mib),
            name=name,
        )(*sources, *after)

    kv_out = pl.pallas_call(
        functools.partial(pack_kv_kernel, kv_heads),
        out_shape=[shape(rows, 2 * kv_width)] * heads,
        in_specs=in_vmem(2),
        out_specs=in_vmem(heads),
        compiler_params=params(2),
        name="pack_kv",
    )(keys, values)
    kv = [kv_out[0]] + [swap(kv_out[m], "head", heads, m) for m in range(1, heads)]

    dests = [[qo_at(1, g) for g in range(kv_heads)]]
    for g in range(kv_heads):
        dests += [[qo_at(2, g)], [qo_at(3, g)]]
    packed = pack([(GW, dests)], (queries, grad_out), kv_out[:1], 4, "pack_qo")
    handed = swap(gate(packed[2], kv[1:]), "head", heads, 1)

    merged, hide = pl.pallas_call(
        functools.partial(merge_kernel, heads),
        out_shape=[shape(SLOT_DEV, 2 * kv_width), shape(kv_heads, tokens, HD)],
        in_specs=in_vmem(1 + heads),
        out_specs=in_vmem(2),
        scratch_shapes=[pltpu.VMEM((tokens, 2 * kv_width), jnp.bfloat16)],
        compiler_params=params(4),
        name="merge",
    )(segment_ids, *kv)

    held = {0: merged}
    for m in range(1, shards):
        low = m & -m
        held[m] = swap(held[m - low], "ctx", shards, low)
    from_core = swap(gate(packed[0], [held[shards // 2]]), "head", heads, 1)
    from_across = [swap(join(packed[1], handed, [merged]), "head", heads, 2)]
    for g in range(1, kv_heads):
        handed = swap(gate(packed[2 * g + 2], [merged]), "head", heads, 1)
        both = join(packed[2 * g + 1], handed, ())
        late = [held[m] for m in range(1, shards - 1)] + from_across[-1:]
        from_across.append(swap(gate(both, late), "head", heads, 2))

    all_rows = tokens * GROUP
    saved = []
    for g in range(kv_heads):
        outs = pl.pallas_call(
            functools.partial(attend_kernel, g, order),
            out_shape=[
                shape(slots, all_rows),
                shape(slots, all_rows),
                shape(rows, all_rows),
                shape(rows, all_rows),
                shape(all_rows, HD),
                shape(all_rows, HD),
                shape(HD, slots),
                shape(half, 2 * HD),
            ],
            in_specs=anywhere(2) + in_vmem(3 + heads + shards) + anywhere(g > 0),
            out_specs=in_vmem(8),
            scratch_shapes=[
                pltpu.VMEM((slots + rows, 2 * HD), jnp.bfloat16),
                pltpu.VMEM((slots + rows, HD), jnp.bfloat16),
                pltpu.VMEM((rows, 2 * GW), jnp.bfloat16),
                pltpu.SemaphoreType.DMA((2,)),
            ],
            compiler_params=params(24),
            cost_estimate=pl.CostEstimate(
                flops=6 * all_rows * (slots + rows) * HD,
                bytes_accessed=8 * 2**20,
                transcendentals=all_rows * slots,
            ),
            name="attend",
        )(
            queries,
            grad_out,
            hide,
            *kv,
            *[held[m] for m in order],
            from_core,
            from_across[g],
            *([saved[-1][2]] if g else []),
        )
        saved.append(outs)
    far = [swap(outs[7], "ctx", shards, 1) for outs in saved]
    near = []
    own = []
    for g in range(kv_heads):
        outs = pl.pallas_call(
            functools.partial(terms_kernel, heads),
            out_shape=[
                shape(half, 2 * HD, dtype=jnp.float32),
                shape(tokens, 2 * HD, dtype=jnp.float32),
            ],
            in_specs=in_vmem(6) + anywhere(1),
            out_specs=in_vmem(2),
            compiler_params=params(16),
            cost_estimate=pl.CostEstimate(
                flops=2 * all_rows * slots * HD, bytes_accessed=2**20, transcendentals=0
            ),
            name="terms",
        )(*saved[g][:6], saved[-1][2])
        near.append(outs[0])
        own.append(outs[1])
    dq = pl.pallas_call(
        functools.partial(queries_kernel, heads),
        out_shape=shape(tokens, kv_heads * GW),
        in_specs=in_vmem(heads + 3 * kv_heads),
        out_specs=in_vmem(1)[0],
        compiler_params=params(16),
        cost_estimate=pl.CostEstimate(
            flops=2 * kv_heads * all_rows * slots * HD, bytes_accessed=2**20, transcendentals=0
        ),
        name="queries",
    )(*kv, *[x for outs in saved for x in (outs[1], outs[3], outs[6])])

    spread_args = []
    for g in range(kv_heads):
        keep, received, step = near[g], far[g], 2
        while step < shards:
            count = keep.shape[0] // 2
            keep, send = pl.pallas_call(
                add_kernel,
                out_shape=[shape(count, 2 * HD, dtype=jnp.float32), shape(count, 2 * HD)],
                in_specs=in_vmem(2),
                out_specs=in_vmem(2),
                compiler_params=params(8),
                name="add",
            )(keep, received)
            received = swap(send, "ctx", shards, step)
            step *= 2
        spread_args += [keep, received, own[g]]

    grad_keys, grad_values = pl.pallas_call(
        functools.partial(spread_kernel, 3),
        out_shape=[shape(tokens, kv_width)] * 2,
        in_specs=in_vmem(1 + len(spread_args)),
        out_specs=in_vmem(2),
        compiler_params=params(12),
        name="spread",
    )(segment_ids, *spread_args)
    return dq, grad_keys, grad_values


def solution(mesh):
    return jax.shard_map(
        local,
        mesh=mesh,
        in_specs=(
            P(("ctx", "head"), None),
            P(("ctx", "head"), None),
            P(("ctx", "head"), None),
            P("head", "ctx"),
            P(("ctx", "head"), None),
        ),
        out_specs=(P("ctx", "head"), P("ctx", "head"), P("ctx", "head")),
        check_vma=False,
    )
```

```python
import functools

import jax
import jax.numpy as jnp
from jax import lax
from jax.experimental import pallas as pl
from jax.experimental.pallas import tpu as pltpu
from jax.sharding import PartitionSpec as P

QH = 64
KVH = 8
HD = 128
SLOT_DEV = 96
GROUP = QH // KVH
GW = GROUP * HD
SCALE = HD ** (-0.5)
LOG2E = 1.4426950408889634
DEAD = 1024.0
HIDDEN = 2.0**96


def nt(a, b):
    return lax.dot_general(a, b, (((1,), (1,)), ((), ())), preferred_element_type=jnp.float32)


def nn(a, b):
    return lax.dot_general(a, b, (((1,), (0,)), ((), ())), preferred_element_type=jnp.float32)


def tn(a, b):
    return lax.dot_general(a, b, (((0,), (0,)), ((), ())), preferred_element_type=jnp.float32)


def slot_picks(seg_row, tokens):
    return lax.broadcasted_iota(jnp.int32, (SLOT_DEV, tokens), 0) == seg_row


def place():
    return lax.axis_index("ctx"), lax.axis_index("head")


def lanes(start, size):
    return pl.ds(pl.multiple_of(start, HD), size)


def run_copies(copies):
    for copy in copies:
        copy.start()
    return copies


def wait_copies(copies):
    for copy in copies:
        copy.wait()


def pack_kernel(jobs, *refs):
    outs = [out for _, dests in jobs for out in dests]
    sources, out_refs, sems = refs[:2], refs[-len(outs) - 1 : -1], refs[-1]
    me = place()[1]
    copies = []
    done = 0
    for width, dests in jobs:
        for out, pieces in zip(out_refs[done:], dests):
            for at, (m, scale, offset) in enumerate(pieces):
                start = lax.bitwise_xor(me, m) * scale + offset
                for part, source in enumerate(sources):
                    rows = source.shape[0]
                    copies.append(
                        pltpu.make_async_copy(
                            source.at[:, lanes(start, width)],
                            out.at[at * rows : (at + 1) * rows, part * width : (part + 1) * width],
                            sems.at[len(copies)],
                        )
                    )
        done += len(dests)
    wait_copies(run_copies(copies))


def gate_kernel(*refs):
    pass


def join_kernel(part, own_ref, handed_ref, *refs):
    out, sems = refs[-2:]
    rows = own_ref.shape[0]
    handed = handed_ref.at[part * rows : (part + 1) * rows, :]
    wait_copies(
        run_copies(
            [
                pltpu.make_async_copy(own_ref, out.at[0:rows, :], sems.at[0]),
                pltpu.make_async_copy(handed, out.at[rows : 2 * rows, :], sems.at[1]),
            ]
        )
    )


def pack_kv_kernel(kv_heads, key_ref, value_ref, *outs):
    me = place()[1]
    width = kv_heads * HD
    for m, out in enumerate(outs):
        start = lax.bitwise_xor(me, m) * width
        out[:, 0:width] = key_ref[:, lanes(start, width)]
        out[:, width : 2 * width] = value_ref[:, lanes(start, width)]


def merge_kernel(heads, seg_ref, *refs):
    pieces, (out, hide_ref, whole) = refs[:heads], refs[-3:]
    kv_heads, tokens = seg_ref.shape
    rows = tokens // heads
    me = place()[1]
    for m, piece in enumerate(pieces):
        start = pl.multiple_of(lax.bitwise_xor(me, m) * rows, 16)
        whole[pl.ds(start, rows), :] = piece[...]
    for g in range(kv_heads):
        picks = slot_picks(seg_ref[g : g + 1, :], tokens).astype(jnp.float32)
        counts = jnp.sum(picks, axis=1, keepdims=True)
        low_picks = picks.astype(jnp.bfloat16)
        sizes = jnp.maximum(counts, 1.0)
        for part in range(2):
            at = slice((part * kv_heads + g) * HD, (part * kv_heads + g + 1) * HD)
            rows_out = nn(low_picks, whole[:, at]) / sizes
            if part == 0:
                rows_out = jnp.where(counts == 0.0, DEAD, rows_out)
            out[:, at] = rows_out.astype(jnp.bfloat16)
        padded = -(-tokens // HD) * HD
        place_in = lax.broadcasted_iota(jnp.int32, (HD, padded), 0)
        seg = jnp.concatenate([seg_ref[g : g + 1, :]] * 2, axis=1)[:, :padded]
        late = (place_in >= seg) & (place_in < SLOT_DEV)
        hide = jnp.where(late, -HIDDEN, jnp.where(place_in == SLOT_DEV, 1.0, 0.0))
        hide_ref[g] = hide.T[:tokens].astype(jnp.bfloat16)


def attend_kernel(g, order, q_ref, o_ref, hide_ref, *refs):
    shards = len(order)
    heads = 4
    kv_pieces, blocks, refs = refs[:heads], refs[heads : heads + shards], refs[heads + shards :]
    qo_pieces = ((refs[0], g), (refs[1], 0), (refs[1], 1))
    (
        p_ref, ds_ref, own_p_ref, own_ds_ref, qs_ref, os_ref, kt_ref, far_ref,
        kx, vx, mine, sems,
    ) = refs[-12:]
    rows = q_ref.shape[0]
    kv_heads = hide_ref.shape[0]
    slots = shards * SLOT_DEV
    shard, me = place()
    key_at = slice(g * HD, (g + 1) * HD)
    value_at = slice((kv_heads + g) * HD, (kv_heads + g + 1) * HD)
    start = (me * kv_heads + g) * GW
    copies = run_copies(
        [
            pltpu.make_async_copy(
                source.at[:, lanes(start, GW)], mine.at[:, part * GW : (part + 1) * GW], sems.at[part]
            )
            for part, source in enumerate((q_ref, o_ref))
        ]
    )

    lane = lax.broadcasted_iota(jnp.int32, (SLOT_DEV, HD), 1)
    row = lax.broadcasted_iota(jnp.int32, (SLOT_DEV, HD), 0)
    for r, (m, block) in enumerate(zip(order, blocks)):
        at = pl.ds(r * SLOT_DEV, SLOT_DEV)
        key = block[:, key_at].astype(jnp.float32)
        vx[at, :] = block[:, value_at]
        if m == 0:
            extra = jnp.where(lane == row, 1.0, 0.0)
        else:
            hide = (key[:, 0:1] > 100.0) | (lax.bitwise_xor(shard, m) > shard)
            extra = jnp.where(hide & (lane >= SLOT_DEV), -HIDDEN, 0.0)
        kx[at, 0:HD] = jnp.where(key > 100.0, 0.0, key).astype(jnp.bfloat16)
        kx[at, HD : 2 * HD] = extra.astype(jnp.bfloat16)
    kx[slots : slots + rows, HD : 2 * HD] = jnp.zeros((rows, HD), jnp.bfloat16)

    width = GROUP * rows
    eye_row = lax.broadcasted_iota(jnp.int32, (rows, width), 0)
    eye_lane = lax.broadcasted_iota(jnp.int32, (rows, width), 1)
    eye = eye_row == lax.rem(eye_lane, rows)
    factor = SCALE * LOG2E

    for m in list(range(1, heads)) + [0]:
        if m == 0:
            wait_copies(copies)
        qo, part = qo_pieces[m - 1] if m else (mine, 0)
        span = slice(part * rows, (part + 1) * rows)
        at = pl.ds(pl.multiple_of(lax.bitwise_xor(me, m) * rows, 16), rows)
        chunk = slice(m * width, (m + 1) * width)
        kx[slots : slots + rows, 0:HD] = kv_pieces[m][:, key_at]
        vx[slots : slots + rows, :] = kv_pieces[m][:, value_at]
        q2 = jnp.concatenate([qo[span, h * HD : (h + 1) * HD] for h in range(GROUP)], axis=0)
        o2 = jnp.concatenate(
            [qo[span, GW + h * HD : GW + (h + 1) * HD] for h in range(GROUP)], axis=0
        )
        qs_ref[chunk, :] = q2
        os_ref[chunk, :] = o2
        qx = jnp.concatenate([q2, jnp.concatenate([hide_ref[g, at, :]] * GROUP, axis=0)], axis=1)
        scores = nt(kx[...], qx)
        own_score = jnp.sum(jnp.where(eye, scores[slots:], 0.0), axis=0, keepdims=True)
        scores = scores[:slots]
        top = jnp.maximum(jnp.max(scores, axis=0, keepdims=True), own_score)
        weights = jnp.exp2((scores - top) * factor)
        own_weight = jnp.exp2((own_score - top) * factor)
        inverse = 1.0 / (jnp.sum(weights, axis=0, keepdims=True) + own_weight)
        probs = weights * inverse
        own_prob = own_weight * inverse
        grad_probs = nt(vx[...], o2)
        own_grad_prob = jnp.sum(jnp.where(eye, grad_probs[slots:], 0.0), axis=0, keepdims=True)
        grad_probs = grad_probs[:slots]
        delta = jnp.sum(probs * grad_probs, axis=0, keepdims=True) + own_prob * own_grad_prob
        ds_ref[:, chunk] = (probs * (grad_probs - delta)).astype(jnp.bfloat16)
        p_ref[:, chunk] = probs.astype(jnp.bfloat16)
        own_grad_score = own_prob * (own_grad_prob - delta)
        own_p_ref[:, chunk] = jnp.where(eye, own_prob, 0.0).astype(jnp.bfloat16)
        own_ds_ref[:, chunk] = jnp.where(eye, own_grad_score, 0.0).astype(jnp.bfloat16)
    far = slice(slots // 2, slots)
    far_ref[:, 0:HD] = (SCALE * nn(ds_ref[far, :], qs_ref[...])).astype(far_ref.dtype)
    far_ref[:, HD : 2 * HD] = nn(p_ref[far, :], os_ref[...]).astype(far_ref.dtype)
    kt_ref[...] = kx[0:slots, 0:HD].astype(jnp.float32).T.astype(jnp.bfloat16)


def terms_kernel(heads, p_ref, ds_ref, own_p_ref, own_ds_ref, qs_ref, os_ref, after_ref, near_ref, own_ref):
    rows = own_p_ref.shape[0]
    near = slice(0, near_ref.shape[0])
    near_ref[:, 0:HD] = SCALE * nn(ds_ref[near, :], qs_ref[...])
    near_ref[:, HD : 2 * HD] = nn(p_ref[near, :], os_ref[...])
    me = place()[1]
    width = GROUP * rows
    for m in range(heads):
        at = pl.ds(pl.multiple_of(lax.bitwise_xor(me, m) * rows, 16), rows)
        chunk = slice(m * width, (m + 1) * width)
        own_ref[at, 0:HD] = SCALE * nn(own_ds_ref[:, chunk], qs_ref[chunk, :])
        own_ref[at, HD : 2 * HD] = nn(own_p_ref[:, chunk], os_ref[chunk, :])


def queries_kernel(heads, *refs):
    kv_pieces, refs, dq_ref = refs[:heads], refs[heads:-1], refs[-1]
    me = place()[1]
    for g in range(len(refs) // 3):
        ds_ref, own_ds_ref, kt_ref = refs[3 * g : 3 * g + 3]
        rows = own_ds_ref.shape[0]
        width = GROUP * rows
        for m in range(heads):
            at = pl.ds(pl.multiple_of(lax.bitwise_xor(me, m) * rows, 16), rows)
            chunk = slice(m * width, (m + 1) * width)
            own_key = kv_pieces[m][:, g * HD : (g + 1) * HD]
            dq = nn(kt_ref[...], ds_ref[:, chunk]) + tn(own_key, own_ds_ref[:, chunk])
            dq = (SCALE * dq).T.astype(jnp.bfloat16)
            for h in range(GROUP):
                column = (g * GROUP + h) * HD
                dq_ref[at, column : column + HD] = dq[h * rows : (h + 1) * rows]


def add_kernel(near_ref, far_ref, keep_ref, send_ref):
    total = near_ref[...] + far_ref[...].astype(jnp.float32)
    half = keep_ref.shape[0]
    keep_ref[...] = total[:half]
    send_ref[...] = total[half:].astype(send_ref.dtype)


def spread_kernel(parts_per_head, seg_ref, *refs):
    kv_heads, tokens = seg_ref.shape
    gk_ref, gv_ref = refs[-2:]
    for g in range(kv_heads):
        parts = refs[g * parts_per_head : (g + 1) * parts_per_head]
        total = parts[0][...].astype(jnp.float32)
        for part in parts[1:-1]:
            total = total + part[...].astype(jnp.float32)
        picks = slot_picks(seg_ref[g : g + 1, :], tokens).astype(jnp.float32)
        counts = jnp.sum(picks, axis=1, keepdims=True)
        total = total / jnp.maximum(counts, 1.0)
        high = total.astype(jnp.bfloat16)
        low = (total - high.astype(jnp.float32)).astype(jnp.bfloat16)
        picks = picks.astype(jnp.bfloat16)
        spread = tn(picks, high) + tn(picks, low) + parts[-1][...]
        gk_ref[:, g * HD : (g + 1) * HD] = spread[:, 0:HD].astype(jnp.bfloat16)
        gv_ref[:, g * HD : (g + 1) * HD] = spread[:, HD : 2 * HD].astype(jnp.bfloat16)


def in_vmem(count):
    return [pl.BlockSpec(memory_space=pltpu.VMEM)] * count


def anywhere(count):
    return [pl.BlockSpec(memory_space=pl.ANY)] * count


def params(mib):
    return pltpu.CompilerParams(vmem_limit_bytes=mib * 2**20)


def shape(*dims, dtype=jnp.bfloat16):
    return jax.ShapeDtypeStruct(dims, dtype)


def swap(x, axis, size, m):
    return lax.ppermute(x, axis, [(i, i ^ m) for i in range(size)])


def gate(value, after):
    return pl.pallas_call(
        gate_kernel,
        out_shape=shape(*value.shape, dtype=value.dtype),
        in_specs=anywhere(1 + len(after)),
        out_specs=anywhere(1)[0],
        input_output_aliases={0: 0},
        compiler_params=params(1),
        name="gate",
    )(value, *after)


def join(own, handed, part, after):
    rows, columns = own.shape
    return pl.pallas_call(
        functools.partial(join_kernel, part),
        out_shape=shape(2 * rows, columns),
        in_specs=anywhere(2 + len(after)),
        out_specs=in_vmem(1)[0],
        scratch_shapes=[pltpu.SemaphoreType.DMA((2,))],
        compiler_params=params(2),
        name="join",
    )(own, handed, *after)


def bit_reversed(count):
    if count == 1:
        return [0]
    half = [2 * i for i in bit_reversed(count // 2)]
    return half + [i + 1 for i in half]


def local(queries, keys, values, segment_ids, grad_out):
    rows = queries.shape[0]
    heads = lax.axis_size("head")
    tokens = rows * heads
    kv_heads = KVH // heads
    shards = lax.axis_size("ctx")
    order = bit_reversed(shards)
    half = SLOT_DEV * shards // 2
    slots = SLOT_DEV * shards
    kv_width = kv_heads * HD

    def kv_at(m):
        return (m, kv_width, 0)

    def qo_at(m, g):
        return (m, kv_heads * GW, g * GW)

    def pack(jobs, sources, after, mib, name):
        outs = [pieces for _, dests in jobs for pieces in dests]
        return pl.pallas_call(
            functools.partial(pack_kernel, jobs),
            out_shape=[
                shape(len(pieces) * rows, 2 * width) for width, dests in jobs for pieces in dests
            ],
            in_specs=anywhere(2 + len(after)),
            out_specs=anywhere(len(outs)),
            scratch_shapes=[
                pltpu.SemaphoreType.DMA((2 * sum(len(p) for _, dests in jobs for p in dests),))
            ],
            compiler_params=params(mib),
            name=name,
        )(*sources, *after)

    kv_out = pl.pallas_call(
        functools.partial(pack_kv_kernel, kv_heads),
        out_shape=[shape(rows, 2 * kv_width)] * heads,
        in_specs=in_vmem(2),
        out_specs=in_vmem(heads),
        compiler_params=params(2),
        name="pack_kv",
    )(keys, values)
    kv = [kv_out[0]] + [swap(kv_out[m], "head", heads, m) for m in range(1, heads)]

    groups = range(kv_heads)
    dests = [[qo_at(1, g) for g in groups], [qo_at(3, g) for g in groups]]
    dests += [[qo_at(2, g)] for g in groups]
    packed = pack([(GW, dests)], (queries, grad_out), kv_out[:1], 4, "pack_qo")
    handed = swap(gate(packed[1], kv[1:]), "head", heads, 1)

    merged, hide = pl.pallas_call(
        functools.partial(merge_kernel, heads),
        out_shape=[shape(SLOT_DEV, 2 * kv_width), shape(kv_heads, tokens, HD)],
        in_specs=in_vmem(1 + heads),
        out_specs=in_vmem(2),
        scratch_shapes=[pltpu.VMEM((tokens, 2 * kv_width), jnp.bfloat16)],
        compiler_params=params(4),
        name="merge",
    )(segment_ids, *kv)

    held = {0: merged}
    for m in range(2, shards, 2):
        held[m] = swap(merged, "ctx", shards, m)
    for m in range(0, shards, 2):
        held[m + 1] = swap(held[m], "ctx", shards, 1)
    from_core = swap(gate(packed[0], [held[shards // 2]]), "head", heads, 1)
    from_across = [swap(join(packed[2], handed, 0, [merged]), "head", heads, 2)]
    for g in range(1, kv_heads):
        both = join(packed[2 + g], handed, g, ())
        late = [held[m] for m in range(1, shards) if m % 2 == 0 or m < 4] + from_across[-1:]
        from_across.append(swap(gate(both, late), "head", heads, 2))

    all_rows = tokens * GROUP
    saved = []
    for g in range(kv_heads):
        outs = pl.pallas_call(
            functools.partial(attend_kernel, g, order),
            out_shape=[
                shape(slots, all_rows),
                shape(slots, all_rows),
                shape(rows, all_rows),
                shape(rows, all_rows),
                shape(all_rows, HD),
                shape(all_rows, HD),
                shape(HD, slots),
                shape(half, 2 * HD),
            ],
            in_specs=anywhere(2) + in_vmem(3 + heads + shards) + anywhere(g > 0),
            out_specs=in_vmem(8),
            scratch_shapes=[
                pltpu.VMEM((slots + rows, 2 * HD), jnp.bfloat16),
                pltpu.VMEM((slots + rows, HD), jnp.bfloat16),
                pltpu.VMEM((rows, 2 * GW), jnp.bfloat16),
                pltpu.SemaphoreType.DMA((2,)),
            ],
            compiler_params=params(24),
            cost_estimate=pl.CostEstimate(
                flops=6 * all_rows * (slots + rows) * HD,
                bytes_accessed=8 * 2**20,
                transcendentals=all_rows * slots,
            ),
            name="attend",
        )(
            queries,
            grad_out,
            hide,
            *kv,
            *[held[m] for m in order],
            from_core,
            from_across[g],
            *([saved[-1][2]] if g else []),
        )
        saved.append(outs)
    far = [swap(outs[7], "ctx", shards, 1) for outs in saved]
    near = []
    own = []
    for g in range(kv_heads):
        outs = pl.pallas_call(
            functools.partial(terms_kernel, heads),
            out_shape=[
                shape(half, 2 * HD, dtype=jnp.float32),
                shape(tokens, 2 * HD, dtype=jnp.float32),
            ],
            in_specs=in_vmem(6) + anywhere(1),
            out_specs=in_vmem(2),
            compiler_params=params(16),
            cost_estimate=pl.CostEstimate(
                flops=2 * all_rows * slots * HD, bytes_accessed=2**20, transcendentals=0
            ),
            name="terms",
        )(*saved[g][:6], saved[-1][2])
        near.append(outs[0])
        own.append(outs[1])
    dq = pl.pallas_call(
        functools.partial(queries_kernel, heads),
        out_shape=shape(tokens, kv_heads * GW),
        in_specs=in_vmem(heads + 3 * kv_heads),
        out_specs=in_vmem(1)[0],
        compiler_params=params(16),
        cost_estimate=pl.CostEstimate(
            flops=2 * kv_heads * all_rows * slots * HD, bytes_accessed=2**20, transcendentals=0
        ),
        name="queries",
    )(*kv, *[x for outs in saved for x in (outs[1], outs[3], outs[6])])

    spread_args = []
    for g in range(kv_heads):
        keep, received, step = near[g], far[g], 2
        while step < shards:
            count = keep.shape[0] // 2
            keep, send = pl.pallas_call(
                add_kernel,
                out_shape=[shape(count, 2 * HD, dtype=jnp.float32), shape(count, 2 * HD)],
                in_specs=in_vmem(2),
                out_specs=in_vmem(2),
                compiler_params=params(8),
                name="add",
            )(keep, received)
            received = swap(send, "ctx", shards, step)
            step *= 2
        spread_args += [keep, received, own[g]]

    grad_keys, grad_values = pl.pallas_call(
        functools.partial(spread_kernel, 3),
        out_shape=[shape(tokens, kv_width)] * 2,
        in_specs=in_vmem(1 + len(spread_args)),
        out_specs=in_vmem(2),
        compiler_params=params(12),
        name="spread",
    )(segment_ids, *spread_args)
    return dq, grad_keys, grad_values


def solution(mesh):
    return jax.shard_map(
        local,
        mesh=mesh,
        in_specs=(
            P(("ctx", "head"), None),
            P(("ctx", "head"), None),
            P(("ctx", "head"), None),
            P("head", "ctx"),
            P(("ctx", "head"), None),
        ),
        out_specs=(P("ctx", "head"), P("ctx", "head"), P("ctx", "head")),
        check_vma=False,
    )
```

```python
import functools

import jax
import jax.numpy as jnp
from jax import lax
from jax.experimental import pallas as pl
from jax.experimental.pallas import tpu as pltpu
from jax.sharding import PartitionSpec as P

QH = 64
KVH = 8
HD = 128
SLOT_DEV = 96
GROUP = QH // KVH
GW = GROUP * HD
SCALE = HD ** (-0.5)
LOG2E = 1.4426950408889634
DEAD = 1024.0
HIDDEN = 2.0**96


def nt(a, b):
    return lax.dot_general(a, b, (((1,), (1,)), ((), ())), preferred_element_type=jnp.float32)


def nn(a, b):
    return lax.dot_general(a, b, (((1,), (0,)), ((), ())), preferred_element_type=jnp.float32)


def tn(a, b):
    return lax.dot_general(a, b, (((0,), (0,)), ((), ())), preferred_element_type=jnp.float32)


def slot_picks(seg_row, tokens):
    return lax.broadcasted_iota(jnp.int32, (SLOT_DEV, tokens), 0) == seg_row


def place():
    return lax.axis_index("ctx"), lax.axis_index("head")


def lanes(start, size):
    return pl.ds(pl.multiple_of(start, HD), size)


def run_copies(copies):
    for copy in copies:
        copy.start()
    return copies


def wait_copies(copies):
    for copy in copies:
        copy.wait()


def pack_kernel(jobs, *refs):
    outs = [out for _, dests in jobs for out in dests]
    sources, out_refs, sems = refs[:2], refs[-len(outs) - 1 : -1], refs[-1]
    me = place()[1]
    copies = []
    done = 0
    for width, dests in jobs:
        for out, pieces in zip(out_refs[done:], dests):
            for at, (m, scale, offset) in enumerate(pieces):
                start = lax.bitwise_xor(me, m) * scale + offset
                for part, source in enumerate(sources):
                    rows = source.shape[0]
                    copies.append(
                        pltpu.make_async_copy(
                            source.at[:, lanes(start, width)],
                            out.at[at * rows : (at + 1) * rows, part * width : (part + 1) * width],
                            sems.at[len(copies)],
                        )
                    )
        done += len(dests)
    wait_copies(run_copies(copies))


def gate_kernel(*refs):
    pass


def pack_kv_kernel(kv_heads, key_ref, value_ref, *outs):
    me = place()[1]
    width = kv_heads * HD
    for m, out in enumerate(outs):
        start = lax.bitwise_xor(me, m) * width
        out[:, 0:width] = key_ref[:, lanes(start, width)]
        out[:, width : 2 * width] = value_ref[:, lanes(start, width)]


def merge_kernel(heads, seg_ref, *refs):
    pieces, (out, hide_ref, whole) = refs[:heads], refs[-3:]
    kv_heads, tokens = seg_ref.shape
    rows = tokens // heads
    me = place()[1]
    for m, piece in enumerate(pieces):
        start = pl.multiple_of(lax.bitwise_xor(me, m) * rows, 16)
        whole[pl.ds(start, rows), :] = piece[...]
    for g in range(kv_heads):
        picks = slot_picks(seg_ref[g : g + 1, :], tokens).astype(jnp.float32)
        counts = jnp.sum(picks, axis=1, keepdims=True)
        low_picks = picks.astype(jnp.bfloat16)
        sizes = jnp.maximum(counts, 1.0)
        for part in range(2):
            at = slice((part * kv_heads + g) * HD, (part * kv_heads + g + 1) * HD)
            rows_out = nn(low_picks, whole[:, at]) / sizes
            if part == 0:
                rows_out = jnp.where(counts == 0.0, DEAD, rows_out)
            out[:, at] = rows_out.astype(jnp.bfloat16)
        padded = -(-tokens // HD) * HD
        place_in = lax.broadcasted_iota(jnp.int32, (HD, padded), 0)
        seg = jnp.concatenate([seg_ref[g : g + 1, :]] * 2, axis=1)[:, :padded]
        late = (place_in >= seg) & (place_in < SLOT_DEV)
        hide = jnp.where(late, -HIDDEN, jnp.where(place_in == SLOT_DEV, 1.0, 0.0))
        hide_ref[g] = hide.T[:tokens].astype(jnp.bfloat16)


def attend_kernel(g, order, q_ref, o_ref, hide_ref, *refs):
    shards = len(order)
    heads = 4
    kv_pieces, blocks, refs = refs[:heads], refs[heads : heads + shards], refs[heads + shards :]
    qo_pieces = refs[: heads - 1]
    (
        p_ref, ds_ref, own_p_ref, own_ds_ref, qs_ref, os_ref, kt_ref, far_ref,
        kx, vx, mine, sems,
    ) = refs[-12:]
    rows = q_ref.shape[0]
    kv_heads = hide_ref.shape[0]
    slots = shards * SLOT_DEV
    shard, me = place()
    key_at = slice(g * HD, (g + 1) * HD)
    value_at = slice((kv_heads + g) * HD, (kv_heads + g + 1) * HD)
    start = (me * kv_heads + g) * GW
    copies = run_copies(
        [
            pltpu.make_async_copy(
                source.at[:, lanes(start, GW)], mine.at[:, part * GW : (part + 1) * GW], sems.at[part]
            )
            for part, source in enumerate((q_ref, o_ref))
        ]
    )

    lane = lax.broadcasted_iota(jnp.int32, (SLOT_DEV, HD), 1)
    row = lax.broadcasted_iota(jnp.int32, (SLOT_DEV, HD), 0)
    for r, (m, block) in enumerate(zip(order, blocks)):
        at = pl.ds(r * SLOT_DEV, SLOT_DEV)
        key = block[:, key_at].astype(jnp.float32)
        vx[at, :] = block[:, value_at]
        if m == 0:
            extra = jnp.where(lane == row, 1.0, 0.0)
        else:
            hide = (key[:, 0:1] > 100.0) | (lax.bitwise_xor(shard, m) > shard)
            extra = jnp.where(hide & (lane >= SLOT_DEV), -HIDDEN, 0.0)
        kx[at, 0:HD] = jnp.where(key > 100.0, 0.0, key).astype(jnp.bfloat16)
        kx[at, HD : 2 * HD] = extra.astype(jnp.bfloat16)
    kx[slots : slots + rows, HD : 2 * HD] = jnp.zeros((rows, HD), jnp.bfloat16)

    width = GROUP * rows
    eye_row = lax.broadcasted_iota(jnp.int32, (rows, width), 0)
    eye_lane = lax.broadcasted_iota(jnp.int32, (rows, width), 1)
    eye = eye_row == lax.rem(eye_lane, rows)
    factor = SCALE * LOG2E

    for m in list(range(1, heads)) + [0]:
        if m == 0:
            wait_copies(copies)
        qo, part = (qo_pieces[m - 1], g) if m else (mine, 0)
        span = slice(part * rows, (part + 1) * rows)
        at = pl.ds(pl.multiple_of(lax.bitwise_xor(me, m) * rows, 16), rows)
        chunk = slice(m * width, (m + 1) * width)
        kx[slots : slots + rows, 0:HD] = kv_pieces[m][:, key_at]
        vx[slots : slots + rows, :] = kv_pieces[m][:, value_at]
        q2 = jnp.concatenate([qo[span, h * HD : (h + 1) * HD] for h in range(GROUP)], axis=0)
        o2 = jnp.concatenate(
            [qo[span, GW + h * HD : GW + (h + 1) * HD] for h in range(GROUP)], axis=0
        )
        qs_ref[chunk, :] = q2
        os_ref[chunk, :] = o2
        qx = jnp.concatenate([q2, jnp.concatenate([hide_ref[g, at, :]] * GROUP, axis=0)], axis=1)
        scores = nt(kx[...], qx)
        own_score = jnp.sum(jnp.where(eye, scores[slots:], 0.0), axis=0, keepdims=True)
        scores = scores[:slots]
        top = jnp.maximum(jnp.max(scores, axis=0, keepdims=True), own_score)
        weights = jnp.exp2((scores - top) * factor)
        own_weight = jnp.exp2((own_score - top) * factor)
        inverse = 1.0 / (jnp.sum(weights, axis=0, keepdims=True) + own_weight)
        probs = weights * inverse
        own_prob = own_weight * inverse
        grad_probs = nt(vx[...], o2)
        own_grad_prob = jnp.sum(jnp.where(eye, grad_probs[slots:], 0.0), axis=0, keepdims=True)
        grad_probs = grad_probs[:slots]
        delta = jnp.sum(probs * grad_probs, axis=0, keepdims=True) + own_prob * own_grad_prob
        ds_ref[:, chunk] = (probs * (grad_probs - delta)).astype(jnp.bfloat16)
        p_ref[:, chunk] = probs.astype(jnp.bfloat16)
        own_grad_score = own_prob * (own_grad_prob - delta)
        own_p_ref[:, chunk] = jnp.where(eye, own_prob, 0.0).astype(jnp.bfloat16)
        own_ds_ref[:, chunk] = jnp.where(eye, own_grad_score, 0.0).astype(jnp.bfloat16)
    far = slice(slots // 2, slots)
    far_ref[:, 0:HD] = (SCALE * nn(ds_ref[far, :], qs_ref[...])).astype(far_ref.dtype)
    far_ref[:, HD : 2 * HD] = nn(p_ref[far, :], os_ref[...]).astype(far_ref.dtype)
    kt_ref[...] = kx[0:slots, 0:HD].astype(jnp.float32).T.astype(jnp.bfloat16)


def terms_kernel(heads, p_ref, ds_ref, own_p_ref, own_ds_ref, qs_ref, os_ref, after_ref, near_ref, own_ref):
    rows = own_p_ref.shape[0]
    near = slice(0, near_ref.shape[0])
    near_ref[:, 0:HD] = SCALE * nn(ds_ref[near, :], qs_ref[...])
    near_ref[:, HD : 2 * HD] = nn(p_ref[near, :], os_ref[...])
    me = place()[1]
    width = GROUP * rows
    for m in range(heads):
        at = pl.ds(pl.multiple_of(lax.bitwise_xor(me, m) * rows, 16), rows)
        chunk = slice(m * width, (m + 1) * width)
        own_ref[at, 0:HD] = SCALE * nn(own_ds_ref[:, chunk], qs_ref[chunk, :])
        own_ref[at, HD : 2 * HD] = nn(own_p_ref[:, chunk], os_ref[chunk, :])


def queries_kernel(heads, *refs):
    kv_pieces, refs, dq_ref = refs[:heads], refs[heads:-1], refs[-1]
    me = place()[1]
    for g in range(len(refs) // 3):
        ds_ref, own_ds_ref, kt_ref = refs[3 * g : 3 * g + 3]
        rows = own_ds_ref.shape[0]
        width = GROUP * rows
        for m in range(heads):
            at = pl.ds(pl.multiple_of(lax.bitwise_xor(me, m) * rows, 16), rows)
            chunk = slice(m * width, (m + 1) * width)
            own_key = kv_pieces[m][:, g * HD : (g + 1) * HD]
            dq = nn(kt_ref[...], ds_ref[:, chunk]) + tn(own_key, own_ds_ref[:, chunk])
            dq = (SCALE * dq).T.astype(jnp.bfloat16)
            for h in range(GROUP):
                column = (g * GROUP + h) * HD
                dq_ref[at, column : column + HD] = dq[h * rows : (h + 1) * rows]


def add_kernel(near_ref, far_ref, keep_ref, send_ref):
    total = near_ref[...] + far_ref[...].astype(jnp.float32)
    half = keep_ref.shape[0]
    keep_ref[...] = total[:half]
    send_ref[...] = total[half:].astype(send_ref.dtype)


def spread_kernel(parts_per_head, seg_ref, *refs):
    kv_heads, tokens = seg_ref.shape
    gk_ref, gv_ref = refs[-2:]
    for g in range(kv_heads):
        parts = refs[g * parts_per_head : (g + 1) * parts_per_head]
        total = parts[0][...].astype(jnp.float32)
        for part in parts[1:-1]:
            total = total + part[...].astype(jnp.float32)
        picks = slot_picks(seg_ref[g : g + 1, :], tokens).astype(jnp.float32)
        counts = jnp.sum(picks, axis=1, keepdims=True)
        total = total / jnp.maximum(counts, 1.0)
        high = total.astype(jnp.bfloat16)
        low = (total - high.astype(jnp.float32)).astype(jnp.bfloat16)
        picks = picks.astype(jnp.bfloat16)
        spread = tn(picks, high) + tn(picks, low) + parts[-1][...]
        gk_ref[:, g * HD : (g + 1) * HD] = spread[:, 0:HD].astype(jnp.bfloat16)
        gv_ref[:, g * HD : (g + 1) * HD] = spread[:, HD : 2 * HD].astype(jnp.bfloat16)


def in_vmem(count):
    return [pl.BlockSpec(memory_space=pltpu.VMEM)] * count


def anywhere(count):
    return [pl.BlockSpec(memory_space=pl.ANY)] * count


def params(mib):
    return pltpu.CompilerParams(vmem_limit_bytes=mib * 2**20)


def shape(*dims, dtype=jnp.bfloat16):
    return jax.ShapeDtypeStruct(dims, dtype)


def swap(x, axis, size, m):
    return lax.ppermute(x, axis, [(i, i ^ m) for i in range(size)])


def gate(value, after, mib=0):
    return pl.pallas_call(
        gate_kernel,
        out_shape=shape(*value.shape, dtype=value.dtype),
        in_specs=anywhere(1 + len(after)),
        out_specs=anywhere(1)[0],
        input_output_aliases={0: 0},
        compiler_params=params(1),
        cost_estimate=pl.CostEstimate(flops=0, bytes_accessed=mib * 2**20, transcendentals=0),
        name="gate",
    )(value, *after)


def bit_reversed(count):
    if count == 1:
        return [0]
    half = [2 * i for i in bit_reversed(count // 2)]
    return half + [i + 1 for i in half]


def local(queries, keys, values, segment_ids, grad_out):
    rows = queries.shape[0]
    heads = lax.axis_size("head")
    tokens = rows * heads
    kv_heads = KVH // heads
    shards = lax.axis_size("ctx")
    order = bit_reversed(shards)
    half = SLOT_DEV * shards // 2
    slots = SLOT_DEV * shards
    kv_width = kv_heads * HD

    def kv_at(m):
        return (m, kv_width, 0)

    def qo_at(m, g):
        return (m, kv_heads * GW, g * GW)

    def pack(jobs, sources, after, mib, name):
        outs = [pieces for _, dests in jobs for pieces in dests]
        return pl.pallas_call(
            functools.partial(pack_kernel, jobs),
            out_shape=[
                shape(len(pieces) * rows, 2 * width) for width, dests in jobs for pieces in dests
            ],
            in_specs=anywhere(2 + len(after)),
            out_specs=anywhere(len(outs)),
            scratch_shapes=[
                pltpu.SemaphoreType.DMA((2 * sum(len(p) for _, dests in jobs for p in dests),))
            ],
            compiler_params=params(mib),
            name=name,
        )(*sources, *after)

    kv_out = pl.pallas_call(
        functools.partial(pack_kv_kernel, kv_heads),
        out_shape=[shape(rows, 2 * kv_width)] * heads,
        in_specs=in_vmem(2),
        out_specs=in_vmem(heads),
        compiler_params=params(2),
        name="pack_kv",
    )(keys, values)
    kv = [kv_out[0]] + [swap(kv_out[m], "head", heads, m) for m in range(1, heads)]

    jobs = [(GW, [[qo_at(m, g) for g in range(kv_heads)] for m in range(1, heads)])]
    packed = pack(jobs, (queries, grad_out), kv_out[:1], 4, "pack_qo")
    handed = swap(gate(packed[2], kv[1:]), "head", heads, 1)
    from_across = swap(gate(packed[1], kv[1:]), "head", heads, 2)
    from_corner = swap(handed, "head", heads, 2)

    merged, hide = pl.pallas_call(
        functools.partial(merge_kernel, heads),
        out_shape=[shape(SLOT_DEV, 2 * kv_width), shape(kv_heads, tokens, HD)],
        in_specs=in_vmem(1 + heads),
        out_specs=in_vmem(2),
        scratch_shapes=[pltpu.VMEM((tokens, 2 * kv_width), jnp.bfloat16)],
        compiler_params=params(4),
        name="merge",
    )(segment_ids, *kv)

    held = {0: merged}
    for m in range(1, shards):
        low = m & -m
        held[m] = swap(held[m - low], "ctx", shards, low)
    late = [held[m] for m in range(1, shards - 1)] + [from_across]
    from_core = swap(gate(packed[0], late), "head", heads, 1)
    from_corner = gate(from_corner, (), 40)
    qo = (from_core, from_across, from_corner)

    all_rows = tokens * GROUP
    saved = []
    for g in range(kv_heads):
        outs = pl.pallas_call(
            functools.partial(attend_kernel, g, order),
            out_shape=[
                shape(slots, all_rows),
                shape(slots, all_rows),
                shape(rows, all_rows),
                shape(rows, all_rows),
                shape(all_rows, HD),
                shape(all_rows, HD),
                shape(HD, slots),
                shape(half, 2 * HD),
            ],
            in_specs=anywhere(2) + in_vmem(heads + heads + shards) + anywhere(g > 0),
            out_specs=in_vmem(8),
            scratch_shapes=[
                pltpu.VMEM((slots + rows, 2 * HD), jnp.bfloat16),
                pltpu.VMEM((slots + rows, HD), jnp.bfloat16),
                pltpu.VMEM((rows, 2 * GW), jnp.bfloat16),
                pltpu.SemaphoreType.DMA((2,)),
            ],
            compiler_params=params(24),
            cost_estimate=pl.CostEstimate(
                flops=6 * all_rows * (slots + rows) * HD,
                bytes_accessed=8 * 2**20,
                transcendentals=all_rows * slots,
            ),
            name="attend",
        )(
            queries,
            grad_out,
            hide,
            *kv,
            *[held[m] for m in order],
            *qo,
            *([saved[-1][2]] if g else []),
        )
        saved.append(outs)
    far = [swap(outs[7], "ctx", shards, 1) for outs in saved]
    near = []
    own = []
    for g in range(kv_heads):
        outs = pl.pallas_call(
            functools.partial(terms_kernel, heads),
            out_shape=[
                shape(half, 2 * HD, dtype=jnp.float32),
                shape(tokens, 2 * HD, dtype=jnp.float32),
            ],
            in_specs=in_vmem(6) + anywhere(1),
            out_specs=in_vmem(2),
            compiler_params=params(16),
            cost_estimate=pl.CostEstimate(
                flops=2 * all_rows * slots * HD, bytes_accessed=2**20, transcendentals=0
            ),
            name="terms",
        )(*saved[g][:6], saved[-1][2])
        near.append(outs[0])
        own.append(outs[1])
    dq = pl.pallas_call(
        functools.partial(queries_kernel, heads),
        out_shape=shape(tokens, kv_heads * GW),
        in_specs=in_vmem(heads + 3 * kv_heads),
        out_specs=in_vmem(1)[0],
        compiler_params=params(16),
        cost_estimate=pl.CostEstimate(
            flops=2 * kv_heads * all_rows * slots * HD, bytes_accessed=2**20, transcendentals=0
        ),
        name="queries",
    )(*kv, *[x for outs in saved for x in (outs[1], outs[3], outs[6])])

    spread_args = []
    for g in range(kv_heads):
        keep, received, step = near[g], far[g], 2
        while step < shards:
            count = keep.shape[0] // 2
            keep, send = pl.pallas_call(
                add_kernel,
                out_shape=[shape(count, 2 * HD, dtype=jnp.float32), shape(count, 2 * HD)],
                in_specs=in_vmem(2),
                out_specs=in_vmem(2),
                compiler_params=params(8),
                name="add",
            )(keep, received)
            received = swap(send, "ctx", shards, step)
            step *= 2
        spread_args += [keep, received, own[g]]

    grad_keys, grad_values = pl.pallas_call(
        functools.partial(spread_kernel, 3),
        out_shape=[shape(tokens, kv_width)] * 2,
        in_specs=in_vmem(1 + len(spread_args)),
        out_specs=in_vmem(2),
        compiler_params=params(12),
        name="spread",
    )(segment_ids, *spread_args)
    return dq, grad_keys, grad_values


def solution(mesh):
    return jax.shard_map(
        local,
        mesh=mesh,
        in_specs=(
            P(("ctx", "head"), None),
            P(("ctx", "head"), None),
            P(("ctx", "head"), None),
            P("head", "ctx"),
            P(("ctx", "head"), None),
        ),
        out_specs=(P("ctx", "head"), P("ctx", "head"), P("ctx", "head")),
        check_vma=False,
    )
```

```python
import functools

import jax
import jax.numpy as jnp
from jax import lax
from jax.experimental import pallas as pl
from jax.experimental.pallas import tpu as pltpu
from jax.sharding import PartitionSpec as P

QH = 64
KVH = 8
HD = 128
SLOT_DEV = 96
GROUP = QH // KVH
GW = GROUP * HD
SCALE = HD ** (-0.5)
LOG2E = 1.4426950408889634
DEAD = 1024.0
HIDDEN = 2.0**96


def nt(a, b):
    return lax.dot_general(a, b, (((1,), (1,)), ((), ())), preferred_element_type=jnp.float32)


def nn(a, b):
    return lax.dot_general(a, b, (((1,), (0,)), ((), ())), preferred_element_type=jnp.float32)


def tn(a, b):
    return lax.dot_general(a, b, (((0,), (0,)), ((), ())), preferred_element_type=jnp.float32)


def slot_picks(seg_row, tokens):
    return lax.broadcasted_iota(jnp.int32, (SLOT_DEV, tokens), 0) == seg_row


def place():
    return lax.axis_index("ctx"), lax.axis_index("head")


def lanes(start, size):
    return pl.ds(pl.multiple_of(start, HD), size)


def run_copies(copies):
    for copy in copies:
        copy.start()
    return copies


def wait_copies(copies):
    for copy in copies:
        copy.wait()


def pack_kernel(jobs, *refs):
    outs = [out for _, dests in jobs for out in dests]
    sources, out_refs, sems = refs[:2], refs[-len(outs) - 1 : -1], refs[-1]
    me = place()[1]
    copies = []
    done = 0
    for width, dests in jobs:
        for out, pieces in zip(out_refs[done:], dests):
            for at, (m, scale, offset) in enumerate(pieces):
                start = lax.bitwise_xor(me, m) * scale + offset
                for part, source in enumerate(sources):
                    rows = source.shape[0]
                    copies.append(
                        pltpu.make_async_copy(
                            source.at[:, lanes(start, width)],
                            out.at[at * rows : (at + 1) * rows, part * width : (part + 1) * width],
                            sems.at[len(copies)],
                        )
                    )
        done += len(dests)
    wait_copies(run_copies(copies))


def gate_kernel(*refs):
    pass


def pack_kv_kernel(kv_heads, key_ref, value_ref, *outs):
    me = place()[1]
    width = kv_heads * HD
    for m, out in enumerate(outs):
        start = lax.bitwise_xor(me, m) * width
        out[:, 0:width] = key_ref[:, lanes(start, width)]
        out[:, width : 2 * width] = value_ref[:, lanes(start, width)]


def merge_kernel(heads, seg_ref, *refs):
    pieces, (out, hide_ref, whole) = refs[:heads], refs[-3:]
    kv_heads, tokens = seg_ref.shape
    rows = tokens // heads
    me = place()[1]
    for m, piece in enumerate(pieces):
        start = pl.multiple_of(lax.bitwise_xor(me, m) * rows, 16)
        whole[pl.ds(start, rows), :] = piece[...]
    for g in range(kv_heads):
        picks = slot_picks(seg_ref[g : g + 1, :], tokens).astype(jnp.float32)
        counts = jnp.sum(picks, axis=1, keepdims=True)
        low_picks = picks.astype(jnp.bfloat16)
        sizes = jnp.maximum(counts, 1.0)
        for part in range(2):
            at = slice((part * kv_heads + g) * HD, (part * kv_heads + g + 1) * HD)
            rows_out = nn(low_picks, whole[:, at]) / sizes
            if part == 0:
                rows_out = jnp.where(counts == 0.0, DEAD, rows_out)
            out[:, at] = rows_out.astype(jnp.bfloat16)
        padded = -(-tokens // HD) * HD
        place_in = lax.broadcasted_iota(jnp.int32, (HD, padded), 0)
        seg = jnp.concatenate([seg_ref[g : g + 1, :]] * 2, axis=1)[:, :padded]
        late = (place_in >= seg) & (place_in < SLOT_DEV)
        hide = jnp.where(late, -HIDDEN, jnp.where(place_in == SLOT_DEV, 1.0, 0.0))
        hide_ref[g] = hide.T[:tokens].astype(jnp.bfloat16)


def folded(x, reduce):
    return reduce(x.reshape(x.shape[0] // 8, 8, x.shape[1]), axis=0)


def attend_kernel(g, order, q_ref, o_ref, hide_ref, *refs):
    shards = len(order)
    heads = 4
    kv_pieces, blocks, refs = refs[:heads], refs[heads : heads + shards], refs[heads + shards :]
    qo_pieces = refs[: heads - 1]
    (
        p_ref, ds_ref, own_p_ref, own_ds_ref, qs_ref, os_ref, kt_ref, far_ref,
        kx, vx, mine, s_ref, g_ref, sems,
    ) = refs[-14:]
    rows = q_ref.shape[0]
    kv_heads = hide_ref.shape[0]
    slots = shards * SLOT_DEV
    shard, me = place()
    key_at = slice(g * HD, (g + 1) * HD)
    value_at = slice((kv_heads + g) * HD, (kv_heads + g + 1) * HD)
    start = (me * kv_heads + g) * GW
    copies = run_copies(
        [
            pltpu.make_async_copy(
                source.at[:, lanes(start, GW)], mine.at[:, part * GW : (part + 1) * GW], sems.at[part]
            )
            for part, source in enumerate((q_ref, o_ref))
        ]
    )

    lane = lax.broadcasted_iota(jnp.int32, (SLOT_DEV, HD), 1)
    row = lax.broadcasted_iota(jnp.int32, (SLOT_DEV, HD), 0)
    for r, (m, block) in enumerate(zip(order, blocks)):
        at = pl.ds(r * SLOT_DEV, SLOT_DEV)
        key = block[:, key_at].astype(jnp.float32)
        vx[at, :] = block[:, value_at]
        if m == 0:
            extra = jnp.where(lane == row, 1.0, 0.0)
        else:
            hide = (key[:, 0:1] > 100.0) | (lax.bitwise_xor(shard, m) > shard)
            extra = jnp.where(hide & (lane >= SLOT_DEV), -HIDDEN, 0.0)
        kx[at, 0:HD] = jnp.where(key > 100.0, 0.0, key).astype(jnp.bfloat16)
        kx[at, HD : 2 * HD] = extra.astype(jnp.bfloat16)
    kx[slots : slots + rows, HD : 2 * HD] = jnp.zeros((rows, HD), jnp.bfloat16)

    width = GROUP * rows
    eye_row = lax.broadcasted_iota(jnp.int32, (rows, width), 0)
    eye_lane = lax.broadcasted_iota(jnp.int32, (rows, width), 1)
    eye = eye_row == lax.rem(eye_lane, rows)
    factor = SCALE * LOG2E

    for m in list(range(1, heads)) + [0]:
        if m == 0:
            wait_copies(copies)
        qo, part = (qo_pieces[m - 1], g) if m else (mine, 0)
        span = slice(part * rows, (part + 1) * rows)
        at = pl.ds(pl.multiple_of(lax.bitwise_xor(me, m) * rows, 16), rows)
        chunk = slice(m * width, (m + 1) * width)
        kx[slots : slots + rows, 0:HD] = kv_pieces[m][:, key_at]
        vx[slots : slots + rows, :] = kv_pieces[m][:, value_at]
        q2 = jnp.concatenate([qo[span, h * HD : (h + 1) * HD] for h in range(GROUP)], axis=0)
        o2 = jnp.concatenate(
            [qo[span, GW + h * HD : GW + (h + 1) * HD] for h in range(GROUP)], axis=0
        )
        qs_ref[chunk, :] = q2
        os_ref[chunk, :] = o2
        qx = jnp.concatenate([q2, jnp.concatenate([hide_ref[g, at, :]] * GROUP, axis=0)], axis=1)
        s_at, g_at = s_ref.at[m % 2], g_ref.at[m % 2]
        s_at[...] = nt(kx[...], qx)
        g_at[...] = nt(vx[...], o2)
        own_score = jnp.sum(jnp.where(eye, s_at[slots:, :], 0.0), axis=0, keepdims=True)
        own_grad_prob = jnp.sum(jnp.where(eye, g_at[slots:, :], 0.0), axis=0, keepdims=True)
        parts = [slice(r * SLOT_DEV, (r + 1) * SLOT_DEV) for r in range(shards)]
        top = folded(functools.reduce(jnp.maximum, [s_at[part, :] for part in parts]), jnp.max)
        top = jnp.maximum(jnp.max(top, axis=0, keepdims=True), own_score)
        total = 0.0
        delta = 0.0
        for part in parts:
            weights = jnp.exp2((s_at[part, :] - top) * factor)
            total = total + folded(weights, jnp.sum)
            delta = delta + folded(weights * g_at[part, :], jnp.sum)
        own_weight = jnp.exp2((own_score - top) * factor)
        total = jnp.sum(total, axis=0, keepdims=True) + own_weight
        delta = jnp.sum(delta, axis=0, keepdims=True) + own_weight * own_grad_prob
        delta = delta / total
        own_prob = own_weight / total
        log_total = jnp.log2(total)
        for part in parts:
            probs = jnp.exp2((s_at[part, :] - top) * factor - log_total)
            p_ref[part, chunk] = probs.astype(jnp.bfloat16)
            ds_ref[part, chunk] = (probs * (g_at[part, :] - delta)).astype(jnp.bfloat16)
        own_grad_score = own_prob * (own_grad_prob - delta)
        own_p_ref[:, chunk] = jnp.where(eye, own_prob, 0.0).astype(jnp.bfloat16)
        own_ds_ref[:, chunk] = jnp.where(eye, own_grad_score, 0.0).astype(jnp.bfloat16)
    far = slice(slots // 2, slots)
    far_ref[:, 0:HD] = (SCALE * nn(ds_ref[far, :], qs_ref[...])).astype(far_ref.dtype)
    far_ref[:, HD : 2 * HD] = nn(p_ref[far, :], os_ref[...]).astype(far_ref.dtype)
    kt_ref[...] = kx[0:slots, 0:HD].astype(jnp.float32).T.astype(jnp.bfloat16)


def terms_kernel(heads, p_ref, ds_ref, own_p_ref, own_ds_ref, qs_ref, os_ref, after_ref, near_ref, own_ref):
    rows = own_p_ref.shape[0]
    near = slice(0, near_ref.shape[0])
    near_ref[:, 0:HD] = SCALE * nn(ds_ref[near, :], qs_ref[...])
    near_ref[:, HD : 2 * HD] = nn(p_ref[near, :], os_ref[...])
    me = place()[1]
    width = GROUP * rows
    for m in range(heads):
        at = pl.ds(pl.multiple_of(lax.bitwise_xor(me, m) * rows, 16), rows)
        chunk = slice(m * width, (m + 1) * width)
        own_ref[at, 0:HD] = SCALE * nn(own_ds_ref[:, chunk], qs_ref[chunk, :])
        own_ref[at, HD : 2 * HD] = nn(own_p_ref[:, chunk], os_ref[chunk, :])


def queries_kernel(heads, *refs):
    kv_pieces, refs, dq_ref = refs[:heads], refs[heads:-1], refs[-1]
    me = place()[1]
    for g in range(len(refs) // 3):
        ds_ref, own_ds_ref, kt_ref = refs[3 * g : 3 * g + 3]
        rows = own_ds_ref.shape[0]
        width = GROUP * rows
        for m in range(heads):
            at = pl.ds(pl.multiple_of(lax.bitwise_xor(me, m) * rows, 16), rows)
            chunk = slice(m * width, (m + 1) * width)
            own_key = kv_pieces[m][:, g * HD : (g + 1) * HD]
            dq = nn(kt_ref[...], ds_ref[:, chunk]) + tn(own_key, own_ds_ref[:, chunk])
            dq = (SCALE * dq).T.astype(jnp.bfloat16)
            for h in range(GROUP):
                column = (g * GROUP + h) * HD
                dq_ref[at, column : column + HD] = dq[h * rows : (h + 1) * rows]


def add_kernel(near_ref, far_ref, keep_ref, send_ref):
    total = near_ref[...] + far_ref[...].astype(jnp.float32)
    half = keep_ref.shape[0]
    keep_ref[...] = total[:half]
    send_ref[...] = total[half:].astype(send_ref.dtype)


def spread_kernel(parts_per_head, seg_ref, *refs):
    kv_heads, tokens = seg_ref.shape
    gk_ref, gv_ref = refs[-2:]
    for g in range(kv_heads):
        parts = refs[g * parts_per_head : (g + 1) * parts_per_head]
        total = parts[0][...].astype(jnp.float32)
        for part in parts[1:-1]:
            total = total + part[...].astype(jnp.float32)
        picks = slot_picks(seg_ref[g : g + 1, :], tokens).astype(jnp.float32)
        counts = jnp.sum(picks, axis=1, keepdims=True)
        total = total / jnp.maximum(counts, 1.0)
        high = total.astype(jnp.bfloat16)
        low = (total - high.astype(jnp.float32)).astype(jnp.bfloat16)
        picks = picks.astype(jnp.bfloat16)
        spread = tn(picks, high) + tn(picks, low) + parts[-1][...]
        gk_ref[:, g * HD : (g + 1) * HD] = spread[:, 0:HD].astype(jnp.bfloat16)
        gv_ref[:, g * HD : (g + 1) * HD] = spread[:, HD : 2 * HD].astype(jnp.bfloat16)


def in_vmem(count):
    return [pl.BlockSpec(memory_space=pltpu.VMEM)] * count


def anywhere(count):
    return [pl.BlockSpec(memory_space=pl.ANY)] * count


def params(mib):
    return pltpu.CompilerParams(vmem_limit_bytes=mib * 2**20)


def shape(*dims, dtype=jnp.bfloat16):
    return jax.ShapeDtypeStruct(dims, dtype)


def swap(x, axis, size, m):
    return lax.ppermute(x, axis, [(i, i ^ m) for i in range(size)])


def gate(value, after, mib=0):
    return pl.pallas_call(
        gate_kernel,
        out_shape=shape(*value.shape, dtype=value.dtype),
        in_specs=anywhere(1 + len(after)),
        out_specs=anywhere(1)[0],
        input_output_aliases={0: 0},
        compiler_params=params(1),
        cost_estimate=pl.CostEstimate(flops=0, bytes_accessed=mib * 2**20, transcendentals=0),
        name="gate",
    )(value, *after)


def bit_reversed(count):
    if count == 1:
        return [0]
    half = [2 * i for i in bit_reversed(count // 2)]
    return half + [i + 1 for i in half]


def local(queries, keys, values, segment_ids, grad_out):
    rows = queries.shape[0]
    heads = lax.axis_size("head")
    tokens = rows * heads
    kv_heads = KVH // heads
    shards = lax.axis_size("ctx")
    order = bit_reversed(shards)
    half = SLOT_DEV * shards // 2
    slots = SLOT_DEV * shards
    kv_width = kv_heads * HD

    def kv_at(m):
        return (m, kv_width, 0)

    def qo_at(m, g):
        return (m, kv_heads * GW, g * GW)

    def pack(jobs, sources, after, mib, name):
        outs = [pieces for _, dests in jobs for pieces in dests]
        return pl.pallas_call(
            functools.partial(pack_kernel, jobs),
            out_shape=[
                shape(len(pieces) * rows, 2 * width) for width, dests in jobs for pieces in dests
            ],
            in_specs=anywhere(2 + len(after)),
            out_specs=anywhere(len(outs)),
            scratch_shapes=[
                pltpu.SemaphoreType.DMA((2 * sum(len(p) for _, dests in jobs for p in dests),))
            ],
            compiler_params=params(mib),
            name=name,
        )(*sources, *after)

    kv_out = pl.pallas_call(
        functools.partial(pack_kv_kernel, kv_heads),
        out_shape=[shape(rows, 2 * kv_width)] * heads,
        in_specs=in_vmem(2),
        out_specs=in_vmem(heads),
        compiler_params=params(2),
        name="pack_kv",
    )(keys, values)
    kv = [kv_out[0]] + [swap(kv_out[m], "head", heads, m) for m in range(1, heads)]

    jobs = [(GW, [[qo_at(m, g) for g in range(kv_heads)] for m in range(1, heads)])]
    packed = pack(jobs, (queries, grad_out), kv_out[:1], 4, "pack_qo")
    handed = swap(gate(packed[2], kv[1:]), "head", heads, 1)
    from_across = swap(gate(packed[1], kv[1:]), "head", heads, 2)
    from_corner = swap(handed, "head", heads, 2)

    merged, hide = pl.pallas_call(
        functools.partial(merge_kernel, heads),
        out_shape=[shape(SLOT_DEV, 2 * kv_width), shape(kv_heads, tokens, HD)],
        in_specs=in_vmem(1 + heads),
        out_specs=in_vmem(2),
        scratch_shapes=[pltpu.VMEM((tokens, 2 * kv_width), jnp.bfloat16)],
        compiler_params=params(4),
        name="merge",
    )(segment_ids, *kv)

    held = {0: merged}
    for m in range(1, shards):
        low = m & -m
        held[m] = swap(held[m - low], "ctx", shards, low)
    late = [held[m] for m in range(1, shards - 1)] + [from_across]
    from_core = swap(gate(packed[0], late), "head", heads, 1)
    from_corner = gate(from_corner, (), 40)
    qo = (from_core, from_across, from_corner)

    all_rows = tokens * GROUP
    saved = []
    for g in range(kv_heads):
        outs = pl.pallas_call(
            functools.partial(attend_kernel, g, order),
            out_shape=[
                shape(slots, all_rows),
                shape(slots, all_rows),
                shape(rows, all_rows),
                shape(rows, all_rows),
                shape(all_rows, HD),
                shape(all_rows, HD),
                shape(HD, slots),
                shape(half, 2 * HD),
            ],
            in_specs=anywhere(2) + in_vmem(heads + heads + shards) + anywhere(g > 0),
            out_specs=in_vmem(8),
            scratch_shapes=[
                pltpu.VMEM((slots + rows, 2 * HD), jnp.bfloat16),
                pltpu.VMEM((slots + rows, HD), jnp.bfloat16),
                pltpu.VMEM((rows, 2 * GW), jnp.bfloat16),
                pltpu.VMEM((2, slots + rows, GROUP * rows), jnp.float32),
                pltpu.VMEM((2, slots + rows, GROUP * rows), jnp.float32),
                pltpu.SemaphoreType.DMA((2,)),
            ],
            compiler_params=params(24),
            cost_estimate=pl.CostEstimate(
                flops=6 * all_rows * (slots + rows) * HD,
                bytes_accessed=8 * 2**20,
                transcendentals=all_rows * slots,
            ),
            name="attend",
        )(
            queries,
            grad_out,
            hide,
            *kv,
            *[held[m] for m in order],
            *qo,
            *([saved[-1][2]] if g else []),
        )
        saved.append(outs)
    far = [swap(outs[7], "ctx", shards, 1) for outs in saved]
    near = []
    own = []
    for g in range(kv_heads):
        outs = pl.pallas_call(
            functools.partial(terms_kernel, heads),
            out_shape=[
                shape(half, 2 * HD, dtype=jnp.float32),
                shape(tokens, 2 * HD, dtype=jnp.float32),
            ],
            in_specs=in_vmem(6) + anywhere(1),
            out_specs=in_vmem(2),
            compiler_params=params(16),
            cost_estimate=pl.CostEstimate(
                flops=2 * all_rows * slots * HD, bytes_accessed=2**20, transcendentals=0
            ),
            name="terms",
        )(*saved[g][:6], saved[-1][2])
        near.append(outs[0])
        own.append(outs[1])
    dq = pl.pallas_call(
        functools.partial(queries_kernel, heads),
        out_shape=shape(tokens, kv_heads * GW),
        in_specs=in_vmem(heads + 3 * kv_heads),
        out_specs=in_vmem(1)[0],
        compiler_params=params(16),
        cost_estimate=pl.CostEstimate(
            flops=2 * kv_heads * all_rows * slots * HD, bytes_accessed=2**20, transcendentals=0
        ),
        name="queries",
    )(*kv, *[x for outs in saved for x in (outs[1], outs[3], outs[6])])

    spread_args = []
    for g in range(kv_heads):
        keep, received, step = near[g], far[g], 2
        while step < shards:
            count = keep.shape[0] // 2
            keep, send = pl.pallas_call(
                add_kernel,
                out_shape=[shape(count, 2 * HD, dtype=jnp.float32), shape(count, 2 * HD)],
                in_specs=in_vmem(2),
                out_specs=in_vmem(2),
                compiler_params=params(8),
                name="add",
            )(keep, received)
            received = swap(send, "ctx", shards, step)
            step *= 2
        spread_args += [keep, received, own[g]]

    grad_keys, grad_values = pl.pallas_call(
        functools.partial(spread_kernel, 3),
        out_shape=[shape(tokens, kv_width)] * 2,
        in_specs=in_vmem(1 + len(spread_args)),
        out_specs=in_vmem(2),
        compiler_params=params(12),
        name="spread",
    )(segment_ids, *spread_args)
    return dq, grad_keys, grad_values


def solution(mesh):
    return jax.shard_map(
        local,
        mesh=mesh,
        in_specs=(
            P(("ctx", "head"), None),
            P(("ctx", "head"), None),
            P(("ctx", "head"), None),
            P("head", "ctx"),
            P(("ctx", "head"), None),
        ),
        out_specs=(P("ctx", "head"), P("ctx", "head"), P("ctx", "head")),
        check_vma=False,
    )
```

```python
import functools

import jax
import jax.numpy as jnp
from jax import lax
from jax.experimental import pallas as pl
from jax.experimental.pallas import tpu as pltpu
from jax.sharding import PartitionSpec as P

QH = 64
KVH = 8
HD = 128
SLOT_DEV = 96
GROUP = QH // KVH
GW = GROUP * HD
SCALE = HD ** (-0.5)
LOG2E = 1.4426950408889634
DEAD = 1024.0
HIDDEN = 2.0**96


def nt(a, b):
    return lax.dot_general(a, b, (((1,), (1,)), ((), ())), preferred_element_type=jnp.float32)


def nn(a, b):
    return lax.dot_general(a, b, (((1,), (0,)), ((), ())), preferred_element_type=jnp.float32)


def tn(a, b):
    return lax.dot_general(a, b, (((0,), (0,)), ((), ())), preferred_element_type=jnp.float32)


def slot_picks(seg_row, tokens):
    return lax.broadcasted_iota(jnp.int32, (SLOT_DEV, tokens), 0) == seg_row


def place():
    return lax.axis_index("ctx"), lax.axis_index("head")


def lanes(start, size):
    return pl.ds(pl.multiple_of(start, HD), size)


def run_copies(copies):
    for copy in copies:
        copy.start()
    return copies


def wait_copies(copies):
    for copy in copies:
        copy.wait()


def pack_kernel(jobs, *refs):
    outs = [out for _, dests in jobs for out in dests]
    sources, out_refs, sems = refs[:2], refs[-len(outs) - 1 : -1], refs[-1]
    me = place()[1]
    copies = []
    done = 0
    for width, dests in jobs:
        for out, pieces in zip(out_refs[done:], dests):
            for at, (m, scale, offset) in enumerate(pieces):
                start = lax.bitwise_xor(me, m) * scale + offset
                for part, source in enumerate(sources):
                    rows = source.shape[0]
                    copies.append(
                        pltpu.make_async_copy(
                            source.at[:, lanes(start, width)],
                            out.at[at * rows : (at + 1) * rows, part * width : (part + 1) * width],
                            sems.at[len(copies)],
                        )
                    )
        done += len(dests)
    wait_copies(run_copies(copies))


def gate_kernel(*refs):
    pass


def pack_kv_kernel(kv_heads, key_ref, value_ref, *outs):
    me = place()[1]
    width = kv_heads * HD
    for m, out in enumerate(outs):
        start = lax.bitwise_xor(me, m) * width
        out[:, 0:width] = key_ref[:, lanes(start, width)]
        out[:, width : 2 * width] = value_ref[:, lanes(start, width)]


def merge_kernel(heads, seg_ref, *refs):
    pieces, (out, hide_ref, whole) = refs[:heads], refs[-3:]
    kv_heads, tokens = seg_ref.shape
    rows = tokens // heads
    me = place()[1]
    for m, piece in enumerate(pieces):
        start = pl.multiple_of(lax.bitwise_xor(me, m) * rows, 16)
        whole[pl.ds(start, rows), :] = piece[...]
    for g in range(kv_heads):
        picks = slot_picks(seg_ref[g : g + 1, :], tokens).astype(jnp.float32)
        counts = jnp.sum(picks, axis=1, keepdims=True)
        low_picks = picks.astype(jnp.bfloat16)
        sizes = jnp.maximum(counts, 1.0)
        for part in range(2):
            at = slice((part * kv_heads + g) * HD, (part * kv_heads + g + 1) * HD)
            rows_out = nn(low_picks, whole[:, at]) / sizes
            if part == 0:
                rows_out = jnp.where(counts == 0.0, DEAD, rows_out)
            out[:, at] = rows_out.astype(jnp.bfloat16)
        padded = -(-tokens // HD) * HD
        place_in = lax.broadcasted_iota(jnp.int32, (HD, padded), 0)
        seg = jnp.concatenate([seg_ref[g : g + 1, :]] * 2, axis=1)[:, :padded]
        late = (place_in >= seg) & (place_in < SLOT_DEV)
        hide = jnp.where(late, -HIDDEN, jnp.where(place_in == SLOT_DEV, 1.0, 0.0))
        hide_ref[g] = hide.T[:tokens].astype(jnp.bfloat16)


def folded(x, reduce):
    return reduce(x.reshape(x.shape[0] // 8, 8, x.shape[1]), axis=0)


def attend_kernel(g, order, far_parts, q_ref, o_ref, hide_ref, *refs):
    shards = len(order)
    heads = 4
    kv_pieces, blocks, refs = refs[:heads], refs[heads : heads + shards], refs[heads + shards :]
    qo_pieces = refs[: heads - 1]
    p_ref, ds_ref, own_p_ref, own_ds_ref, qs_ref, os_ref, kt_ref = refs[-13 - far_parts :][:7]
    far_refs, (kx, vx, mine, s_ref, g_ref, sems) = refs[-6 - far_parts : -6], refs[-6:]
    rows = q_ref.shape[0]
    kv_heads = hide_ref.shape[0]
    slots = shards * SLOT_DEV
    shard, me = place()
    key_at = slice(g * HD, (g + 1) * HD)
    value_at = slice((kv_heads + g) * HD, (kv_heads + g + 1) * HD)
    start = (me * kv_heads + g) * GW
    copies = run_copies(
        [
            pltpu.make_async_copy(
                source.at[:, lanes(start, GW)], mine.at[:, part * GW : (part + 1) * GW], sems.at[part]
            )
            for part, source in enumerate((q_ref, o_ref))
        ]
    )

    lane = lax.broadcasted_iota(jnp.int32, (SLOT_DEV, HD), 1)
    row = lax.broadcasted_iota(jnp.int32, (SLOT_DEV, HD), 0)
    for r, (m, block) in enumerate(zip(order, blocks)):
        at = pl.ds(r * SLOT_DEV, SLOT_DEV)
        key = block[:, key_at].astype(jnp.float32)
        vx[at, :] = block[:, value_at]
        if m == 0:
            extra = jnp.where(lane == row, 1.0, 0.0)
        else:
            hide = (key[:, 0:1] > 100.0) | (lax.bitwise_xor(shard, m) > shard)
            extra = jnp.where(hide & (lane >= SLOT_DEV), -HIDDEN, 0.0)
        kx[at, 0:HD] = jnp.where(key > 100.0, 0.0, key).astype(jnp.bfloat16)
        kx[at, HD : 2 * HD] = extra.astype(jnp.bfloat16)
    kx[slots : slots + rows, HD : 2 * HD] = jnp.zeros((rows, HD), jnp.bfloat16)

    width = GROUP * rows
    eye_row = lax.broadcasted_iota(jnp.int32, (rows, width), 0)
    eye_lane = lax.broadcasted_iota(jnp.int32, (rows, width), 1)
    eye = eye_row == lax.rem(eye_lane, rows)
    factor = SCALE * LOG2E

    for m in list(range(1, heads)) + [0]:
        if m == 0:
            wait_copies(copies)
        qo, part = (qo_pieces[m - 1], g) if m else (mine, 0)
        span = slice(part * rows, (part + 1) * rows)
        at = pl.ds(pl.multiple_of(lax.bitwise_xor(me, m) * rows, 16), rows)
        chunk = slice(m * width, (m + 1) * width)
        kx[slots : slots + rows, 0:HD] = kv_pieces[m][:, key_at]
        vx[slots : slots + rows, :] = kv_pieces[m][:, value_at]
        q2 = jnp.concatenate([qo[span, h * HD : (h + 1) * HD] for h in range(GROUP)], axis=0)
        o2 = jnp.concatenate(
            [qo[span, GW + h * HD : GW + (h + 1) * HD] for h in range(GROUP)], axis=0
        )
        qs_ref[chunk, :] = q2
        os_ref[chunk, :] = o2
        qx = jnp.concatenate([q2, jnp.concatenate([hide_ref[g, at, :]] * GROUP, axis=0)], axis=1)
        s_at, g_at = s_ref.at[m % 2], g_ref.at[m % 2]
        s_at[...] = nt(kx[...], qx)
        g_at[...] = nt(vx[...], o2)
        own_score = jnp.sum(jnp.where(eye, s_at[slots:, :], 0.0), axis=0, keepdims=True)
        own_grad_prob = jnp.sum(jnp.where(eye, g_at[slots:, :], 0.0), axis=0, keepdims=True)
        parts = [slice(r * SLOT_DEV, (r + 1) * SLOT_DEV) for r in range(shards)]
        top = folded(functools.reduce(jnp.maximum, [s_at[part, :] for part in parts]), jnp.max)
        top = jnp.maximum(jnp.max(top, axis=0, keepdims=True), own_score)
        total = 0.0
        delta = 0.0
        for part in parts:
            weights = jnp.exp2((s_at[part, :] - top) * factor)
            total = total + folded(weights, jnp.sum)
            delta = delta + folded(weights * g_at[part, :], jnp.sum)
        own_weight = jnp.exp2((own_score - top) * factor)
        total = jnp.sum(total, axis=0, keepdims=True) + own_weight
        delta = jnp.sum(delta, axis=0, keepdims=True) + own_weight * own_grad_prob
        delta = delta / total
        own_prob = own_weight / total
        log_total = jnp.log2(total)
        for part in parts:
            probs = jnp.exp2((s_at[part, :] - top) * factor - log_total)
            p_ref[part, chunk] = probs.astype(jnp.bfloat16)
            ds_ref[part, chunk] = (probs * (g_at[part, :] - delta)).astype(jnp.bfloat16)
        own_grad_score = own_prob * (own_grad_prob - delta)
        own_p_ref[:, chunk] = jnp.where(eye, own_prob, 0.0).astype(jnp.bfloat16)
        own_ds_ref[:, chunk] = jnp.where(eye, own_grad_score, 0.0).astype(jnp.bfloat16)
    stop = slots
    for far_ref in far_refs:
        far = slice(stop - far_ref.shape[0], stop)
        far_ref[:, 0:HD] = (SCALE * nn(ds_ref[far, :], qs_ref[...])).astype(far_ref.dtype)
        far_ref[:, HD : 2 * HD] = nn(p_ref[far, :], os_ref[...]).astype(far_ref.dtype)
        stop = far.start
    kt_ref[...] = kx[0:slots, 0:HD].astype(jnp.float32).T.astype(jnp.bfloat16)


def terms_kernel(heads, p_ref, ds_ref, own_p_ref, own_ds_ref, qs_ref, os_ref, after_ref, near_ref, own_ref):
    rows = own_p_ref.shape[0]
    near = slice(0, near_ref.shape[0])
    near_ref[:, 0:HD] = SCALE * nn(ds_ref[near, :], qs_ref[...])
    near_ref[:, HD : 2 * HD] = nn(p_ref[near, :], os_ref[...])
    me = place()[1]
    width = GROUP * rows
    for m in range(heads):
        at = pl.ds(pl.multiple_of(lax.bitwise_xor(me, m) * rows, 16), rows)
        chunk = slice(m * width, (m + 1) * width)
        own_ref[at, 0:HD] = SCALE * nn(own_ds_ref[:, chunk], qs_ref[chunk, :])
        own_ref[at, HD : 2 * HD] = nn(own_p_ref[:, chunk], os_ref[chunk, :])


def queries_kernel(heads, *refs):
    kv_pieces, refs, dq_ref = refs[:heads], refs[heads:-1], refs[-1]
    me = place()[1]
    for g in range(len(refs) // 3):
        ds_ref, own_ds_ref, kt_ref = refs[3 * g : 3 * g + 3]
        rows = own_ds_ref.shape[0]
        width = GROUP * rows
        for m in range(heads):
            at = pl.ds(pl.multiple_of(lax.bitwise_xor(me, m) * rows, 16), rows)
            chunk = slice(m * width, (m + 1) * width)
            own_key = kv_pieces[m][:, g * HD : (g + 1) * HD]
            dq = nn(kt_ref[...], ds_ref[:, chunk]) + tn(own_key, own_ds_ref[:, chunk])
            dq = (SCALE * dq).T.astype(jnp.bfloat16)
            for h in range(GROUP):
                column = (g * GROUP + h) * HD
                dq_ref[at, column : column + HD] = dq[h * rows : (h + 1) * rows]


def add_kernel(starts, *refs):
    out = refs[-1]
    rows = out.shape[0]
    total = 0.0
    for start, ref in zip(starts, refs[:-1]):
        total = total + ref[start : start + rows, :].astype(jnp.float32)
    out[...] = total.astype(out.dtype)


def spread_kernel(parts_per_head, seg_ref, *refs):
    kv_heads, tokens = seg_ref.shape
    gk_ref, gv_ref = refs[-2:]
    for g in range(kv_heads):
        parts = refs[g * parts_per_head : (g + 1) * parts_per_head]
        total = 0.0
        for part in parts[:-1]:
            total = total + part[0:SLOT_DEV, :].astype(jnp.float32)
        picks = slot_picks(seg_ref[g : g + 1, :], tokens).astype(jnp.float32)
        counts = jnp.sum(picks, axis=1, keepdims=True)
        total = total / jnp.maximum(counts, 1.0)
        high = total.astype(jnp.bfloat16)
        low = (total - high.astype(jnp.float32)).astype(jnp.bfloat16)
        picks = picks.astype(jnp.bfloat16)
        spread = tn(picks, high) + tn(picks, low) + parts[-1][...]
        gk_ref[:, g * HD : (g + 1) * HD] = spread[:, 0:HD].astype(jnp.bfloat16)
        gv_ref[:, g * HD : (g + 1) * HD] = spread[:, HD : 2 * HD].astype(jnp.bfloat16)


def in_vmem(count):
    return [pl.BlockSpec(memory_space=pltpu.VMEM)] * count


def anywhere(count):
    return [pl.BlockSpec(memory_space=pl.ANY)] * count


def params(mib):
    return pltpu.CompilerParams(vmem_limit_bytes=mib * 2**20)


def shape(*dims, dtype=jnp.bfloat16):
    return jax.ShapeDtypeStruct(dims, dtype)


def swap(x, axis, size, m):
    return lax.ppermute(x, axis, [(i, i ^ m) for i in range(size)])


def gate(value, after, mib=0):
    return pl.pallas_call(
        gate_kernel,
        out_shape=shape(*value.shape, dtype=value.dtype),
        in_specs=anywhere(1 + len(after)),
        out_specs=anywhere(1)[0],
        input_output_aliases={0: 0},
        compiler_params=params(1),
        cost_estimate=pl.CostEstimate(flops=0, bytes_accessed=mib * 2**20, transcendentals=0),
        name="gate",
    )(value, *after)


def bit_reversed(count):
    if count == 1:
        return [0]
    half = [2 * i for i in bit_reversed(count // 2)]
    return half + [i + 1 for i in half]


def local(queries, keys, values, segment_ids, grad_out):
    rows = queries.shape[0]
    heads = lax.axis_size("head")
    tokens = rows * heads
    kv_heads = KVH // heads
    shards = lax.axis_size("ctx")
    order = bit_reversed(shards)
    half = SLOT_DEV * shards // 2
    slots = SLOT_DEV * shards
    kv_width = kv_heads * HD

    def kv_at(m):
        return (m, kv_width, 0)

    def qo_at(m, g):
        return (m, kv_heads * GW, g * GW)

    def pack(jobs, sources, after, mib, name):
        outs = [pieces for _, dests in jobs for pieces in dests]
        return pl.pallas_call(
            functools.partial(pack_kernel, jobs),
            out_shape=[
                shape(len(pieces) * rows, 2 * width) for width, dests in jobs for pieces in dests
            ],
            in_specs=anywhere(2 + len(after)),
            out_specs=anywhere(len(outs)),
            scratch_shapes=[
                pltpu.SemaphoreType.DMA((2 * sum(len(p) for _, dests in jobs for p in dests),))
            ],
            compiler_params=params(mib),
            name=name,
        )(*sources, *after)

    kv_out = pl.pallas_call(
        functools.partial(pack_kv_kernel, kv_heads),
        out_shape=[shape(rows, 2 * kv_width)] * heads,
        in_specs=in_vmem(2),
        out_specs=in_vmem(heads),
        compiler_params=params(2),
        name="pack_kv",
    )(keys, values)
    kv = [kv_out[0]] + [swap(kv_out[m], "head", heads, m) for m in range(1, heads)]

    jobs = [(GW, [[qo_at(m, g) for g in range(kv_heads)] for m in range(1, heads)])]
    packed = pack(jobs, (queries, grad_out), kv_out[:1], 4, "pack_qo")
    handed = swap(gate(packed[2], kv[1:]), "head", heads, 1)
    from_across = swap(gate(packed[1], kv[1:]), "head", heads, 2)
    from_corner = swap(handed, "head", heads, 2)

    merged, hide = pl.pallas_call(
        functools.partial(merge_kernel, heads),
        out_shape=[shape(SLOT_DEV, 2 * kv_width), shape(kv_heads, tokens, HD)],
        in_specs=in_vmem(1 + heads),
        out_specs=in_vmem(2),
        scratch_shapes=[pltpu.VMEM((tokens, 2 * kv_width), jnp.bfloat16)],
        compiler_params=params(4),
        name="merge",
    )(segment_ids, *kv)

    held = {0: merged}
    for m in range(1, shards):
        low = m & -m
        held[m] = swap(held[m - low], "ctx", shards, low)
    late = [held[m] for m in range(1, shards - 1)] + [from_across]
    from_core = swap(gate(packed[0], late), "head", heads, 1)
    from_corner = gate(from_corner, (), 40)
    qo = (from_core, from_across, from_corner)

    all_rows = tokens * GROUP
    saved = []
    for g in range(kv_heads):
        far_parts = 2 if g == kv_heads - 1 else 1
        outs = pl.pallas_call(
            functools.partial(attend_kernel, g, order, far_parts),
            out_shape=[
                shape(slots, all_rows),
                shape(slots, all_rows),
                shape(rows, all_rows),
                shape(rows, all_rows),
                shape(all_rows, HD),
                shape(all_rows, HD),
                shape(HD, slots),
            ]
            + [shape(half // far_parts, 2 * HD)] * far_parts,
            in_specs=anywhere(2) + in_vmem(heads + heads + shards) + anywhere(g > 0),
            out_specs=in_vmem(7 + far_parts),
            scratch_shapes=[
                pltpu.VMEM((slots + rows, 2 * HD), jnp.bfloat16),
                pltpu.VMEM((slots + rows, HD), jnp.bfloat16),
                pltpu.VMEM((rows, 2 * GW), jnp.bfloat16),
                pltpu.VMEM((2, slots + rows, GROUP * rows), jnp.float32),
                pltpu.VMEM((2, slots + rows, GROUP * rows), jnp.float32),
                pltpu.SemaphoreType.DMA((2,)),
            ],
            compiler_params=params(24),
            cost_estimate=pl.CostEstimate(
                flops=6 * all_rows * (slots + rows) * HD,
                bytes_accessed=8 * 2**20,
                transcendentals=all_rows * slots,
            ),
            name="attend",
        )(
            queries,
            grad_out,
            hide,
            *kv,
            *[held[m] for m in order],
            *qo,
            *([saved[-1][2]] if g else []),
        )
        saved.append(outs)
    far = [[swap(part, "ctx", shards, 1) for part in outs[7:]] for outs in saved]
    near = []
    own = []
    for g in range(kv_heads):
        outs = pl.pallas_call(
            functools.partial(terms_kernel, heads),
            out_shape=[
                shape(half, 2 * HD, dtype=jnp.float32),
                shape(tokens, 2 * HD, dtype=jnp.float32),
            ],
            in_specs=in_vmem(6) + anywhere(1),
            out_specs=in_vmem(2),
            compiler_params=params(16),
            cost_estimate=pl.CostEstimate(
                flops=2 * all_rows * slots * HD, bytes_accessed=2**20, transcendentals=0
            ),
            name="terms",
        )(*saved[g][:6], saved[-1][2])
        near.append(outs[0])
        own.append(outs[1])
    dq = pl.pallas_call(
        functools.partial(queries_kernel, heads),
        out_shape=shape(tokens, kv_heads * GW),
        in_specs=in_vmem(heads + 3 * kv_heads),
        out_specs=in_vmem(1)[0],
        compiler_params=params(16),
        cost_estimate=pl.CostEstimate(
            flops=2 * kv_heads * all_rows * slots * HD, bytes_accessed=2**20, transcendentals=0
        ),
        name="queries",
    )(*kv, *[x for outs in saved for x in (outs[1], outs[3], outs[6])])

    spread_args = []
    for g in range(kv_heads):
        rows_left, step = half // 2, 2
        first, rest = far[g][0], far[g][-1]
        terms = [(near[g], rows_left), (first, rows_left % first.shape[0])]
        kept = [near[g], rest]
        while step < shards:
            send = pl.pallas_call(
                functools.partial(add_kernel, [start for _, start in terms]),
                out_shape=shape(rows_left, 2 * HD),
                in_specs=in_vmem(len(terms)),
                out_specs=in_vmem(1)[0],
                compiler_params=params(8),
                name="add",
            )(*[term for term, _ in terms])
            kept.append(swap(send, "ctx", shards, step))
            rows_left //= 2
            step *= 2
            terms = [(term, rows_left) for term in kept]
        spread_args += kept + [own[g]]
    parts_per_head = len(spread_args) // kv_heads

    grad_keys, grad_values = pl.pallas_call(
        functools.partial(spread_kernel, parts_per_head),
        out_shape=[shape(tokens, kv_width)] * 2,
        in_specs=in_vmem(1 + len(spread_args)),
        out_specs=in_vmem(2),
        compiler_params=params(12),
        name="spread",
    )(segment_ids, *spread_args)
    return dq, grad_keys, grad_values


def solution(mesh):
    return jax.shard_map(
        local,
        mesh=mesh,
        in_specs=(
            P(("ctx", "head"), None),
            P(("ctx", "head"), None),
            P(("ctx", "head"), None),
            P("head", "ctx"),
            P(("ctx", "head"), None),
        ),
        out_specs=(P("ctx", "head"), P("ctx", "head"), P("ctx", "head")),
        check_vma=False,
    )
```

```python
import functools

import jax
import jax.numpy as jnp
from jax import lax
from jax.experimental import pallas as pl
from jax.experimental.pallas import tpu as pltpu
from jax.sharding import PartitionSpec as P

QH = 64
KVH = 8
HD = 128
SLOT_DEV = 96
GROUP = QH // KVH
GW = GROUP * HD
SCALE = HD ** (-0.5)
LOG2E = 1.4426950408889634
DEAD = 1024.0
HIDDEN = 2.0**96


def nt(a, b):
    return lax.dot_general(a, b, (((1,), (1,)), ((), ())), preferred_element_type=jnp.float32)


def nn(a, b):
    return lax.dot_general(a, b, (((1,), (0,)), ((), ())), preferred_element_type=jnp.float32)


def tn(a, b):
    return lax.dot_general(a, b, (((0,), (0,)), ((), ())), preferred_element_type=jnp.float32)


def slot_picks(seg_row, tokens):
    return lax.broadcasted_iota(jnp.int32, (SLOT_DEV, tokens), 0) == seg_row


def place():
    return lax.axis_index("ctx"), lax.axis_index("head")


def lanes(start, size):
    return pl.ds(pl.multiple_of(start, HD), size)


def run_copies(copies):
    for copy in copies:
        copy.start()
    return copies


def wait_copies(copies):
    for copy in copies:
        copy.wait()


def pack_kernel(jobs, *refs):
    outs = [out for _, dests in jobs for out in dests]
    sources, out_refs, sems = refs[:2], refs[-len(outs) - 1 : -1], refs[-1]
    me = place()[1]
    copies = []
    done = 0
    for width, dests in jobs:
        for out, pieces in zip(out_refs[done:], dests):
            for at, (m, scale, offset) in enumerate(pieces):
                start = lax.bitwise_xor(me, m) * scale + offset
                for part, source in enumerate(sources):
                    rows = source.shape[0]
                    copies.append(
                        pltpu.make_async_copy(
                            source.at[:, lanes(start, width)],
                            out.at[at * rows : (at + 1) * rows, part * width : (part + 1) * width],
                            sems.at[len(copies)],
                        )
                    )
        done += len(dests)
    wait_copies(run_copies(copies))


def gate_kernel(*refs):
    pass


def pack_kv_kernel(kv_heads, key_ref, value_ref, *outs):
    me = place()[1]
    width = kv_heads * HD
    for m, out in enumerate(outs):
        start = lax.bitwise_xor(me, m) * width
        out[:, 0:width] = key_ref[:, lanes(start, width)]
        out[:, width : 2 * width] = value_ref[:, lanes(start, width)]


def merge_kernel(heads, seg_ref, *refs):
    pieces, (out, hide_ref, whole) = refs[:heads], refs[-3:]
    kv_heads, tokens = seg_ref.shape
    rows = tokens // heads
    me = place()[1]
    for m, piece in enumerate(pieces):
        start = pl.multiple_of(lax.bitwise_xor(me, m) * rows, 16)
        whole[pl.ds(start, rows), :] = piece[...]
    for g in range(kv_heads):
        picks = slot_picks(seg_ref[g : g + 1, :], tokens).astype(jnp.float32)
        counts = jnp.sum(picks, axis=1, keepdims=True)
        low_picks = picks.astype(jnp.bfloat16)
        sizes = jnp.maximum(counts, 1.0)
        for part in range(2):
            at = slice((part * kv_heads + g) * HD, (part * kv_heads + g + 1) * HD)
            rows_out = nn(low_picks, whole[:, at]) / sizes
            if part == 0:
                rows_out = jnp.where(counts == 0.0, DEAD, rows_out)
            out[:, at] = rows_out.astype(jnp.bfloat16)
        padded = -(-tokens // HD) * HD
        place_in = lax.broadcasted_iota(jnp.int32, (HD, padded), 0)
        seg = jnp.concatenate([seg_ref[g : g + 1, :]] * 2, axis=1)[:, :padded]
        late = (place_in >= seg) & (place_in < SLOT_DEV)
        hide = jnp.where(late, -HIDDEN, jnp.where(place_in == SLOT_DEV, 1.0, 0.0))
        hide_ref[g] = hide.T[:tokens].astype(jnp.bfloat16)


def folded(x, reduce):
    return reduce(x.reshape(x.shape[0] // 8, 8, x.shape[1]), axis=0)


def attend_kernel(g, order, far_parts, q_ref, o_ref, hide_ref, *refs):
    shards = len(order)
    heads = 4
    kv_pieces, blocks, refs = refs[:heads], refs[heads : heads + shards], refs[heads + shards :]
    qo_pieces = refs[: heads - 1]
    p_ref, ds_ref, own_p_ref, own_ds_ref, qs_ref, os_ref, kt_ref = refs[-13 - far_parts :][:7]
    far_refs, (kx, vx, mine, s_ref, g_ref, sems) = refs[-6 - far_parts : -6], refs[-6:]
    rows = q_ref.shape[0]
    kv_heads = hide_ref.shape[0]
    slots = shards * SLOT_DEV
    shard, me = place()
    key_at = slice(g * HD, (g + 1) * HD)
    value_at = slice((kv_heads + g) * HD, (kv_heads + g + 1) * HD)
    start = (me * kv_heads + g) * GW
    copies = run_copies(
        [
            pltpu.make_async_copy(
                source.at[:, lanes(start, GW)], mine.at[:, part * GW : (part + 1) * GW], sems.at[part]
            )
            for part, source in enumerate((q_ref, o_ref))
        ]
    )

    lane = lax.broadcasted_iota(jnp.int32, (SLOT_DEV, HD), 1)
    row = lax.broadcasted_iota(jnp.int32, (SLOT_DEV, HD), 0)
    for r, (m, block) in enumerate(zip(order, blocks)):
        at = pl.ds(r * SLOT_DEV, SLOT_DEV)
        key = block[:, key_at].astype(jnp.float32)
        vx[at, :] = block[:, value_at]
        if m == 0:
            extra = jnp.where(lane == row, 1.0, 0.0)
        else:
            hide = (key[:, 0:1] > 100.0) | (lax.bitwise_xor(shard, m) > shard)
            extra = jnp.where(hide & (lane >= SLOT_DEV), -HIDDEN, 0.0)
        kx[at, 0:HD] = jnp.where(key > 100.0, 0.0, key).astype(jnp.bfloat16)
        kx[at, HD : 2 * HD] = extra.astype(jnp.bfloat16)
    kx[slots : slots + rows, HD : 2 * HD] = jnp.zeros((rows, HD), jnp.bfloat16)

    width = GROUP * rows
    eye_row = lax.broadcasted_iota(jnp.int32, (rows, width), 0)
    eye_lane = lax.broadcasted_iota(jnp.int32, (rows, width), 1)
    eye = eye_row == lax.rem(eye_lane, rows)
    factor = SCALE * LOG2E

    for m in list(range(1, heads)) + [0]:
        if m == 0:
            wait_copies(copies)
        qo, part = (qo_pieces[m - 1], g) if m else (mine, 0)
        span = slice(part * rows, (part + 1) * rows)
        at = pl.ds(pl.multiple_of(lax.bitwise_xor(me, m) * rows, 16), rows)
        chunk = slice(m * width, (m + 1) * width)
        kx[slots : slots + rows, 0:HD] = kv_pieces[m][:, key_at]
        vx[slots : slots + rows, :] = kv_pieces[m][:, value_at]
        q2 = jnp.concatenate([qo[span, h * HD : (h + 1) * HD] for h in range(GROUP)], axis=0)
        o2 = jnp.concatenate(
            [qo[span, GW + h * HD : GW + (h + 1) * HD] for h in range(GROUP)], axis=0
        )
        qs_ref[chunk, :] = q2
        os_ref[chunk, :] = o2
        qx = jnp.concatenate([q2, jnp.concatenate([hide_ref[g, at, :]] * GROUP, axis=0)], axis=1)
        s_at, g_at = s_ref.at[m % 2], g_ref.at[m % 2]
        s_at[...] = nt(kx[...], qx)
        g_at[...] = nt(vx[...], o2)
        own_score = jnp.sum(jnp.where(eye, s_at[slots:, :], 0.0), axis=0, keepdims=True)
        own_grad_prob = jnp.sum(jnp.where(eye, g_at[slots:, :], 0.0), axis=0, keepdims=True)
        parts = [slice(r * SLOT_DEV, (r + 1) * SLOT_DEV) for r in range(shards)]
        top = folded(functools.reduce(jnp.maximum, [s_at[part, :] for part in parts]), jnp.max)
        top = jnp.maximum(jnp.max(top, axis=0, keepdims=True), own_score)
        total = 0.0
        delta = 0.0
        for part in parts:
            weights = jnp.exp2((s_at[part, :] - top) * factor)
            total = total + folded(weights, jnp.sum)
            delta = delta + folded(weights * g_at[part, :], jnp.sum)
        own_weight = jnp.exp2((own_score - top) * factor)
        total = jnp.sum(total, axis=0, keepdims=True) + own_weight
        delta = jnp.sum(delta, axis=0, keepdims=True) + own_weight * own_grad_prob
        delta = delta / total
        own_prob = own_weight / total
        log_total = jnp.log2(total)
        for part in parts:
            probs = jnp.exp2((s_at[part, :] - top) * factor - log_total)
            p_ref[part, chunk] = probs.astype(jnp.bfloat16)
            ds_ref[part, chunk] = (probs * (g_at[part, :] - delta)).astype(jnp.bfloat16)
        own_grad_score = own_prob * (own_grad_prob - delta)
        own_p_ref[:, chunk] = jnp.where(eye, own_prob, 0.0).astype(jnp.bfloat16)
        own_ds_ref[:, chunk] = jnp.where(eye, own_grad_score, 0.0).astype(jnp.bfloat16)
    stop = slots
    for far_ref in far_refs:
        far = slice(stop - far_ref.shape[0], stop)
        far_ref[:, 0:HD] = (SCALE * nn(ds_ref[far, :], qs_ref[...])).astype(far_ref.dtype)
        far_ref[:, HD : 2 * HD] = nn(p_ref[far, :], os_ref[...]).astype(far_ref.dtype)
        stop = far.start
    kt_ref[...] = kx[0:slots, 0:HD].astype(jnp.float32).T.astype(jnp.bfloat16)


def terms_kernel(heads, p_ref, ds_ref, own_p_ref, own_ds_ref, qs_ref, os_ref, after_ref, near_ref, own_ref):
    rows = own_p_ref.shape[0]
    near = slice(0, near_ref.shape[0])
    near_ref[:, 0:HD] = SCALE * nn(ds_ref[near, :], qs_ref[...])
    near_ref[:, HD : 2 * HD] = nn(p_ref[near, :], os_ref[...])
    me = place()[1]
    width = GROUP * rows
    for m in range(heads):
        at = pl.ds(pl.multiple_of(lax.bitwise_xor(me, m) * rows, 16), rows)
        chunk = slice(m * width, (m + 1) * width)
        own_ref[at, 0:HD] = SCALE * nn(own_ds_ref[:, chunk], qs_ref[chunk, :])
        own_ref[at, HD : 2 * HD] = nn(own_p_ref[:, chunk], os_ref[chunk, :])


def queries_kernel(heads, *refs):
    kv_pieces, refs, dq_ref = refs[:heads], refs[heads:-1], refs[-1]
    me = place()[1]
    for g in range(len(refs) // 3):
        ds_ref, own_ds_ref, kt_ref = refs[3 * g : 3 * g + 3]
        rows = own_ds_ref.shape[0]
        width = GROUP * rows
        for m in range(heads):
            at = pl.ds(pl.multiple_of(lax.bitwise_xor(me, m) * rows, 16), rows)
            chunk = slice(m * width, (m + 1) * width)
            own_key = kv_pieces[m][:, g * HD : (g + 1) * HD]
            dq = nn(kt_ref[...], ds_ref[:, chunk]) + tn(own_key, own_ds_ref[:, chunk])
            dq = (SCALE * dq).T.astype(jnp.bfloat16)
            for h in range(GROUP):
                column = (g * GROUP + h) * HD
                dq_ref[at, column : column + HD] = dq[h * rows : (h + 1) * rows]


def add_kernel(starts, *refs):
    out = refs[-1]
    rows = out.shape[0]
    total = 0.0
    for start, ref in zip(starts, refs[:-1]):
        total = total + ref[start : start + rows, :].astype(jnp.float32)
    out[...] = total.astype(out.dtype)


def spread_kernel(parts_per_head, seg_ref, *refs):
    kv_heads, tokens = seg_ref.shape
    gk_ref, gv_ref = refs[-2:]
    for g in range(kv_heads):
        parts = refs[g * parts_per_head : (g + 1) * parts_per_head]
        total = 0.0
        for part in parts[:-1]:
            total = total + part[0:SLOT_DEV, :].astype(jnp.float32)
        picks = slot_picks(seg_ref[g : g + 1, :], tokens).astype(jnp.float32)
        counts = jnp.sum(picks, axis=1, keepdims=True)
        total = total / jnp.maximum(counts, 1.0)
        high = total.astype(jnp.bfloat16)
        low = (total - high.astype(jnp.float32)).astype(jnp.bfloat16)
        picks = picks.astype(jnp.bfloat16)
        spread = tn(picks, high) + tn(picks, low) + parts[-1][...]
        gk_ref[:, g * HD : (g + 1) * HD] = spread[:, 0:HD].astype(jnp.bfloat16)
        gv_ref[:, g * HD : (g + 1) * HD] = spread[:, HD : 2 * HD].astype(jnp.bfloat16)


def in_vmem(count):
    return [pl.BlockSpec(memory_space=pltpu.VMEM)] * count


def anywhere(count):
    return [pl.BlockSpec(memory_space=pl.ANY)] * count


def params(mib):
    return pltpu.CompilerParams(vmem_limit_bytes=mib * 2**20)


def shape(*dims, dtype=jnp.bfloat16):
    return jax.ShapeDtypeStruct(dims, dtype)


def swap(x, axis, size, m):
    return lax.ppermute(x, axis, [(i, i ^ m) for i in range(size)])


def gate(value, after, mib=0):
    return pl.pallas_call(
        gate_kernel,
        out_shape=shape(*value.shape, dtype=value.dtype),
        in_specs=anywhere(1 + len(after)),
        out_specs=anywhere(1)[0],
        input_output_aliases={0: 0},
        compiler_params=params(1),
        cost_estimate=pl.CostEstimate(flops=0, bytes_accessed=mib * 2**20, transcendentals=0),
        name="gate",
    )(value, *after)


def bit_reversed(count):
    if count == 1:
        return [0]
    half = [2 * i for i in bit_reversed(count // 2)]
    return half + [i + 1 for i in half]


def local(queries, keys, values, segment_ids, grad_out):
    rows = queries.shape[0]
    heads = lax.axis_size("head")
    tokens = rows * heads
    kv_heads = KVH // heads
    shards = lax.axis_size("ctx")
    order = bit_reversed(shards)
    half = SLOT_DEV * shards // 2
    slots = SLOT_DEV * shards
    kv_width = kv_heads * HD

    def kv_at(m):
        return (m, kv_width, 0)

    def qo_at(m, g):
        return (m, kv_heads * GW, g * GW)

    def pack(jobs, sources, after, mib, name):
        outs = [pieces for _, dests in jobs for pieces in dests]
        return pl.pallas_call(
            functools.partial(pack_kernel, jobs),
            out_shape=[
                shape(len(pieces) * rows, 2 * width) for width, dests in jobs for pieces in dests
            ],
            in_specs=anywhere(2 + len(after)),
            out_specs=anywhere(len(outs)),
            scratch_shapes=[
                pltpu.SemaphoreType.DMA((2 * sum(len(p) for _, dests in jobs for p in dests),))
            ],
            compiler_params=params(mib),
            name=name,
        )(*sources, *after)

    kv_out = pl.pallas_call(
        functools.partial(pack_kv_kernel, kv_heads),
        out_shape=[shape(rows, 2 * kv_width)] * heads,
        in_specs=in_vmem(2),
        out_specs=in_vmem(heads),
        compiler_params=params(2),
        name="pack_kv",
    )(keys, values)
    kv = [kv_out[0]] + [swap(kv_out[m], "head", heads, m) for m in range(1, heads)]

    jobs = [(GW, [[qo_at(m, g) for g in range(kv_heads)] for m in range(1, heads)])]
    packed = pack(jobs, (queries, grad_out), kv_out[:1], 4, "pack_qo")
    handed = swap(gate(packed[2], kv[1:]), "head", heads, 1)
    from_across = swap(gate(packed[1], kv[1:]), "head", heads, 2)
    from_corner = swap(handed, "head", heads, 2)

    merged, hide = pl.pallas_call(
        functools.partial(merge_kernel, heads),
        out_shape=[shape(SLOT_DEV, 2 * kv_width), shape(kv_heads, tokens, HD)],
        in_specs=in_vmem(1 + heads),
        out_specs=in_vmem(2),
        scratch_shapes=[pltpu.VMEM((tokens, 2 * kv_width), jnp.bfloat16)],
        compiler_params=params(4),
        name="merge",
    )(segment_ids, *kv)

    held = {0: merged}
    for m in range(1, shards):
        low = m & -m
        held[m] = swap(held[m - low], "ctx", shards, low)
    late = [held[m] for m in range(1, shards - 1)] + [from_across]
    from_core = swap(gate(packed[0], late), "head", heads, 1)
    from_corner = gate(from_corner, (), 40)
    qo = (from_core, from_across, from_corner)

    all_rows = tokens * GROUP
    saved = []
    for g in range(kv_heads):
        far_parts = 2 if g == kv_heads - 1 else 1
        outs = pl.pallas_call(
            functools.partial(attend_kernel, g, order, far_parts),
            out_shape=[
                shape(slots, all_rows),
                shape(slots, all_rows),
                shape(rows, all_rows),
                shape(rows, all_rows),
                shape(all_rows, HD),
                shape(all_rows, HD),
                shape(HD, slots),
            ]
            + [shape(half // far_parts, 2 * HD)] * far_parts,
            in_specs=anywhere(2) + in_vmem(heads + heads + shards) + anywhere(g > 0),
            out_specs=in_vmem(7 + far_parts),
            scratch_shapes=[
                pltpu.VMEM((slots + rows, 2 * HD), jnp.bfloat16),
                pltpu.VMEM((slots + rows, HD), jnp.bfloat16),
                pltpu.VMEM((rows, 2 * GW), jnp.bfloat16),
                pltpu.VMEM((2, slots + rows, GROUP * rows), jnp.float32),
                pltpu.VMEM((2, slots + rows, GROUP * rows), jnp.float32),
                pltpu.SemaphoreType.DMA((2,)),
            ],
            compiler_params=params(24),
            cost_estimate=pl.CostEstimate(
                flops=6 * all_rows * (slots + rows) * HD,
                bytes_accessed=8 * 2**20,
                transcendentals=all_rows * slots,
            ),
            name="attend",
        )(
            queries,
            grad_out,
            hide,
            *kv,
            *[held[m] for m in order],
            *qo,
            *([saved[-1][2]] if g else []),
        )
        saved.append(outs)
    far = []
    for outs in saved:
        received = [swap(outs[7], "ctx", shards, 1)]
        for part in outs[8:]:
            received.append(swap(gate(part, received), "ctx", shards, 1))
        far.append(received)
    near = []
    own = []
    for g in range(kv_heads):
        outs = pl.pallas_call(
            functools.partial(terms_kernel, heads),
            out_shape=[
                shape(half, 2 * HD, dtype=jnp.float32),
                shape(tokens, 2 * HD, dtype=jnp.float32),
            ],
            in_specs=in_vmem(6) + anywhere(1),
            out_specs=in_vmem(2),
            compiler_params=params(16),
            cost_estimate=pl.CostEstimate(
                flops=2 * all_rows * slots * HD, bytes_accessed=2**20, transcendentals=0
            ),
            name="terms",
        )(*saved[g][:6], saved[-1][2])
        near.append(outs[0])
        own.append(outs[1])
    dq = pl.pallas_call(
        functools.partial(queries_kernel, heads),
        out_shape=shape(tokens, kv_heads * GW),
        in_specs=in_vmem(heads + 3 * kv_heads),
        out_specs=in_vmem(1)[0],
        compiler_params=params(16),
        cost_estimate=pl.CostEstimate(
            flops=2 * kv_heads * all_rows * slots * HD, bytes_accessed=2**20, transcendentals=0
        ),
        name="queries",
    )(*kv, *[x for outs in saved for x in (outs[1], outs[3], outs[6])])

    spread_args = []
    before = {}
    for g in range(kv_heads):
        rows_left, step = half // 2, 2
        first, rest = far[g][0], far[g][-1]
        terms = [(near[g], rows_left), (first, rows_left % first.shape[0])]
        kept = [near[g], rest]
        while step < shards:
            send = pl.pallas_call(
                functools.partial(add_kernel, [start for _, start in terms]),
                out_shape=shape(rows_left, 2 * HD),
                in_specs=in_vmem(len(terms)) + anywhere(step in before),
                out_specs=in_vmem(1)[0],
                compiler_params=params(8),
                name="add",
            )(*[term for term, _ in terms], *[before[s] for s in [step] if s in before])
            kept.append(swap(send, "ctx", shards, step))
            before[step] = send if step == 2 else kept[-2]
            rows_left //= 2
            step *= 2
            terms = [(term, rows_left) for term in kept]
        spread_args += kept + [own[g]]
    parts_per_head = len(spread_args) // kv_heads

    grad_keys, grad_values = pl.pallas_call(
        functools.partial(spread_kernel, parts_per_head),
        out_shape=[shape(tokens, kv_width)] * 2,
        in_specs=in_vmem(1 + len(spread_args)),
        out_specs=in_vmem(2),
        compiler_params=params(12),
        name="spread",
    )(segment_ids, *spread_args)
    return dq, grad_keys, grad_values


def solution(mesh):
    return jax.shard_map(
        local,
        mesh=mesh,
        in_specs=(
            P(("ctx", "head"), None),
            P(("ctx", "head"), None),
            P(("ctx", "head"), None),
            P("head", "ctx"),
            P(("ctx", "head"), None),
        ),
        out_specs=(P("ctx", "head"), P("ctx", "head"), P("ctx", "head")),
        check_vma=False,
    )
```

```python
import functools

import jax
import jax.numpy as jnp
from jax import lax
from jax.experimental import pallas as pl
from jax.experimental.pallas import tpu as pltpu
from jax.sharding import PartitionSpec as P

QH = 64
KVH = 8
HD = 128
SLOT_DEV = 96
GROUP = QH // KVH
GW = GROUP * HD
SCALE = HD ** (-0.5)
LOG2E = 1.4426950408889634
DEAD = 1024.0
HIDDEN = 2.0**96
PAIR = 2
PART = 48


def nt(a, b):
    return lax.dot_general(a, b, (((1,), (1,)), ((), ())), preferred_element_type=jnp.float32)


def nn(a, b):
    return lax.dot_general(a, b, (((1,), (0,)), ((), ())), preferred_element_type=jnp.float32)


def tn(a, b):
    return lax.dot_general(a, b, (((0,), (0,)), ((), ())), preferred_element_type=jnp.float32)


def slot_picks(seg_row, tokens):
    return lax.broadcasted_iota(jnp.int32, (SLOT_DEV, tokens), 0) == seg_row


def place():
    return lax.axis_index("ctx"), lax.axis_index("head")


def lanes(start, size):
    return pl.ds(pl.multiple_of(start, HD), size)


def run_copies(copies):
    for copy in copies:
        copy.start()
    return copies


def wait_copies(copies):
    for copy in copies:
        copy.wait()


def pack_kernel(jobs, *refs):
    outs = [out for _, dests in jobs for out in dests]
    sources, out_refs, sems = refs[:2], refs[-len(outs) - 1 : -1], refs[-1]
    me = place()[1]
    copies = []
    done = 0
    for width, dests in jobs:
        for out, pieces in zip(out_refs[done:], dests):
            for at, (m, scale, offset) in enumerate(pieces):
                start = lax.bitwise_xor(me, m) * scale + offset
                for part, source in enumerate(sources):
                    rows = source.shape[0]
                    copies.append(
                        pltpu.make_async_copy(
                            source.at[:, lanes(start, width)],
                            out.at[at * rows : (at + 1) * rows, part * width : (part + 1) * width],
                            sems.at[len(copies)],
                        )
                    )
        done += len(dests)
    wait_copies(run_copies(copies))


def gate_kernel(*refs):
    pass


def pack_kv_kernel(kv_heads, key_ref, value_ref, *outs):
    me = place()[1]
    width = kv_heads * HD
    for m, out in enumerate(outs):
        start = lax.bitwise_xor(me, m) * width
        out[:, 0:width] = key_ref[:, lanes(start, width)]
        out[:, width : 2 * width] = value_ref[:, lanes(start, width)]


def merge_kernel(heads, seg_ref, *refs):
    pieces, (out, hide_ref, whole) = refs[:heads], refs[-3:]
    kv_heads, tokens = seg_ref.shape
    rows = tokens // heads
    me = place()[1]
    for m, piece in enumerate(pieces):
        start = pl.multiple_of(lax.bitwise_xor(me, m) * rows, 16)
        whole[pl.ds(start, rows), :] = piece[...]
    for g in range(kv_heads):
        picks = slot_picks(seg_ref[g : g + 1, :], tokens).astype(jnp.float32)
        counts = jnp.sum(picks, axis=1, keepdims=True)
        low_picks = picks.astype(jnp.bfloat16)
        sizes = jnp.maximum(counts, 1.0)
        for part in range(2):
            at = slice((part * kv_heads + g) * HD, (part * kv_heads + g + 1) * HD)
            rows_out = nn(low_picks, whole[:, at]) / sizes
            if part == 0:
                rows_out = jnp.where(counts == 0.0, DEAD, rows_out)
            out[:, at] = rows_out.astype(jnp.bfloat16)
        padded = -(-tokens // HD) * HD
        place_in = lax.broadcasted_iota(jnp.int32, (HD, padded), 0)
        seg = jnp.concatenate([seg_ref[g : g + 1, :]] * 2, axis=1)[:, :padded]
        late = (place_in >= seg) & (place_in < SLOT_DEV)
        hide = jnp.where(late, -HIDDEN, jnp.where(place_in == SLOT_DEV, 1.0, 0.0))
        hide_ref[g] = hide.T[:tokens].astype(jnp.bfloat16)


def folded(x, reduce):
    return reduce(x.reshape(x.shape[0] // 8, 8, x.shape[1]), axis=0)


def attend_kernel(g, order, q_ref, o_ref, hide_ref, *refs):
    shards = len(order)
    heads = 4
    kv_pieces, blocks, refs = refs[:heads], refs[heads : heads + shards], refs[heads + shards :]
    qo_pieces = refs[: heads - 1]
    (
        p_ref, ds_ref, own_p_ref, own_ds_ref, qs_ref, os_ref, key_ref, far_ref,
        kx, vx, mine, s_ref, g_ref, sems,
    ) = refs[-14:]
    rows = q_ref.shape[0]
    kv_heads = hide_ref.shape[0]
    slots = shards * SLOT_DEV
    shard, me = place()
    key_at = slice(g * HD, (g + 1) * HD)
    value_at = slice((kv_heads + g) * HD, (kv_heads + g + 1) * HD)
    start = (me * kv_heads + g) * GW
    copies = run_copies(
        [
            pltpu.make_async_copy(
                source.at[:, lanes(start, GW)], mine.at[:, part * GW : (part + 1) * GW], sems.at[part]
            )
            for part, source in enumerate((q_ref, o_ref))
        ]
    )

    lane = lax.broadcasted_iota(jnp.int32, (SLOT_DEV, HD), 1)
    row = lax.broadcasted_iota(jnp.int32, (SLOT_DEV, HD), 0)
    for r, (m, block) in enumerate(zip(order, blocks)):
        at = pl.ds(r * SLOT_DEV, SLOT_DEV)
        key = block[:, key_at].astype(jnp.float32)
        vx[at, :] = block[:, value_at]
        if m == 0:
            extra = jnp.where(lane == row, 1.0, 0.0)
        else:
            hide = (key[:, 0:1] > 100.0) | (lax.bitwise_xor(shard, m) > shard)
            extra = jnp.where(hide & (lane >= SLOT_DEV), -HIDDEN, 0.0)
        kx[at, 0:HD] = jnp.where(key > 100.0, 0.0, key).astype(jnp.bfloat16)
        kx[at, HD : 2 * HD] = extra.astype(jnp.bfloat16)
    kx[slots:, HD : 2 * HD] = jnp.zeros((PAIR * rows, HD), jnp.bfloat16)

    width = GROUP * rows
    span = PAIR * width
    eye_row = lax.broadcasted_iota(jnp.int32, (PAIR * rows, span), 0)
    eye_lane = lax.broadcasted_iota(jnp.int32, (PAIR * rows, span), 1)
    eye = (eye_row // rows == eye_lane // width) & (eye_row % rows == eye_lane % rows)
    factor = SCALE * LOG2E

    turns = list(range(1, heads)) + [0]
    for turn in range(0, heads, PAIR):
        pair = turns[turn : turn + PAIR]
        if 0 in pair:
            wait_copies(copies)
        queries = []
        cotangents = []
        hides = []
        for i, m in enumerate(pair):
            qo, part = (qo_pieces[m - 1], g) if m else (mine, 0)
            at = slice(part * rows, (part + 1) * rows)
            here = slice(slots + i * rows, slots + (i + 1) * rows)
            kx[here, 0:HD] = kv_pieces[m][:, key_at]
            vx[here, :] = kv_pieces[m][:, value_at]
            q2 = jnp.concatenate([qo[at, h * HD : (h + 1) * HD] for h in range(GROUP)], axis=0)
            o2 = jnp.concatenate(
                [qo[at, GW + h * HD : GW + (h + 1) * HD] for h in range(GROUP)], axis=0
            )
            chunk = slice(m * width, (m + 1) * width)
            qs_ref[chunk, :] = q2
            os_ref[chunk, :] = o2
            queries.append(q2)
            cotangents.append(o2)
            tokens_at = pl.ds(pl.multiple_of(lax.bitwise_xor(me, m) * rows, 16), rows)
            hides += [hide_ref[g, tokens_at, :]] * GROUP
        qx = jnp.concatenate(
            [jnp.concatenate(queries, axis=0), jnp.concatenate(hides, axis=0)], axis=1
        )
        held = turn // PAIR % s_ref.shape[0]
        s_at, g_at = s_ref.at[held], g_ref.at[held]
        s_at[...] = nt(kx[...], qx)
        g_at[...] = nt(vx[...], jnp.concatenate(cotangents, axis=0))
        own_score = jnp.sum(jnp.where(eye, s_at[slots:, :], 0.0), axis=0, keepdims=True)
        own_grad_prob = jnp.sum(jnp.where(eye, g_at[slots:, :], 0.0), axis=0, keepdims=True)
        parts = [slice(r, r + PART) for r in range(0, slots, PART)]
        top = folded(functools.reduce(jnp.maximum, [s_at[part, :] for part in parts]), jnp.max)
        top = jnp.maximum(jnp.max(top, axis=0, keepdims=True), own_score)
        total = 0.0
        delta = 0.0
        for part in parts:
            weights = jnp.exp2((s_at[part, :] - top) * factor)
            total = total + folded(weights, jnp.sum)
            delta = delta + folded(weights * g_at[part, :], jnp.sum)
        own_weight = jnp.exp2((own_score - top) * factor)
        total = jnp.sum(total, axis=0, keepdims=True) + own_weight
        delta = jnp.sum(delta, axis=0, keepdims=True) + own_weight * own_grad_prob
        delta = delta / total
        own_prob = own_weight / total
        log_total = jnp.log2(total)
        for part in parts:
            probs = jnp.exp2((s_at[part, :] - top) * factor - log_total)
            low_probs = probs.astype(jnp.bfloat16)
            low_grads = (probs * (g_at[part, :] - delta)).astype(jnp.bfloat16)
            for i, m in enumerate(pair):
                p_ref[part, m * width : (m + 1) * width] = low_probs[:, i * width : (i + 1) * width]
                ds_ref[part, m * width : (m + 1) * width] = low_grads[:, i * width : (i + 1) * width]
        own_grad_score = own_prob * (own_grad_prob - delta)
        for i, m in enumerate(pair):
            chunk = slice(m * width, (m + 1) * width)
            here = slice(i * width, (i + 1) * width)
            one = eye[0:rows, 0:width]
            own_p_ref[:, chunk] = jnp.where(one, own_prob[:, here], 0.0).astype(jnp.bfloat16)
            own_ds_ref[:, chunk] = jnp.where(one, own_grad_score[:, here], 0.0).astype(jnp.bfloat16)
    far = slice(slots // 2, slots)
    far_ref[:, 0:HD] = (SCALE * nn(ds_ref[far, :], qs_ref[...])).astype(far_ref.dtype)
    far_ref[:, HD : 2 * HD] = nn(p_ref[far, :], os_ref[...]).astype(far_ref.dtype)
    key_ref[...] = kx[0:slots, 0:HD]


def terms_kernel(heads, p_ref, ds_ref, own_p_ref, own_ds_ref, qs_ref, os_ref, after_ref, near_ref, own_ref):
    rows = own_p_ref.shape[0]
    near = slice(0, near_ref.shape[0])
    near_ref[:, 0:HD] = SCALE * nn(ds_ref[near, :], qs_ref[...])
    near_ref[:, HD : 2 * HD] = nn(p_ref[near, :], os_ref[...])
    me = place()[1]
    width = GROUP * rows
    for m in range(heads):
        at = pl.ds(pl.multiple_of(lax.bitwise_xor(me, m) * rows, 16), rows)
        chunk = slice(m * width, (m + 1) * width)
        own_ref[at, 0:HD] = SCALE * nn(own_ds_ref[:, chunk], qs_ref[chunk, :])
        own_ref[at, HD : 2 * HD] = nn(own_p_ref[:, chunk], os_ref[chunk, :])


def queries_kernel(heads, *refs):
    kv_pieces, refs, dq_ref = refs[:heads], refs[heads:-1], refs[-1]
    me = place()[1]
    for g in range(len(refs) // 3):
        ds_ref, own_ds_ref, key_ref = refs[3 * g : 3 * g + 3]
        turned = key_ref[...].astype(jnp.float32).T.astype(jnp.bfloat16)
        rows = own_ds_ref.shape[0]
        width = GROUP * rows
        for m in range(heads):
            at = pl.ds(pl.multiple_of(lax.bitwise_xor(me, m) * rows, 16), rows)
            chunk = slice(m * width, (m + 1) * width)
            own_key = kv_pieces[m][:, g * HD : (g + 1) * HD]
            dq = nn(turned, ds_ref[:, chunk]) + tn(own_key, own_ds_ref[:, chunk])
            dq = (SCALE * dq).T.astype(jnp.bfloat16)
            for h in range(GROUP):
                column = (g * GROUP + h) * HD
                dq_ref[at, column : column + HD] = dq[h * rows : (h + 1) * rows]


def add_kernel(near_ref, far_ref, keep_ref, send_ref):
    total = near_ref[...] + far_ref[...].astype(jnp.float32)
    half = keep_ref.shape[0]
    keep_ref[...] = total[:half]
    send_ref[...] = total[half:].astype(send_ref.dtype)


def spread_kernel(parts_per_head, seg_ref, *refs):
    kv_heads, tokens = seg_ref.shape
    gk_ref, gv_ref = refs[-2:]
    for g in range(kv_heads):
        parts = refs[g * parts_per_head : (g + 1) * parts_per_head]
        total = parts[0][...].astype(jnp.float32)
        for part in parts[1:-1]:
            total = total + part[...].astype(jnp.float32)
        picks = slot_picks(seg_ref[g : g + 1, :], tokens).astype(jnp.float32)
        counts = jnp.sum(picks, axis=1, keepdims=True)
        total = total / jnp.maximum(counts, 1.0)
        high = total.astype(jnp.bfloat16)
        low = (total - high.astype(jnp.float32)).astype(jnp.bfloat16)
        picks = picks.astype(jnp.bfloat16)
        spread = tn(picks, high) + tn(picks, low) + parts[-1][...]
        gk_ref[:, g * HD : (g + 1) * HD] = spread[:, 0:HD].astype(jnp.bfloat16)
        gv_ref[:, g * HD : (g + 1) * HD] = spread[:, HD : 2 * HD].astype(jnp.bfloat16)


def in_vmem(count):
    return [pl.BlockSpec(memory_space=pltpu.VMEM)] * count


def anywhere(count):
    return [pl.BlockSpec(memory_space=pl.ANY)] * count


def params(mib):
    return pltpu.CompilerParams(vmem_limit_bytes=mib * 2**20)


def shape(*dims, dtype=jnp.bfloat16):
    return jax.ShapeDtypeStruct(dims, dtype)


def swap(x, axis, size, m):
    return lax.ppermute(x, axis, [(i, i ^ m) for i in range(size)])


def gate(value, after, mib=0):
    return pl.pallas_call(
        gate_kernel,
        out_shape=shape(*value.shape, dtype=value.dtype),
        in_specs=anywhere(1 + len(after)),
        out_specs=anywhere(1)[0],
        input_output_aliases={0: 0},
        compiler_params=params(1),
        cost_estimate=pl.CostEstimate(flops=0, bytes_accessed=mib * 2**20, transcendentals=0),
        name="gate",
    )(value, *after)


def bit_reversed(count):
    if count == 1:
        return [0]
    half = [2 * i for i in bit_reversed(count // 2)]
    return half + [i + 1 for i in half]


def local(queries, keys, values, segment_ids, grad_out):
    rows = queries.shape[0]
    heads = lax.axis_size("head")
    tokens = rows * heads
    kv_heads = KVH // heads
    shards = lax.axis_size("ctx")
    order = bit_reversed(shards)
    half = SLOT_DEV * shards // 2
    slots = SLOT_DEV * shards
    kv_width = kv_heads * HD

    def kv_at(m):
        return (m, kv_width, 0)

    def qo_at(m, g):
        return (m, kv_heads * GW, g * GW)

    def pack(jobs, sources, after, mib, name):
        outs = [pieces for _, dests in jobs for pieces in dests]
        return pl.pallas_call(
            functools.partial(pack_kernel, jobs),
            out_shape=[
                shape(len(pieces) * rows, 2 * width) for width, dests in jobs for pieces in dests
            ],
            in_specs=anywhere(2 + len(after)),
            out_specs=anywhere(len(outs)),
            scratch_shapes=[
                pltpu.SemaphoreType.DMA((2 * sum(len(p) for _, dests in jobs for p in dests),))
            ],
            compiler_params=params(mib),
            name=name,
        )(*sources, *after)

    kv_out = pl.pallas_call(
        functools.partial(pack_kv_kernel, kv_heads),
        out_shape=[shape(rows, 2 * kv_width)] * heads,
        in_specs=in_vmem(2),
        out_specs=in_vmem(heads),
        compiler_params=params(2),
        name="pack_kv",
    )(keys, values)
    kv = [kv_out[0]] + [swap(kv_out[m], "head", heads, m) for m in range(1, heads)]

    jobs = [(GW, [[qo_at(m, g) for g in range(kv_heads)] for m in range(1, heads)])]
    packed = pack(jobs, (queries, grad_out), kv_out[:1], 4, "pack_qo")
    handed = swap(gate(packed[2], kv[1:]), "head", heads, 1)
    from_across = swap(gate(packed[1], kv[1:]), "head", heads, 2)
    from_corner = swap(handed, "head", heads, 2)

    merged, hide = pl.pallas_call(
        functools.partial(merge_kernel, heads),
        out_shape=[shape(SLOT_DEV, 2 * kv_width), shape(kv_heads, tokens, HD)],
        in_specs=in_vmem(1 + heads),
        out_specs=in_vmem(2),
        scratch_shapes=[pltpu.VMEM((tokens, 2 * kv_width), jnp.bfloat16)],
        compiler_params=params(4),
        name="merge",
    )(segment_ids, *kv)

    held = {0: merged}
    for m in range(1, shards):
        low = m & -m
        held[m] = swap(held[m - low], "ctx", shards, low)
    late = [held[m] for m in range(1, shards - 1)] + [from_across]
    from_core = swap(gate(packed[0], late), "head", heads, 1)
    from_corner = gate(from_corner, (), 40)
    qo = (from_core, from_across, from_corner)

    all_rows = tokens * GROUP
    saved = []
    buffers = 2 if slots <= 1024 else 1
    for g in range(kv_heads):
        outs = pl.pallas_call(
            functools.partial(attend_kernel, g, order),
            out_shape=[
                shape(slots, all_rows),
                shape(slots, all_rows),
                shape(rows, all_rows),
                shape(rows, all_rows),
                shape(all_rows, HD),
                shape(all_rows, HD),
                shape(slots, HD),
                shape(half, 2 * HD),
            ],
            in_specs=anywhere(2) + in_vmem(heads + heads + shards) + anywhere(g > 0),
            out_specs=in_vmem(8),
            scratch_shapes=[
                pltpu.VMEM((slots + PAIR * rows, 2 * HD), jnp.bfloat16),
                pltpu.VMEM((slots + PAIR * rows, HD), jnp.bfloat16),
                pltpu.VMEM((rows, 2 * GW), jnp.bfloat16),
                pltpu.VMEM((buffers, slots + PAIR * rows, PAIR * GROUP * rows), jnp.float32),
                pltpu.VMEM((buffers, slots + PAIR * rows, PAIR * GROUP * rows), jnp.float32),
                pltpu.SemaphoreType.DMA((2,)),
            ],
            compiler_params=params(24),
            cost_estimate=pl.CostEstimate(
                flops=6 * all_rows * (slots + rows) * HD,
                bytes_accessed=8 * 2**20,
                transcendentals=all_rows * slots,
            ),
            name="attend",
        )(
            queries,
            grad_out,
            hide,
            *kv,
            *[held[m] for m in order],
            *qo,
            *([saved[-1][2]] if g else []),
        )
        saved.append(outs)
    far = [swap(outs[7], "ctx", shards, 1) for outs in saved]
    near = []
    own = []
    for g in range(kv_heads):
        outs = pl.pallas_call(
            functools.partial(terms_kernel, heads),
            out_shape=[
                shape(half, 2 * HD, dtype=jnp.float32),
                shape(tokens, 2 * HD, dtype=jnp.float32),
            ],
            in_specs=in_vmem(6) + anywhere(1),
            out_specs=in_vmem(2),
            compiler_params=params(16),
            cost_estimate=pl.CostEstimate(
                flops=2 * all_rows * slots * HD, bytes_accessed=2**20, transcendentals=0
            ),
            name="terms",
        )(*saved[g][:6], saved[-1][2])
        near.append(outs[0])
        own.append(outs[1])
    dq = pl.pallas_call(
        functools.partial(queries_kernel, heads),
        out_shape=shape(tokens, kv_heads * GW),
        in_specs=in_vmem(heads + 3 * kv_heads),
        out_specs=in_vmem(1)[0],
        compiler_params=params(16),
        cost_estimate=pl.CostEstimate(
            flops=2 * kv_heads * all_rows * slots * HD, bytes_accessed=2**20, transcendentals=0
        ),
        name="queries",
    )(*kv, *[x for outs in saved for x in (outs[1], outs[3], outs[6])])

    spread_args = []
    for g in range(kv_heads):
        keep, received, step = near[g], far[g], 2
        while step < shards:
            count = keep.shape[0] // 2
            keep, send = pl.pallas_call(
                add_kernel,
                out_shape=[shape(count, 2 * HD, dtype=jnp.float32), shape(count, 2 * HD)],
                in_specs=in_vmem(2),
                out_specs=in_vmem(2),
                compiler_params=params(8),
                name="add",
            )(keep, received)
            received = swap(send, "ctx", shards, step)
            step *= 2
        spread_args += [keep, received, own[g]]

    grad_keys, grad_values = pl.pallas_call(
        functools.partial(spread_kernel, 3),
        out_shape=[shape(tokens, kv_width)] * 2,
        in_specs=in_vmem(1 + len(spread_args)),
        out_specs=in_vmem(2),
        compiler_params=params(12),
        name="spread",
    )(segment_ids, *spread_args)
    return dq, grad_keys, grad_values


def solution(mesh):
    return jax.shard_map(
        local,
        mesh=mesh,
        in_specs=(
            P(("ctx", "head"), None),
            P(("ctx", "head"), None),
            P(("ctx", "head"), None),
            P("head", "ctx"),
            P(("ctx", "head"), None),
        ),
        out_specs=(P("ctx", "head"), P("ctx", "head"), P("ctx", "head")),
        check_vma=False,
    )
```

```python
import functools

import jax
import jax.numpy as jnp
from jax import lax
from jax.experimental import pallas as pl
from jax.experimental.pallas import tpu as pltpu
from jax.sharding import PartitionSpec as P

QH = 64
KVH = 8
HD = 128
SLOT_DEV = 96
GROUP = QH // KVH
GW = GROUP * HD
SCALE = HD ** (-0.5)
LOG2E = 1.4426950408889634
DEAD = 1024.0
HIDDEN = 2.0**96
PAIR = 2
PART = 48


def nt(a, b):
    return lax.dot_general(a, b, (((1,), (1,)), ((), ())), preferred_element_type=jnp.float32)


def nn(a, b):
    return lax.dot_general(a, b, (((1,), (0,)), ((), ())), preferred_element_type=jnp.float32)


def tn(a, b):
    return lax.dot_general(a, b, (((0,), (0,)), ((), ())), preferred_element_type=jnp.float32)


def slot_picks(seg_row, tokens):
    return lax.broadcasted_iota(jnp.int32, (SLOT_DEV, tokens), 0) == seg_row


def place():
    return lax.axis_index("ctx"), lax.axis_index("head")


def lanes(start, size):
    return pl.ds(pl.multiple_of(start, HD), size)


def run_copies(copies):
    for copy in copies:
        copy.start()
    return copies


def wait_copies(copies):
    for copy in copies:
        copy.wait()


def pack_kernel(jobs, *refs):
    outs = [out for _, dests in jobs for out in dests]
    sources, out_refs, sems = refs[:2], refs[-len(outs) - 1 : -1], refs[-1]
    me = place()[1]
    copies = []
    done = 0
    for width, dests in jobs:
        for out, pieces in zip(out_refs[done:], dests):
            for at, (m, scale, offset) in enumerate(pieces):
                start = lax.bitwise_xor(me, m) * scale + offset
                for part, source in enumerate(sources):
                    rows = source.shape[0]
                    copies.append(
                        pltpu.make_async_copy(
                            source.at[:, lanes(start, width)],
                            out.at[at * rows : (at + 1) * rows, part * width : (part + 1) * width],
                            sems.at[len(copies)],
                        )
                    )
        done += len(dests)
    wait_copies(run_copies(copies))


def gate_kernel(*refs):
    pass


def pack_kv_kernel(kv_heads, key_ref, value_ref, *outs):
    me = place()[1]
    width = kv_heads * HD
    for m, out in enumerate(outs):
        start = lax.bitwise_xor(me, m) * width
        out[:, 0:width] = key_ref[:, lanes(start, width)]
        out[:, width : 2 * width] = value_ref[:, lanes(start, width)]


def merge_kernel(heads, seg_ref, *refs):
    pieces, (out, hide_ref, whole) = refs[:heads], refs[-3:]
    kv_heads, tokens = seg_ref.shape
    rows = tokens // heads
    me = place()[1]
    for m, piece in enumerate(pieces):
        start = pl.multiple_of(lax.bitwise_xor(me, m) * rows, 16)
        whole[pl.ds(start, rows), :] = piece[...]
    for g in range(kv_heads):
        picks = slot_picks(seg_ref[g : g + 1, :], tokens).astype(jnp.float32)
        counts = jnp.sum(picks, axis=1, keepdims=True)
        low_picks = picks.astype(jnp.bfloat16)
        sizes = jnp.maximum(counts, 1.0)
        for part in range(2):
            at = slice((part * kv_heads + g) * HD, (part * kv_heads + g + 1) * HD)
            rows_out = nn(low_picks, whole[:, at]) / sizes
            if part == 0:
                rows_out = jnp.where(counts == 0.0, DEAD, rows_out)
            out[:, at] = rows_out.astype(jnp.bfloat16)
        padded = -(-tokens // HD) * HD
        place_in = lax.broadcasted_iota(jnp.int32, (HD, padded), 0)
        seg = jnp.concatenate([seg_ref[g : g + 1, :]] * 2, axis=1)[:, :padded]
        late = (place_in >= seg) & (place_in < SLOT_DEV)
        hide = jnp.where(late, -HIDDEN, jnp.where(place_in == SLOT_DEV, 1.0, 0.0))
        hide_ref[g] = hide.T[:tokens].astype(jnp.bfloat16)


def folded(x, reduce):
    return reduce(x.reshape(x.shape[0] // 8, 8, x.shape[1]), axis=0)


def attend_kernel(g, order, q_ref, o_ref, hide_ref, *refs):
    shards = len(order)
    heads = 4
    kv_pieces, blocks, refs = refs[:heads], refs[heads : heads + shards], refs[heads + shards :]
    qo_pieces = refs[: heads - 1]
    (
        p_ref, ds_ref, own_p_ref, own_ds_ref, qs_ref, os_ref, key_ref, far_ref,
        kx, vx, mine, s_ref, g_ref, sems,
    ) = refs[-14:]
    rows = q_ref.shape[0]
    kv_heads = hide_ref.shape[0]
    slots = shards * SLOT_DEV
    shard, me = place()
    key_at = slice(g * HD, (g + 1) * HD)
    value_at = slice((kv_heads + g) * HD, (kv_heads + g + 1) * HD)
    start = (me * kv_heads + g) * GW
    copies = run_copies(
        [
            pltpu.make_async_copy(
                source.at[:, lanes(start, GW)], mine.at[:, part * GW : (part + 1) * GW], sems.at[part]
            )
            for part, source in enumerate((q_ref, o_ref))
        ]
    )

    lane = lax.broadcasted_iota(jnp.int32, (SLOT_DEV, HD), 1)
    row = lax.broadcasted_iota(jnp.int32, (SLOT_DEV, HD), 0)
    for r, (m, block) in enumerate(zip(order, blocks)):
        at = pl.ds(r * SLOT_DEV, SLOT_DEV)
        key = block[:, key_at].astype(jnp.float32)
        vx[at, :] = block[:, value_at]
        if m == 0:
            extra = jnp.where(lane == row, 1.0, 0.0)
        else:
            hide = (key[:, 0:1] > 100.0) | (lax.bitwise_xor(shard, m) > shard)
            extra = jnp.where(hide & (lane >= SLOT_DEV), -HIDDEN, 0.0)
        kx[at, 0:HD] = jnp.where(key > 100.0, 0.0, key).astype(jnp.bfloat16)
        kx[at, HD : 2 * HD] = extra.astype(jnp.bfloat16)
    kx[slots:, HD : 2 * HD] = jnp.zeros((PAIR * rows, HD), jnp.bfloat16)

    width = GROUP * rows
    span = PAIR * width
    eye_row = lax.broadcasted_iota(jnp.int32, (PAIR * rows, span), 0)
    eye_lane = lax.broadcasted_iota(jnp.int32, (PAIR * rows, span), 1)
    eye = (eye_row // rows == eye_lane // width) & (eye_row % rows == eye_lane % rows)
    factor = SCALE * LOG2E

    turns = list(range(1, heads)) + [0]
    for turn in range(0, heads, PAIR):
        pair = turns[turn : turn + PAIR]
        if 0 in pair:
            wait_copies(copies)
        queries = []
        cotangents = []
        hides = []
        for i, m in enumerate(pair):
            qo, part = (qo_pieces[m - 1], g) if m else (mine, 0)
            at = slice(part * rows, (part + 1) * rows)
            here = slice(slots + i * rows, slots + (i + 1) * rows)
            kx[here, 0:HD] = kv_pieces[m][:, key_at]
            vx[here, :] = kv_pieces[m][:, value_at]
            q2 = jnp.concatenate([qo[at, h * HD : (h + 1) * HD] for h in range(GROUP)], axis=0)
            o2 = jnp.concatenate(
                [qo[at, GW + h * HD : GW + (h + 1) * HD] for h in range(GROUP)], axis=0
            )
            chunk = slice(m * width, (m + 1) * width)
            qs_ref[chunk, :] = q2
            os_ref[chunk, :] = o2
            queries.append(q2)
            cotangents.append(o2)
            tokens_at = pl.ds(pl.multiple_of(lax.bitwise_xor(me, m) * rows, 16), rows)
            hides += [hide_ref[g, tokens_at, :]] * GROUP
        qx = jnp.concatenate(
            [jnp.concatenate(queries, axis=0), jnp.concatenate(hides, axis=0)], axis=1
        )
        held = turn // PAIR % s_ref.shape[0]
        s_at, g_at = s_ref.at[held], g_ref.at[held]
        s_at[...] = nt(kx[...], qx)
        g_at[...] = nt(vx[...], jnp.concatenate(cotangents, axis=0))
        own_score = jnp.sum(jnp.where(eye, s_at[slots:, :], 0.0), axis=0, keepdims=True)
        own_grad_prob = jnp.sum(jnp.where(eye, g_at[slots:, :], 0.0), axis=0, keepdims=True)
        parts = [slice(r, r + PART) for r in range(0, slots, PART)]
        top = folded(functools.reduce(jnp.maximum, [s_at[part, :] for part in parts]), jnp.max)
        top = jnp.maximum(jnp.max(top, axis=0, keepdims=True), own_score)
        total = 0.0
        delta = 0.0
        for part in parts:
            weights = jnp.exp2((s_at[part, :] - top) * factor)
            s_at[part, :] = weights
            total = total + folded(weights, jnp.sum)
            delta = delta + folded(weights * g_at[part, :], jnp.sum)
        own_weight = jnp.exp2((own_score - top) * factor)
        total = jnp.sum(total, axis=0, keepdims=True) + own_weight
        delta = jnp.sum(delta, axis=0, keepdims=True) + own_weight * own_grad_prob
        delta = delta / total
        own_prob = own_weight / total
        inverse = 1.0 / total
        for part in parts:
            probs = s_at[part, :] * inverse
            low_probs = probs.astype(jnp.bfloat16)
            low_grads = (probs * (g_at[part, :] - delta)).astype(jnp.bfloat16)
            for i, m in enumerate(pair):
                p_ref[part, m * width : (m + 1) * width] = low_probs[:, i * width : (i + 1) * width]
                ds_ref[part, m * width : (m + 1) * width] = low_grads[:, i * width : (i + 1) * width]
        own_grad_score = own_prob * (own_grad_prob - delta)
        for i, m in enumerate(pair):
            chunk = slice(m * width, (m + 1) * width)
            here = slice(i * width, (i + 1) * width)
            one = eye[0:rows, 0:width]
            own_p_ref[:, chunk] = jnp.where(one, own_prob[:, here], 0.0).astype(jnp.bfloat16)
            own_ds_ref[:, chunk] = jnp.where(one, own_grad_score[:, here], 0.0).astype(jnp.bfloat16)
    far = slice(slots // 2, slots)
    far_ref[:, 0:HD] = (SCALE * nn(ds_ref[far, :], qs_ref[...])).astype(far_ref.dtype)
    far_ref[:, HD : 2 * HD] = nn(p_ref[far, :], os_ref[...]).astype(far_ref.dtype)
    key_ref[...] = kx[0:slots, 0:HD]


def terms_kernel(heads, p_ref, ds_ref, own_p_ref, own_ds_ref, qs_ref, os_ref, after_ref, near_ref, own_ref):
    rows = own_p_ref.shape[0]
    near = slice(0, near_ref.shape[0])
    near_ref[:, 0:HD] = SCALE * nn(ds_ref[near, :], qs_ref[...])
    near_ref[:, HD : 2 * HD] = nn(p_ref[near, :], os_ref[...])
    me = place()[1]
    width = GROUP * rows
    for m in range(heads):
        at = pl.ds(pl.multiple_of(lax.bitwise_xor(me, m) * rows, 16), rows)
        chunk = slice(m * width, (m + 1) * width)
        own_ref[at, 0:HD] = SCALE * nn(own_ds_ref[:, chunk], qs_ref[chunk, :])
        own_ref[at, HD : 2 * HD] = nn(own_p_ref[:, chunk], os_ref[chunk, :])


def queries_kernel(heads, *refs):
    kv_pieces, refs, dq_ref = refs[:heads], refs[heads:-1], refs[-1]
    me = place()[1]
    for g in range(len(refs) // 3):
        ds_ref, own_ds_ref, key_ref = refs[3 * g : 3 * g + 3]
        turned = key_ref[...].astype(jnp.float32).T.astype(jnp.bfloat16)
        rows = own_ds_ref.shape[0]
        width = GROUP * rows
        for m in range(heads):
            at = pl.ds(pl.multiple_of(lax.bitwise_xor(me, m) * rows, 16), rows)
            chunk = slice(m * width, (m + 1) * width)
            own_key = kv_pieces[m][:, g * HD : (g + 1) * HD]
            dq = nn(turned, ds_ref[:, chunk]) + tn(own_key, own_ds_ref[:, chunk])
            dq = (SCALE * dq).T.astype(jnp.bfloat16)
            for h in range(GROUP):
                column = (g * GROUP + h) * HD
                dq_ref[at, column : column + HD] = dq[h * rows : (h + 1) * rows]


def add_kernel(near_ref, far_ref, keep_ref, send_ref):
    total = near_ref[...] + far_ref[...].astype(jnp.float32)
    half = keep_ref.shape[0]
    keep_ref[...] = total[:half]
    send_ref[...] = total[half:].astype(send_ref.dtype)


def spread_kernel(parts_per_head, seg_ref, *refs):
    kv_heads, tokens = seg_ref.shape
    gk_ref, gv_ref = refs[-2:]
    for g in range(kv_heads):
        parts = refs[g * parts_per_head : (g + 1) * parts_per_head]
        total = parts[0][...].astype(jnp.float32)
        for part in parts[1:-1]:
            total = total + part[...].astype(jnp.float32)
        picks = slot_picks(seg_ref[g : g + 1, :], tokens).astype(jnp.float32)
        counts = jnp.sum(picks, axis=1, keepdims=True)
        total = total / jnp.maximum(counts, 1.0)
        high = total.astype(jnp.bfloat16)
        low = (total - high.astype(jnp.float32)).astype(jnp.bfloat16)
        picks = picks.astype(jnp.bfloat16)
        spread = tn(picks, high) + tn(picks, low) + parts[-1][...]
        gk_ref[:, g * HD : (g + 1) * HD] = spread[:, 0:HD].astype(jnp.bfloat16)
        gv_ref[:, g * HD : (g + 1) * HD] = spread[:, HD : 2 * HD].astype(jnp.bfloat16)


def in_vmem(count):
    return [pl.BlockSpec(memory_space=pltpu.VMEM)] * count


def anywhere(count):
    return [pl.BlockSpec(memory_space=pl.ANY)] * count


def params(mib):
    return pltpu.CompilerParams(vmem_limit_bytes=mib * 2**20)


def shape(*dims, dtype=jnp.bfloat16):
    return jax.ShapeDtypeStruct(dims, dtype)


def swap(x, axis, size, m):
    return lax.ppermute(x, axis, [(i, i ^ m) for i in range(size)])


def gate(value, after, mib=0):
    return pl.pallas_call(
        gate_kernel,
        out_shape=shape(*value.shape, dtype=value.dtype),
        in_specs=anywhere(1 + len(after)),
        out_specs=anywhere(1)[0],
        input_output_aliases={0: 0},
        compiler_params=params(1),
        cost_estimate=pl.CostEstimate(flops=0, bytes_accessed=mib * 2**20, transcendentals=0),
        name="gate",
    )(value, *after)


def bit_reversed(count):
    if count == 1:
        return [0]
    half = [2 * i for i in bit_reversed(count // 2)]
    return half + [i + 1 for i in half]


def local(queries, keys, values, segment_ids, grad_out):
    rows = queries.shape[0]
    heads = lax.axis_size("head")
    tokens = rows * heads
    kv_heads = KVH // heads
    shards = lax.axis_size("ctx")
    order = bit_reversed(shards)
    half = SLOT_DEV * shards // 2
    slots = SLOT_DEV * shards
    kv_width = kv_heads * HD

    def kv_at(m):
        return (m, kv_width, 0)

    def qo_at(m, g):
        return (m, kv_heads * GW, g * GW)

    def pack(jobs, sources, after, mib, name):
        outs = [pieces for _, dests in jobs for pieces in dests]
        return pl.pallas_call(
            functools.partial(pack_kernel, jobs),
            out_shape=[
                shape(len(pieces) * rows, 2 * width) for width, dests in jobs for pieces in dests
            ],
            in_specs=anywhere(2 + len(after)),
            out_specs=anywhere(len(outs)),
            scratch_shapes=[
                pltpu.SemaphoreType.DMA((2 * sum(len(p) for _, dests in jobs for p in dests),))
            ],
            compiler_params=params(mib),
            name=name,
        )(*sources, *after)

    kv_out = pl.pallas_call(
        functools.partial(pack_kv_kernel, kv_heads),
        out_shape=[shape(rows, 2 * kv_width)] * heads,
        in_specs=in_vmem(2),
        out_specs=in_vmem(heads),
        compiler_params=params(2),
        name="pack_kv",
    )(keys, values)
    kv = [kv_out[0]] + [swap(kv_out[m], "head", heads, m) for m in range(1, heads)]

    jobs = [(GW, [[qo_at(m, g) for g in range(kv_heads)] for m in range(1, heads)])]
    packed = pack(jobs, (queries, grad_out), kv_out[:1], 4, "pack_qo")
    handed = swap(gate(packed[2], kv[1:]), "head", heads, 1)
    from_across = swap(gate(packed[1], kv[1:]), "head", heads, 2)
    from_corner = swap(handed, "head", heads, 2)

    merged, hide = pl.pallas_call(
        functools.partial(merge_kernel, heads),
        out_shape=[shape(SLOT_DEV, 2 * kv_width), shape(kv_heads, tokens, HD)],
        in_specs=in_vmem(1 + heads),
        out_specs=in_vmem(2),
        scratch_shapes=[pltpu.VMEM((tokens, 2 * kv_width), jnp.bfloat16)],
        compiler_params=params(4),
        name="merge",
    )(segment_ids, *kv)

    held = {0: merged}
    for m in range(1, shards):
        low = m & -m
        held[m] = swap(held[m - low], "ctx", shards, low)
    late = [held[m] for m in range(1, shards - 1)] + [from_across]
    from_core = swap(gate(packed[0], late), "head", heads, 1)
    from_corner = gate(from_corner, (), 40)
    qo = (from_core, from_across, from_corner)

    all_rows = tokens * GROUP
    saved = []
    buffers = 2 if slots <= 1024 else 1
    for g in range(kv_heads):
        outs = pl.pallas_call(
            functools.partial(attend_kernel, g, order),
            out_shape=[
                shape(slots, all_rows),
                shape(slots, all_rows),
                shape(rows, all_rows),
                shape(rows, all_rows),
                shape(all_rows, HD),
                shape(all_rows, HD),
                shape(slots, HD),
                shape(half, 2 * HD),
            ],
            in_specs=anywhere(2) + in_vmem(heads + heads + shards) + anywhere(g > 0),
            out_specs=in_vmem(8),
            scratch_shapes=[
                pltpu.VMEM((slots + PAIR * rows, 2 * HD), jnp.bfloat16),
                pltpu.VMEM((slots + PAIR * rows, HD), jnp.bfloat16),
                pltpu.VMEM((rows, 2 * GW), jnp.bfloat16),
                pltpu.VMEM((buffers, slots + PAIR * rows, PAIR * GROUP * rows), jnp.float32),
                pltpu.VMEM((buffers, slots + PAIR * rows, PAIR * GROUP * rows), jnp.float32),
                pltpu.SemaphoreType.DMA((2,)),
            ],
            compiler_params=params(24),
            cost_estimate=pl.CostEstimate(
                flops=6 * all_rows * (slots + rows) * HD,
                bytes_accessed=8 * 2**20,
                transcendentals=all_rows * slots,
            ),
            name="attend",
        )(
            queries,
            grad_out,
            hide,
            *kv,
            *[held[m] for m in order],
            *qo,
            *([saved[-1][2]] if g else []),
        )
        saved.append(outs)
    far = [swap(outs[7], "ctx", shards, 1) for outs in saved]
    near = []
    own = []
    for g in range(kv_heads):
        outs = pl.pallas_call(
            functools.partial(terms_kernel, heads),
            out_shape=[
                shape(half, 2 * HD, dtype=jnp.float32),
                shape(tokens, 2 * HD, dtype=jnp.float32),
            ],
            in_specs=in_vmem(6) + anywhere(1),
            out_specs=in_vmem(2),
            compiler_params=params(16),
            cost_estimate=pl.CostEstimate(
                flops=2 * all_rows * slots * HD, bytes_accessed=2**20, transcendentals=0
            ),
            name="terms",
        )(*saved[g][:6], saved[-1][2])
        near.append(outs[0])
        own.append(outs[1])
    dq = pl.pallas_call(
        functools.partial(queries_kernel, heads),
        out_shape=shape(tokens, kv_heads * GW),
        in_specs=in_vmem(heads + 3 * kv_heads),
        out_specs=in_vmem(1)[0],
        compiler_params=params(16),
        cost_estimate=pl.CostEstimate(
            flops=2 * kv_heads * all_rows * slots * HD, bytes_accessed=2**20, transcendentals=0
        ),
        name="queries",
    )(*kv, *[x for outs in saved for x in (outs[1], outs[3], outs[6])])

    spread_args = []
    for g in range(kv_heads):
        keep, received, step = near[g], far[g], 2
        while step < shards:
            count = keep.shape[0] // 2
            keep, send = pl.pallas_call(
                add_kernel,
                out_shape=[shape(count, 2 * HD, dtype=jnp.float32), shape(count, 2 * HD)],
                in_specs=in_vmem(2),
                out_specs=in_vmem(2),
                compiler_params=params(8),
                name="add",
            )(keep, received)
            received = swap(send, "ctx", shards, step)
            step *= 2
        spread_args += [keep, received, own[g]]

    grad_keys, grad_values = pl.pallas_call(
        functools.partial(spread_kernel, 3),
        out_shape=[shape(tokens, kv_width)] * 2,
        in_specs=in_vmem(1 + len(spread_args)),
        out_specs=in_vmem(2),
        compiler_params=params(12),
        name="spread",
    )(segment_ids, *spread_args)
    return dq, grad_keys, grad_values


def solution(mesh):
    return jax.shard_map(
        local,
        mesh=mesh,
        in_specs=(
            P(("ctx", "head"), None),
            P(("ctx", "head"), None),
            P(("ctx", "head"), None),
            P("head", "ctx"),
            P(("ctx", "head"), None),
        ),
        out_specs=(P("ctx", "head"), P("ctx", "head"), P("ctx", "head")),
        check_vma=False,
    )
```

```python
import functools

import jax
import jax.numpy as jnp
from jax import lax
from jax.experimental import pallas as pl
from jax.experimental.pallas import tpu as pltpu
from jax.sharding import PartitionSpec as P

QH = 64
KVH = 8
HD = 128
SLOT_DEV = 96
GROUP = QH // KVH
GW = GROUP * HD
SCALE = HD ** (-0.5)
LOG2E = 1.4426950408889634
DEAD = 1024.0
HIDDEN = 2.0**96
PAIR = 2
PART = 16


def nt(a, b):
    return lax.dot_general(a, b, (((1,), (1,)), ((), ())), preferred_element_type=jnp.float32)


def nn(a, b):
    return lax.dot_general(a, b, (((1,), (0,)), ((), ())), preferred_element_type=jnp.float32)


def tn(a, b):
    return lax.dot_general(a, b, (((0,), (0,)), ((), ())), preferred_element_type=jnp.float32)


def slot_picks(seg_row, tokens):
    return lax.broadcasted_iota(jnp.int32, (SLOT_DEV, tokens), 0) == seg_row


def place():
    return lax.axis_index("ctx"), lax.axis_index("head")


def lanes(start, size):
    return pl.ds(pl.multiple_of(start, HD), size)


def run_copies(copies):
    for copy in copies:
        copy.start()
    return copies


def wait_copies(copies):
    for copy in copies:
        copy.wait()


def pack_kernel(jobs, *refs):
    outs = [out for _, dests in jobs for out in dests]
    sources, out_refs, sems = refs[:2], refs[-len(outs) - 1 : -1], refs[-1]
    me = place()[1]
    copies = []
    done = 0
    for width, dests in jobs:
        for out, pieces in zip(out_refs[done:], dests):
            for at, (m, scale, offset) in enumerate(pieces):
                start = lax.bitwise_xor(me, m) * scale + offset
                for part, source in enumerate(sources):
                    rows = source.shape[0]
                    copies.append(
                        pltpu.make_async_copy(
                            source.at[:, lanes(start, width)],
                            out.at[at * rows : (at + 1) * rows, part * width : (part + 1) * width],
                            sems.at[len(copies)],
                        )
                    )
        done += len(dests)
    wait_copies(run_copies(copies))


def gate_kernel(*refs):
    pass


def pack_kv_kernel(kv_heads, key_ref, value_ref, *outs):
    me = place()[1]
    width = kv_heads * HD
    for m, out in enumerate(outs):
        start = lax.bitwise_xor(me, m) * width
        out[:, 0:width] = key_ref[:, lanes(start, width)]
        out[:, width : 2 * width] = value_ref[:, lanes(start, width)]


def merge_kernel(heads, seg_ref, *refs):
    pieces, (out, hide_ref, whole) = refs[:heads], refs[-3:]
    kv_heads, tokens = seg_ref.shape
    rows = tokens // heads
    me = place()[1]
    for m, piece in enumerate(pieces):
        start = pl.multiple_of(lax.bitwise_xor(me, m) * rows, 16)
        whole[pl.ds(start, rows), :] = piece[...]
    for g in range(kv_heads):
        picks = slot_picks(seg_ref[g : g + 1, :], tokens).astype(jnp.float32)
        counts = jnp.sum(picks, axis=1, keepdims=True)
        low_picks = picks.astype(jnp.bfloat16)
        sizes = jnp.maximum(counts, 1.0)
        for part in range(2):
            at = slice((part * kv_heads + g) * HD, (part * kv_heads + g + 1) * HD)
            rows_out = nn(low_picks, whole[:, at]) / sizes
            if part == 0:
                rows_out = jnp.where(counts == 0.0, DEAD, rows_out)
            out[:, at] = rows_out.astype(jnp.bfloat16)
        padded = -(-tokens // HD) * HD
        place_in = lax.broadcasted_iota(jnp.int32, (HD, padded), 0)
        seg = jnp.concatenate([seg_ref[g : g + 1, :]] * 2, axis=1)[:, :padded]
        late = (place_in >= seg) & (place_in < SLOT_DEV)
        hide = jnp.where(late, -HIDDEN, jnp.where(place_in == SLOT_DEV, 1.0, 0.0))
        hide_ref[g] = hide.T[:tokens].astype(jnp.bfloat16)


def folded(x, reduce):
    return reduce(x.reshape(x.shape[0] // 8, 8, x.shape[1]), axis=0)


def attend_kernel(g, order, q_ref, o_ref, hide_ref, *refs):
    shards = len(order)
    heads = 4
    kv_pieces, blocks, refs = refs[:heads], refs[heads : heads + shards], refs[heads + shards :]
    qo_pieces = refs[: heads - 1]
    (
        p_ref, ds_ref, own_p_ref, own_ds_ref, qs_ref, os_ref, key_ref, far_ref,
        kx, vx, mine, s_ref, g_ref, sems,
    ) = refs[-14:]
    rows = q_ref.shape[0]
    kv_heads = hide_ref.shape[0]
    slots = shards * SLOT_DEV
    shard, me = place()
    key_at = slice(g * HD, (g + 1) * HD)
    value_at = slice((kv_heads + g) * HD, (kv_heads + g + 1) * HD)
    start = (me * kv_heads + g) * GW
    copies = run_copies(
        [
            pltpu.make_async_copy(
                source.at[:, lanes(start, GW)], mine.at[:, part * GW : (part + 1) * GW], sems.at[part]
            )
            for part, source in enumerate((q_ref, o_ref))
        ]
    )

    lane = lax.broadcasted_iota(jnp.int32, (SLOT_DEV, HD), 1)
    row = lax.broadcasted_iota(jnp.int32, (SLOT_DEV, HD), 0)
    for r, (m, block) in enumerate(zip(order, blocks)):
        at = pl.ds(r * SLOT_DEV, SLOT_DEV)
        key = block[:, key_at].astype(jnp.float32)
        vx[at, :] = block[:, value_at]
        if m == 0:
            extra = jnp.where(lane == row, 1.0, 0.0)
        else:
            hide = (key[:, 0:1] > 100.0) | (lax.bitwise_xor(shard, m) > shard)
            extra = jnp.where(hide & (lane >= SLOT_DEV), -HIDDEN, 0.0)
        kx[at, 0:HD] = jnp.where(key > 100.0, 0.0, key).astype(jnp.bfloat16)
        kx[at, HD : 2 * HD] = extra.astype(jnp.bfloat16)
    kx[slots:, HD : 2 * HD] = jnp.zeros((PAIR * rows, HD), jnp.bfloat16)

    width = GROUP * rows
    span = PAIR * width
    eye_row = lax.broadcasted_iota(jnp.int32, (PAIR * rows, span), 0)
    eye_lane = lax.broadcasted_iota(jnp.int32, (PAIR * rows, span), 1)
    eye = (eye_row // rows == eye_lane // width) & (eye_row % rows == eye_lane % rows)
    factor = SCALE * LOG2E

    turns = list(range(1, heads)) + [0]
    for turn in range(0, heads, PAIR):
        pair = turns[turn : turn + PAIR]
        if 0 in pair:
            wait_copies(copies)
        queries = []
        cotangents = []
        hides = []
        for i, m in enumerate(pair):
            qo, part = (qo_pieces[m - 1], g) if m else (mine, 0)
            at = slice(part * rows, (part + 1) * rows)
            here = slice(slots + i * rows, slots + (i + 1) * rows)
            kx[here, 0:HD] = kv_pieces[m][:, key_at]
            vx[here, :] = kv_pieces[m][:, value_at]
            q2 = jnp.concatenate([qo[at, h * HD : (h + 1) * HD] for h in range(GROUP)], axis=0)
            o2 = jnp.concatenate(
                [qo[at, GW + h * HD : GW + (h + 1) * HD] for h in range(GROUP)], axis=0
            )
            chunk = slice(m * width, (m + 1) * width)
            qs_ref[chunk, :] = q2
            os_ref[chunk, :] = o2
            queries.append(q2)
            cotangents.append(o2)
            tokens_at = pl.ds(pl.multiple_of(lax.bitwise_xor(me, m) * rows, 16), rows)
            hides += [hide_ref[g, tokens_at, :]] * GROUP
        qx = jnp.concatenate(
            [jnp.concatenate(queries, axis=0), jnp.concatenate(hides, axis=0)], axis=1
        )
        held = turn // PAIR % s_ref.shape[0]
        s_at, g_at = s_ref.at[held], g_ref.at[held]
        s_at[...] = nt(kx[...], qx)
        g_at[...] = nt(vx[...], jnp.concatenate(cotangents, axis=0))
        own_score = jnp.sum(jnp.where(eye, s_at[slots:, :], 0.0), axis=0, keepdims=True)
        own_grad_prob = jnp.sum(jnp.where(eye, g_at[slots:, :], 0.0), axis=0, keepdims=True)
        parts = [slice(r, r + PART) for r in range(0, slots, PART)]
        top = folded(functools.reduce(jnp.maximum, [s_at[part, :] for part in parts]), jnp.max)
        top = jnp.maximum(jnp.max(top, axis=0, keepdims=True), own_score)
        total = 0.0
        delta = 0.0
        for part in parts:
            weights = jnp.exp2((s_at[part, :] - top) * factor)
            s_at[part, :] = weights
            total = total + folded(weights, jnp.sum)
            delta = delta + folded(weights * g_at[part, :], jnp.sum)
        own_weight = jnp.exp2((own_score - top) * factor)
        total = jnp.sum(total, axis=0, keepdims=True) + own_weight
        delta = jnp.sum(delta, axis=0, keepdims=True) + own_weight * own_grad_prob
        delta = delta / total
        own_prob = own_weight / total
        inverse = 1.0 / total
        for part in parts:
            probs = s_at[part, :] * inverse
            low_probs = probs.astype(jnp.bfloat16)
            low_grads = (probs * (g_at[part, :] - delta)).astype(jnp.bfloat16)
            for i, m in enumerate(pair):
                p_ref[part, m * width : (m + 1) * width] = low_probs[:, i * width : (i + 1) * width]
                ds_ref[part, m * width : (m + 1) * width] = low_grads[:, i * width : (i + 1) * width]
        own_grad_score = own_prob * (own_grad_prob - delta)
        for i, m in enumerate(pair):
            chunk = slice(m * width, (m + 1) * width)
            here = slice(i * width, (i + 1) * width)
            one = eye[0:rows, 0:width]
            own_p_ref[:, chunk] = jnp.where(one, own_prob[:, here], 0.0).astype(jnp.bfloat16)
            own_ds_ref[:, chunk] = jnp.where(one, own_grad_score[:, here], 0.0).astype(jnp.bfloat16)
    far = slice(slots // 2, slots)
    far_ref[:, 0:HD] = (SCALE * nn(ds_ref[far, :], qs_ref[...])).astype(far_ref.dtype)
    far_ref[:, HD : 2 * HD] = nn(p_ref[far, :], os_ref[...]).astype(far_ref.dtype)
    key_ref[...] = kx[0:slots, 0:HD]


def terms_kernel(heads, p_ref, ds_ref, own_p_ref, own_ds_ref, qs_ref, os_ref, after_ref, near_ref, own_ref):
    rows = own_p_ref.shape[0]
    near = slice(0, near_ref.shape[0])
    near_ref[:, 0:HD] = SCALE * nn(ds_ref[near, :], qs_ref[...])
    near_ref[:, HD : 2 * HD] = nn(p_ref[near, :], os_ref[...])
    me = place()[1]
    width = GROUP * rows
    for m in range(heads):
        at = pl.ds(pl.multiple_of(lax.bitwise_xor(me, m) * rows, 16), rows)
        chunk = slice(m * width, (m + 1) * width)
        own_ref[at, 0:HD] = SCALE * nn(own_ds_ref[:, chunk], qs_ref[chunk, :])
        own_ref[at, HD : 2 * HD] = nn(own_p_ref[:, chunk], os_ref[chunk, :])


def queries_kernel(heads, *refs):
    kv_pieces, refs, dq_ref = refs[:heads], refs[heads:-1], refs[-1]
    me = place()[1]
    for g in range(len(refs) // 3):
        ds_ref, own_ds_ref, key_ref = refs[3 * g : 3 * g + 3]
        turned = key_ref[...].astype(jnp.float32).T.astype(jnp.bfloat16)
        rows = own_ds_ref.shape[0]
        width = GROUP * rows
        for m in range(heads):
            at = pl.ds(pl.multiple_of(lax.bitwise_xor(me, m) * rows, 16), rows)
            chunk = slice(m * width, (m + 1) * width)
            own_key = kv_pieces[m][:, g * HD : (g + 1) * HD]
            dq = nn(turned, ds_ref[:, chunk]) + tn(own_key, own_ds_ref[:, chunk])
            dq = (SCALE * dq).T.astype(jnp.bfloat16)
            for h in range(GROUP):
                column = (g * GROUP + h) * HD
                dq_ref[at, column : column + HD] = dq[h * rows : (h + 1) * rows]


def add_kernel(near_ref, far_ref, keep_ref, send_ref):
    total = near_ref[...] + far_ref[...].astype(jnp.float32)
    half = keep_ref.shape[0]
    keep_ref[...] = total[:half]
    send_ref[...] = total[half:].astype(send_ref.dtype)


def spread_kernel(parts_per_head, seg_ref, *refs):
    kv_heads, tokens = seg_ref.shape
    gk_ref, gv_ref = refs[-2:]
    for g in range(kv_heads):
        parts = refs[g * parts_per_head : (g + 1) * parts_per_head]
        total = parts[0][...].astype(jnp.float32)
        for part in parts[1:-1]:
            total = total + part[...].astype(jnp.float32)
        picks = slot_picks(seg_ref[g : g + 1, :], tokens).astype(jnp.float32)
        counts = jnp.sum(picks, axis=1, keepdims=True)
        total = total / jnp.maximum(counts, 1.0)
        high = total.astype(jnp.bfloat16)
        low = (total - high.astype(jnp.float32)).astype(jnp.bfloat16)
        picks = picks.astype(jnp.bfloat16)
        spread = tn(picks, high) + tn(picks, low) + parts[-1][...]
        gk_ref[:, g * HD : (g + 1) * HD] = spread[:, 0:HD].astype(jnp.bfloat16)
        gv_ref[:, g * HD : (g + 1) * HD] = spread[:, HD : 2 * HD].astype(jnp.bfloat16)


def in_vmem(count):
    return [pl.BlockSpec(memory_space=pltpu.VMEM)] * count


def anywhere(count):
    return [pl.BlockSpec(memory_space=pl.ANY)] * count


def params(mib):
    return pltpu.CompilerParams(vmem_limit_bytes=mib * 2**20)


def shape(*dims, dtype=jnp.bfloat16):
    return jax.ShapeDtypeStruct(dims, dtype)


def swap(x, axis, size, m):
    return lax.ppermute(x, axis, [(i, i ^ m) for i in range(size)])


def gate(value, after, mib=0):
    return pl.pallas_call(
        gate_kernel,
        out_shape=shape(*value.shape, dtype=value.dtype),
        in_specs=anywhere(1 + len(after)),
        out_specs=anywhere(1)[0],
        input_output_aliases={0: 0},
        compiler_params=params(1),
        cost_estimate=pl.CostEstimate(flops=0, bytes_accessed=mib * 2**20, transcendentals=0),
        name="gate",
    )(value, *after)


def bit_reversed(count):
    if count == 1:
        return [0]
    half = [2 * i for i in bit_reversed(count // 2)]
    return half + [i + 1 for i in half]


def local(queries, keys, values, segment_ids, grad_out):
    rows = queries.shape[0]
    heads = lax.axis_size("head")
    tokens = rows * heads
    kv_heads = KVH // heads
    shards = lax.axis_size("ctx")
    order = bit_reversed(shards)
    half = SLOT_DEV * shards // 2
    slots = SLOT_DEV * shards
    kv_width = kv_heads * HD

    def kv_at(m):
        return (m, kv_width, 0)

    def qo_at(m, g):
        return (m, kv_heads * GW, g * GW)

    def pack(jobs, sources, after, mib, name):
        outs = [pieces for _, dests in jobs for pieces in dests]
        return pl.pallas_call(
            functools.partial(pack_kernel, jobs),
            out_shape=[
                shape(len(pieces) * rows, 2 * width) for width, dests in jobs for pieces in dests
            ],
            in_specs=anywhere(2 + len(after)),
            out_specs=anywhere(len(outs)),
            scratch_shapes=[
                pltpu.SemaphoreType.DMA((2 * sum(len(p) for _, dests in jobs for p in dests),))
            ],
            compiler_params=params(mib),
            name=name,
        )(*sources, *after)

    kv_out = pl.pallas_call(
        functools.partial(pack_kv_kernel, kv_heads),
        out_shape=[shape(rows, 2 * kv_width)] * heads,
        in_specs=in_vmem(2),
        out_specs=in_vmem(heads),
        compiler_params=params(2),
        name="pack_kv",
    )(keys, values)
    kv = [kv_out[0]] + [swap(kv_out[m], "head", heads, m) for m in range(1, heads)]

    jobs = [(GW, [[qo_at(m, g) for g in range(kv_heads)] for m in range(1, heads)])]
    packed = pack(jobs, (queries, grad_out), kv_out[:1], 4, "pack_qo")
    handed = swap(gate(packed[2], kv[1:]), "head", heads, 1)
    from_across = swap(gate(packed[1], kv[1:]), "head", heads, 2)
    from_corner = swap(handed, "head", heads, 2)

    merged, hide = pl.pallas_call(
        functools.partial(merge_kernel, heads),
        out_shape=[shape(SLOT_DEV, 2 * kv_width), shape(kv_heads, tokens, HD)],
        in_specs=in_vmem(1 + heads),
        out_specs=in_vmem(2),
        scratch_shapes=[pltpu.VMEM((tokens, 2 * kv_width), jnp.bfloat16)],
        compiler_params=params(4),
        name="merge",
    )(segment_ids, *kv)

    held = {0: merged}
    for m in range(1, shards):
        low = m & -m
        held[m] = swap(held[m - low], "ctx", shards, low)
    late = [held[m] for m in range(1, shards - 1)] + [from_across]
    from_core = swap(gate(packed[0], late), "head", heads, 1)
    from_corner = gate(from_corner, (), 40)
    qo = (from_core, from_across, from_corner)

    all_rows = tokens * GROUP
    saved = []
    buffers = 2 if slots <= 1024 else 1
    for g in range(kv_heads):
        outs = pl.pallas_call(
            functools.partial(attend_kernel, g, order),
            out_shape=[
                shape(slots, all_rows),
                shape(slots, all_rows),
                shape(rows, all_rows),
                shape(rows, all_rows),
                shape(all_rows, HD),
                shape(all_rows, HD),
                shape(slots, HD),
                shape(half, 2 * HD),
            ],
            in_specs=anywhere(2) + in_vmem(heads + heads + shards) + anywhere(g > 0),
            out_specs=in_vmem(8),
            scratch_shapes=[
                pltpu.VMEM((slots + PAIR * rows, 2 * HD), jnp.bfloat16),
                pltpu.VMEM((slots + PAIR * rows, HD), jnp.bfloat16),
                pltpu.VMEM((rows, 2 * GW), jnp.bfloat16),
                pltpu.VMEM((buffers, slots + PAIR * rows, PAIR * GROUP * rows), jnp.float32),
                pltpu.VMEM((buffers, slots + PAIR * rows, PAIR * GROUP * rows), jnp.float32),
                pltpu.SemaphoreType.DMA((2,)),
            ],
            compiler_params=params(24),
            cost_estimate=pl.CostEstimate(
                flops=6 * all_rows * (slots + rows) * HD,
                bytes_accessed=8 * 2**20,
                transcendentals=all_rows * slots,
            ),
            name="attend",
        )(
            queries,
            grad_out,
            hide,
            *kv,
            *[held[m] for m in order],
            *qo,
            *([saved[-1][2]] if g else []),
        )
        saved.append(outs)
    far = [swap(outs[7], "ctx", shards, 1) for outs in saved]
    near = []
    own = []
    for g in range(kv_heads):
        outs = pl.pallas_call(
            functools.partial(terms_kernel, heads),
            out_shape=[
                shape(half, 2 * HD, dtype=jnp.float32),
                shape(tokens, 2 * HD, dtype=jnp.float32),
            ],
            in_specs=in_vmem(6) + anywhere(1),
            out_specs=in_vmem(2),
            compiler_params=params(16),
            cost_estimate=pl.CostEstimate(
                flops=2 * all_rows * slots * HD, bytes_accessed=2**20, transcendentals=0
            ),
            name="terms",
        )(*saved[g][:6], saved[-1][2])
        near.append(outs[0])
        own.append(outs[1])
    dq = pl.pallas_call(
        functools.partial(queries_kernel, heads),
        out_shape=shape(tokens, kv_heads * GW),
        in_specs=in_vmem(heads + 3 * kv_heads),
        out_specs=in_vmem(1)[0],
        compiler_params=params(16),
        cost_estimate=pl.CostEstimate(
            flops=2 * kv_heads * all_rows * slots * HD, bytes_accessed=2**20, transcendentals=0
        ),
        name="queries",
    )(*kv, *[x for outs in saved for x in (outs[1], outs[3], outs[6])])

    spread_args = []
    for g in range(kv_heads):
        keep, received, step = near[g], far[g], 2
        while step < shards:
            count = keep.shape[0] // 2
            keep, send = pl.pallas_call(
                add_kernel,
                out_shape=[shape(count, 2 * HD, dtype=jnp.float32), shape(count, 2 * HD)],
                in_specs=in_vmem(2),
                out_specs=in_vmem(2),
                compiler_params=params(8),
                name="add",
            )(keep, received)
            received = swap(send, "ctx", shards, step)
            step *= 2
        spread_args += [keep, received, own[g]]

    grad_keys, grad_values = pl.pallas_call(
        functools.partial(spread_kernel, 3),
        out_shape=[shape(tokens, kv_width)] * 2,
        in_specs=in_vmem(1 + len(spread_args)),
        out_specs=in_vmem(2),
        compiler_params=params(12),
        name="spread",
    )(segment_ids, *spread_args)
    return dq, grad_keys, grad_values


def solution(mesh):
    return jax.shard_map(
        local,
        mesh=mesh,
        in_specs=(
            P(("ctx", "head"), None),
            P(("ctx", "head"), None),
            P(("ctx", "head"), None),
            P("head", "ctx"),
            P(("ctx", "head"), None),
        ),
        out_specs=(P("ctx", "head"), P("ctx", "head"), P("ctx", "head")),
        check_vma=False,
    )
```
